128 devices in a mesh: grp: 8 (over z, core), own: 16 (over y, x).
Axes of the slice: x: 4, y: 4, z: 4, core: 2. Of those that a mesh axis runs over, the one named last changes fastest.
Arguments:
- vectors: bfloat16 [32768, 768], P(('grp', 'own')), may hold values from -64 to 64
- candidates: int32 [32768, 8], P(('grp', 'own')), may hold values from 0 to 511, all different within a row; in each aligned block of 256 rows (0 to 255, 256 to 511, ...) at most 8 rows name the same one
- centroids: bfloat16 [65536, 768], P('own'), may hold values from -8 to 8
Outputs:
- refined: bfloat16 [65536, 768], P('own')
The draws below stay inside these ranges and needn't reach their ends.
Inputs may be any that keep to these rules, and one draw needn't show every extreme that they name: `candidates`: the 8 cells named by one vector are distinct. Among the vectors of one device no cell is named by more than 8 of them, and in every draw some cell is named by exactly 8.
All inputs are finite; a program needn't handle non-finite values.
Results may differ from the reference program's by a relative error of at most 0.006.
Values may be sent and summed in bfloat16 or wider, within the bound.
A program may use at most 128 MiB of HBM per device.

```python
import math
import jax
import jax.numpy as jnp
import numpy as np
from jax import lax

D = 768
K = 65536
CELL = 128
CAND = 8
VEC_DEV = 256
CELLS = 512
MOST = 8
VECTORS = 32768
N_GRP = 8
N_OWN = 16


def draw_vectors(key, part):
    key = jax.random.fold_in(key, 11)
    base_key = jax.random.fold_in(key, 0)
    values = jnp.clip(jax.random.normal(base_key, (VECTORS, D), jnp.float32), -6.0, 6.0)
    return values.astype(jnp.bfloat16)


def draw_centroids(key, part):
    key = jax.random.fold_in(key, 23)
    base_key, scale_key = jax.random.split(key, 2)
    row_scale = jnp.exp(jax.random.uniform(scale_key, (K, 1), jnp.float32, math.log(0.97), math.log(1.03)))
    values = jnp.clip(jax.random.normal(base_key, (K, D), jnp.float32), -5.0, 5.0) * row_scale
    return values.astype(jnp.bfloat16)


def shared_out(rng, own, number, rows, amount, top, bound, slope):
    ranking = jax.random.permutation(rng, amount)
    crowded, ordinary = shares(amount, rows * top, bound, slope, True), shares(amount, rows * top, bound, slope, False)
    places = jnp.arange(amount)

    def named(tallies, rotation):
        used = int((tallies > 0).sum())
        fixed = max(1, used // 4)
        passed = fixed + (places - fixed + rotation * (used - fixed)) % max(1, amount - fixed)
        return jnp.zeros((amount,), jnp.int32).at[ranking[jnp.where(places < fixed, places, passed)]].set(jnp.asarray(tallies, jnp.int32))

    tallies = jnp.where(number % 4 == 0, named(crowded, number // 4), named(ordinary, number - number // 4 - 1))
    mixed = jax.random.permutation(jax.random.fold_in(own, 3), amount)
    donor, receiver = mixed[0:amount // 2 * 2:2], mixed[1:amount // 2 * 2:2]
    room = jnp.minimum(tallies[donor] - 1, bound - tallies[receiver]) // 2
    room = jnp.where((donor == ranking[0]) | (receiver == ranking[0]) | (tallies[receiver] == 0), 0, jnp.maximum(room, 0))
    passed = jax.random.randint(jax.random.fold_in(own, 4), (amount // 2,), 0, 1 << 20) % (room + 1)
    tallies = tallies.at[donor].add(-passed).at[receiver].add(passed)
    labels = jnp.searchsorted(jnp.cumsum(tallies), jnp.arange(rows * top), side="right").astype(jnp.int32)
    grid = labels.reshape(top, rows).T
    grid = grid[jax.random.permutation(jax.random.fold_in(own, 1), rows)]
    rotation = jax.random.randint(jax.random.fold_in(own, 2), (rows, 1), 0, top)
    return jnp.take_along_axis(grid, (jnp.arange(top)[None, :] + rotation) % top, axis=1)


def shares(count, total, bound, skew, full):
    weights = [(1 << 20) // math.isqrt(rank ** skew) + 1 for rank in range(1, count + 1)]
    largest = bound if full else min(bound, max(-(-total // count), total * weights[0] // sum(weights)))
    least = 1 if total - largest >= count - 1 else 0
    counts, surplus = [largest] + [least] * (count - 1), total - largest - least * (count - 1)
    while surplus > 0:
        free = [i for i in range(1, count) if counts[i] < largest] or [i for i in range(1, count) if counts[i] < bound]
        mass, left = sum([weights[i] for i in free]), surplus
        for i in free:
            more = min(bound - counts[i], max(1, left * weights[i] // mass), surplus)
            counts[i] = counts[i] + more
            surplus = surplus - more
    return np.array(counts)


def setup_inputs(seed: int = 0) -> dict:
    seeds = jax.random.split(jax.random.key(seed), 4)
    vectors = draw_vectors(jax.random.fold_in(seeds[3], 71), 0)
    candidates_keys = jax.random.split(jax.random.fold_in(seeds[1], 1), VECTORS // VEC_DEV)
    candidates_turns = jax.random.permutation(jax.random.fold_in(seeds[1], 3), VECTORS // VEC_DEV)
    candidates = jax.vmap(lambda own, number: shared_out(jax.random.fold_in(seeds[1], 2), own, number, VEC_DEV, CELLS, CAND, MOST, 2))(candidates_keys, candidates_turns).reshape((VECTORS, CAND))
    centroids = draw_centroids(jax.random.fold_in(seeds[3], 71), 0)
    return dict(vectors=vectors, candidates=candidates, centroids=centroids)


PRIOR_MASS = 1.0


def pair_slots(candidates):
    cell_flat = candidates.reshape(-1).astype(jnp.int32)
    pair_total = cell_flat.shape[0]
    sort_order = jnp.argsort(cell_flat, stable=True).astype(jnp.int32)
    cell_counts = jax.ops.segment_sum(jnp.ones((pair_total,), jnp.int32), cell_flat, num_segments=CELLS)
    cell_starts = jnp.cumsum(cell_counts) - cell_counts
    sorted_cells = cell_flat[sort_order]
    sorted_rank = jnp.arange(pair_total, dtype=jnp.int32) - cell_starts[sorted_cells]
    slot_rank = jnp.zeros((pair_total,), jnp.int32).at[sort_order].set(sorted_rank.astype(jnp.int32))
    return cell_flat, slot_rank


def reference(vectors, candidates, centroids):
    capacity = N_GRP * N_OWN * MOST
    vec_total = vectors.shape[0]
    cell_flat, slot_rank = pair_slots(candidates)
    vector_ids = jnp.repeat(jnp.arange(vec_total, dtype=jnp.int32), CAND)
    row_table = jnp.full((CELLS, capacity), vec_total, jnp.int32).at[cell_flat, slot_rank].set(vector_ids)
    padded = jnp.concatenate([vectors, jnp.zeros((1, D), vectors.dtype)], axis=0)
    cell_centroids = centroids.reshape(CELLS, CELL, D)
    logit_scale = D ** -0.5

    def cell_scores(operands):
        row_ids, cell_block = operands
        gathered = jnp.take(padded, row_ids, axis=0)
        products = jnp.dot(gathered, cell_block.T, preferred_element_type=jnp.float32)
        block_float = cell_block.astype(jnp.float32)
        sq_norms = jnp.sum(block_float * block_float, axis=1)
        return (2.0 * products - sq_norms[None, :]) * logit_scale

    score_table = lax.map(cell_scores, (row_table, cell_centroids))
    pair_scores = score_table[cell_flat, slot_rank].reshape(vec_total, CAND * CELL)
    row_top = jnp.max(pair_scores, axis=1, keepdims=True)
    exponent = jnp.exp(pair_scores - row_top)
    weights = (exponent / jnp.sum(exponent, axis=1, keepdims=True)).astype(jnp.bfloat16)
    weight_table = jnp.zeros((CELLS, capacity, CELL), jnp.bfloat16).at[cell_flat, slot_rank].set(
        weights.reshape(vec_total * CAND, CELL))

    def cell_sums(operands):
        row_ids, cell_weights = operands
        gathered = jnp.take(padded, row_ids, axis=0)
        weighted = jnp.dot(cell_weights.T, gathered, preferred_element_type=jnp.float32)
        weight_mass = jnp.sum(cell_weights.astype(jnp.float32), axis=0)
        return weighted, weight_mass

    weighted, weight_mass = lax.map(cell_sums, (row_table, weight_table))
    weighted = weighted.reshape(K, D)
    weight_mass = weight_mass.reshape(K)
    refined = (weighted + PRIOR_MASS * centroids.astype(jnp.float32)) / (weight_mass[:, None] + PRIOR_MASS)
    return refined.astype(jnp.bfloat16)
```

```python
import functools

import jax
import jax.numpy as jnp
from jax import lax
from jax.experimental import pallas as pl
from jax.experimental.pallas import tpu as pltpu
from jax.sharding import PartitionSpec as P

MESH = pl.DeviceIdType.MESH
F32 = jnp.float32
BF16 = jnp.bfloat16

CELL = 128
SLOTS = 8
VEC = 256
D = 768
SIDE = 4
PLANE = SIDE * SIDE
SRC = 2 * PLANE
MINE = 16
QUARTER = MINE // SIDE
ROWS = SRC * SLOTS
PRIOR_MASS = 1.0
LOW = -1e30
HIGH = 1e30

HALF = VEC // 2
FOURTH = VEC // 4


def ring(i):
    return lax.rem(i + 2 * SIDE, SIDE)


def kernel(
    vec, cand, cents, out,
    X, CD, C, R, RK, U, SQ, L, LB, SH, LVS, PV, LV2, MS, MR, S, SF, RN, RP, F,
    load_sem, cand_sem, ag_send, ag_recv, sib_send, sib_recv, lse_sem,
    rs_send, rs_recv, mass_sem, og_send, og_recv, os_send, os_recv, keep_sem,
):
    grp = lax.axis_index("grp")
    own = lax.axis_index("own")
    z, k = lax.div(grp, 2), lax.rem(grp, 2)
    y, x = lax.div(own, SIDE), lax.rem(own, SIDE)
    sibling = (z * 2 + 1 - k, own)
    z_next = (ring(z + 1) * 2 + k, own)
    z_prev = (ring(z - 1) * 2 + k, own)
    z_far = (ring(z + 2) * 2 + k, own)
    me = k * PLANE + own

    def at(dx, dy):
        return ring(y + dy) * SIDE + ring(x + dx)

    def remote(src, dst, send, recv, device):
        return pltpu.make_async_remote_copy(
            src_ref=src, dst_ref=dst, send_sem=send, recv_sem=recv,
            device_id=device, device_id_type=MESH,
        )

    loads = [
        pltpu.make_async_copy(vec, X.at[me], load_sem.at[0]),
        pltpu.make_async_copy(cand, CD.at[me], load_sem.at[1]),
        pltpu.make_async_copy(cents.at[pl.ds(k * MINE, MINE)], C, load_sem.at[2]),
    ]
    for load in loads:
        load.start()

    def peer(d):
        t = lax.rem(me + d, SRC)
        return t, (z * 2 + lax.div(t, PLANE), lax.rem(t, PLANE))

    barrier = pltpu.get_barrier_semaphore()

    def greet(d, carry):
        pl.semaphore_signal(barrier, inc=1, device_id=peer(d)[1], device_id_type=MESH)
        return carry

    lax.fori_loop(1, SRC, greet, 0)
    for device in (z_next, z_prev, z_far):
        pl.semaphore_signal(barrier, inc=1, device_id=device, device_id_type=MESH)
    pl.semaphore_wait(barrier, SRC - 1 + 3)
    loads[0].wait()
    loads[1].wait()

    def block(h, first, second):
        return at(first, second) if h == 0 else at(second, first)

    def axis_peer(h, stage, step):
        along_x = (h == 0) == (stage == 1)
        return (grp, at(step, 0) if along_x else at(0, step))

    def rows_of(h, part):
        if part == 2:
            return pl.ds(h * HALF, HALF)
        return pl.ds(h * HALF + part * FOURTH, FOURTH)

    def message(h, stage, d, kind):
        place = 0 if stage == 1 else 1 + d
        number = 4 * place + kind
        step = 1 if kind in (0, 2) else -1
        back = 0 if kind < 2 else -step
        offset = (0, 1, -1, 2)[d]
        blk = block(h, back, 0) if stage == 1 else block(h, offset, back)
        ref = X.at[k * PLANE + blk, rows_of(h, 2 if kind < 2 else kind - 2)]
        return remote(
            ref, ref, ag_send.at[h, number], ag_recv.at[h, number], axis_peer(h, stage, step)
        )

    def start(h, stage, d, kind):
        message(h, stage, d, kind).start()

    def arrive(h, stage, d, kind):
        message(h, stage, d, kind).wait_recv()

    spots = [(dx, dy) for dy in (0, 1, -1, 2) for dx in (0, 1, -1, 2)]

    def to_sibling(h, dx, dy):
        place = spots.index((dx, dy))
        ref = X.at[k * PLANE + at(dx, dy), rows_of(h, 2)]
        return remote(ref, ref, sib_send.at[h, place], sib_recv.at[h, place], sibling)

    def pass_on(h, first, second):
        dx, dy = (first, second) if h == 0 else (second, first)
        to_sibling(h, dx, dy).start()

    def take(spot):
        for h in (0, 1):
            to_sibling(h, *spot).wait_recv()

    for h in (0, 1):
        for kind in (0, 1):
            start(h, 1, 0, kind)

    def send_cand(d, carry):
        ref = CD.at[me]
        remote(
            ref, ref, cand_sem.at[0], cand_sem.at[1], (grp, lax.rem(own + d, PLANE))
        ).start()
        return carry

    lax.fori_loop(1, PLANE, send_cand, 0)

    for h in (0, 1):
        for kind in (0, 1):
            start(h, 2, 0, kind)
        pass_on(h, 0, 0)

    loads[2].wait()
    ones = jnp.ones((8, D), BF16)
    last = (((1,), (1,)), ((), ()))

    def norms(c, carry):
        value = C[c].astype(F32)
        square = value * value
        high = square.astype(BF16)
        low = (square - high.astype(F32)).astype(BF16)
        SQ[c] = lax.dot_general(
            ones, high, last, preferred_element_type=F32
        ) + lax.dot_general(ones, low, last, preferred_element_type=F32)
        return carry

    lax.fori_loop(0, MINE, norms, 0)

    many = CD.at[pl.ds(k * PLANE, PLANE - 1)]
    pltpu.make_async_copy(many, many, cand_sem.at[1]).wait()
    group_cand = CD.at[pl.ds(k * PLANE, PLANE)]
    cand_over = remote(group_cand, group_cand, cand_sem.at[2], cand_sem.at[3], sibling)
    cand_over.start()
    U[...] = jnp.where(
        lax.broadcasted_iota(jnp.int32, (VEC, VEC), 0)
        < lax.broadcasted_iota(jnp.int32, (VEC, VEC), 1),
        1.0,
        0.0,
    ).astype(BF16)
    labels = lax.broadcasted_iota(jnp.int32, (MINE, VEC), 0) + (own * 2 + k) * MINE

    def ranks(s, carry):
        named = CD[s]
        hit = named[0:1] == labels
        for i in range(1, 8):
            hit = hit | (named[i : i + 1] == labels)
        rank = jnp.dot(jnp.where(hit, 1.0, 0.0).astype(BF16), U[...], preferred_element_type=F32)
        RK[s] = jnp.where(hit, rank, -1.0)
        return carry

    def slot_mask(s):
        number = lax.broadcasted_iota(jnp.int32, (MINE, SLOTS, VEC), 1).astype(F32)
        return RK[s][:, None, :] == number

    def place_rows(o):
        parts = []
        for kk in (0, 1):
            s = kk * PLANE + o
            pick = jnp.where(slot_mask(s), 1.0, 0.0).reshape(MINE * SLOTS, VEC).astype(BF16)
            rows = jnp.dot(pick, X[s], preferred_element_type=F32)
            parts.append(rows.reshape(MINE, SLOTS, D))
        base = pl.multiple_of(o * 2 * SLOTS, 2 * SLOTS)
        R[:, pl.ds(base, 2 * SLOTS), :] = jnp.concatenate(parts, axis=1).astype(BF16)

    def place_all(count, offsets):
        def one(i, carry):
            place_rows(at(*offsets(i)))
            return carry

        lax.fori_loop(0, count, one, 0)

    both = (0, 1)
    for h in both:
        for kind in (0, 1):
            arrive(h, 1, 0, kind)
            start(h, 1, 0, 2 + kind)
            d = 2 - kind
            start(h, 2, d, 0)
            start(h, 2, d, 1)
            pass_on(h, 1 if d == 1 else -1, 0)

    lax.fori_loop(k * PLANE, k * PLANE + PLANE, ranks, 0)
    cand_over.wait_recv()
    lax.fori_loop((1 - k) * PLANE, (1 - k) * PLANE + PLANE, ranks, 0)

    for h in both:
        for kind in (0, 1):
            arrive(h, 2, 0, kind)
            start(h, 2, 0, 2 + kind)
            pass_on(h, 0, -1 if kind == 0 else 1)
    for h in both:
        for kind in (2, 3):
            arrive(h, 1, 0, kind)
        start(h, 2, 3, 0)
        start(h, 2, 3, 1)
        pass_on(h, 2, 0)
    for spot in ((0, 0), (1, 0), (-1, 0), (0, 1), (0, -1)):
        take(spot)
    place_rows(own)

    def cross(i):
        sign, turn = lax.rem(i, 2) * 2 - 1, lax.div(i, 2)
        return sign * (1 - turn), sign * turn

    place_all(4, cross)
    for d in (1, 2):
        for h in both:
            for kind in (0, 1):
                arrive(h, 2, d, kind)
                start(h, 2, d, 2 + kind)
                pass_on(h, 1 if d == 1 else -1, -1 if kind == 0 else 1)
    for h in both:
        for kind in (2, 3):
            arrive(h, 2, 0, kind)
        pass_on(h, 0, 2)
    for spot in ((1, 1), (1, -1), (-1, 1), (-1, -1)):
        take(spot)
    place_all(4, lambda i: (lax.rem(i, 2) * 2 - 1, lax.div(i, 2) * 2 - 1))
    for h in both:
        for kind in (0, 1):
            arrive(h, 2, 3, kind)
            start(h, 2, 3, 2 + kind)
            pass_on(h, 2, -1 if kind == 0 else 1)
    for spot in ((2, 0), (0, 2)):
        take(spot)
    place_all(2, lambda i: (2 * i, 2 - 2 * i))
    for d in (1, 2):
        for h in both:
            for kind in (2, 3):
                arrive(h, 2, d, kind)
            pass_on(h, 1 if d == 1 else -1, 2)
    for spot in ((2, 1), (2, -1), (1, 2), (-1, 2)):
        take(spot)

    def outer(i):
        sign, turn = lax.rem(i, 2) * 2 - 1, lax.div(i, 2)
        return 2 * turn + sign * (1 - turn), 2 * (1 - turn) + sign * turn

    place_all(4, outer)
    for h in both:
        for kind in (2, 3):
            arrive(h, 2, 3, kind)
        pass_on(h, 2, 2)
    take((2, 2))
    place_rows(at(2, 2))

    def logits(c, carry):
        products = lax.dot_general(R[c], C[c], last, preferred_element_type=F32)
        value = (2.0 * products - SQ[c][0:1]) * D**-0.5
        L[c] = value
        top = jnp.max(value, axis=1, keepdims=True)
        total = jnp.sum(jnp.exp(value - top), axis=1, keepdims=True)
        LB[c] = jnp.broadcast_to(top + jnp.log(total), (ROWS, CELL))
        return carry

    lax.fori_loop(0, MINE, logits, 0)

    def slots_of(s):
        base = lax.rem(s, PLANE) * 2 * SLOTS + lax.div(s, PLANE) * SLOTS
        return pl.ds(pl.multiple_of(base, SLOTS), SLOTS)

    def partial(s):
        part = LB[:, slots_of(s), :]
        wide = jnp.concatenate([part, part], axis=2)
        mask = slot_mask(s)
        known = jnp.where(mask, wide, LOW)
        top = jnp.max(jnp.max(known, axis=0), axis=0, keepdims=True)
        terms = jnp.where(mask, jnp.exp(known - top[None]), 0.0)
        total = jnp.sum(jnp.sum(terms, axis=0), axis=0, keepdims=True)
        return top + jnp.log(jnp.maximum(total, 1e-30))

    PV[me] = partial(me)

    def send_partial(d, carry):
        s, device = peer(d)
        LVS[s] = partial(s)
        remote(LVS.at[s], PV.at[me], lse_sem.at[0], lse_sem.at[1], device).start()
        return carry

    lax.fori_loop(1, SRC, send_partial, 0)
    others = PV.at[pl.ds(0, SRC - 1)]
    pltpu.make_async_copy(others, others, lse_sem.at[1]).wait()
    parts = PV[...]
    top = jnp.max(parts, axis=0, keepdims=True)
    LV2[pl.ds(me, 1)] = top + jnp.log(jnp.sum(jnp.exp(parts - top), axis=0, keepdims=True))

    def send_total(d, carry):
        remote(LV2.at[me], LV2.at[me], lse_sem.at[2], lse_sem.at[3], peer(d)[1]).start()
        return carry

    lax.fori_loop(1, SRC, send_total, 0)
    others = LV2.at[pl.ds(0, SRC - 1)]
    pltpu.make_async_copy(others, others, lse_sem.at[3]).wait()

    def shifts(s, carry):
        found = jnp.where(slot_mask(s), LV2[s][None], HIGH)
        low = jnp.min(found, axis=2, keepdims=True)
        SH[:, slots_of(s), :] = jnp.broadcast_to(low, (MINE, SLOTS, CELL))
        return carry

    lax.fori_loop(0, SRC, shifts, 0)

    def cell_sum(c):
        weights = jnp.exp(L[c] - SH[c]).astype(BF16)
        MS[c] = jnp.sum(weights.astype(F32), axis=0, keepdims=True)
        return lax.dot_general(
            weights, R[c], (((0,), (0,)), ((), ())), preferred_element_type=F32
        )

    def cell_of(step, i):
        return ring(z + step) * QUARTER + i

    landing = (RN, RP)
    toward = (z_next, z_prev)

    def reduce_message(way, number):
        return remote(
            S.at[way, number], landing[way].at[number],
            rs_send.at[way, number], rs_recv.at[way, number], toward[way],
        )

    for i in (0, 1):
        for way in (0, 1):
            S[way, i] = cell_sum(cell_of(2, i + 2 * way)).astype(BF16)
            reduce_message(way, i).start()
    for i in (0, 1):
        for way in (0, 1):
            number = 2 + i + (2 - 2 * way)
            step = 1 - 2 * way
            S[way, number] = cell_sum(cell_of(step, number - 2)).astype(BF16)
            reduce_message(way, number).start()
    for i in (0, 1):
        for way in (0, 1):
            SF[2 * i + way] = cell_sum(cell_of(1 - 2 * way, i + 2 * way))

    def own_sum(i, carry):
        SF[4 + i] = cell_sum(z * QUARTER + i)
        return carry

    lax.fori_loop(0, QUARTER, own_sum, 0)
    MR[z] = MS[...]
    for j, device in enumerate((z_next, z_prev, z_far)):
        remote(MS, MR.at[z], mass_sem.at[j], mass_sem.at[3], device).start()
    for i in (0, 1):
        for way in (0, 1):
            number = 2 + i + 2 * way
            reduce_message(way, i).wait_recv()
            S[way, number] = (SF[2 * i + way] + landing[way][i].astype(F32)).astype(BF16)
            reduce_message(way, number).start()
    others = MR.at[pl.ds(0, SIDE - 1)]
    pltpu.make_async_copy(others, others, mass_sem.at[3]).wait()

    def out_cell(step, i, core):
        return out.at[core * MINE + cell_of(step, i)]

    def out_message(kind, i):
        step = (0, 0, -1, 1)[kind]
        ref = out_cell(step, i, k)
        src = F.at[i] if kind < 2 else ref
        return remote(
            src, ref, og_send.at[kind, i], og_recv.at[kind, i], toward[kind % 2]
        )

    def out_sibling(step, i):
        ref = out_cell(step, i, k)
        src = F.at[i] if step == 0 else ref
        return remote(src, ref, os_send.at[step % 4, i], os_recv.at[step % 4, i], sibling)

    diagonal = lax.broadcasted_iota(jnp.int32, (CELL, CELL), 0) == lax.broadcasted_iota(
        jnp.int32, (CELL, CELL), 1
    )
    order = (0, 2, 1, 3)
    keeps = []
    for i in order:
        reduce_message(0, 2 + i).wait_recv()
        reduce_message(1, 2 + i).wait_recv()
        c = z * QUARTER + i
        mass = MR[0, c] + MR[1, c] + MR[2, c] + MR[3, c]
        column = jnp.sum(
            jnp.where(diagonal, jnp.broadcast_to(mass, (CELL, CELL)), 0.0), axis=1, keepdims=True
        )
        total = SF[4 + i] + RN[2 + i].astype(F32) + RP[2 + i].astype(F32)
        F[i] = ((total + PRIOR_MASS * C[c].astype(F32)) / (column + PRIOR_MASS)).astype(BF16)
        out_message(0, i).start()
        out_message(1, i).start()
        out_sibling(0, i).start()
        keep = pltpu.make_async_copy(F.at[i], out_cell(0, i, k), keep_sem.at[i])
        keep.start()
        keeps.append(keep)
    for i in order:
        for kind in (0, 1):
            out_message(kind, i).wait_recv()
            if i // 2 == kind:
                out_message(2 + kind, i).start()
            out_sibling(-1 if kind == 0 else 1, i).start()
    for i in order:
        out_message(2 + i // 2, i).wait_recv()
        out_sibling(2, i).start()
    for step in (0, -1, 1, 2):
        for i in order:
            out_sibling(step, i).wait_recv()

    for keep in keeps:
        keep.wait()
    for h in both:
        for stage, d in ((1, 0), (2, 0), (2, 1), (2, 2), (2, 3)):
            for kind in range(4):
                message(h, stage, d, kind).wait_send()
        for spot in spots:
            to_sibling(h, *spot).wait_send()
    many = CD.at[pl.ds(0, PLANE - 1)]
    pltpu.make_async_copy(many, many, cand_sem.at[0]).wait()
    cand_over.wait_send()
    sent = PV.at[pl.ds(0, SRC - 1)]
    pltpu.make_async_copy(sent, sent, lse_sem.at[0]).wait()
    pltpu.make_async_copy(sent, sent, lse_sem.at[2]).wait()
    for way in (0, 1):
        for number in range(6):
            reduce_message(way, number).wait_send()
    for j, device in enumerate((z_next, z_prev, z_far)):
        remote(MS, MR.at[z], mass_sem.at[j], mass_sem.at[3], device).wait_send()
    for i in range(QUARTER):
        out_message(0, i).wait_send()
        out_message(1, i).wait_send()
        out_message(2 + i // 2, i).wait_send()
        for step in (0, -1, 1, 2):
            out_sibling(step, i).wait_send()


def body(vectors, candidates, centroids):
    cells = centroids.shape[0] // CELL
    dma = pltpu.SemaphoreType.DMA
    any_space = pl.BlockSpec(memory_space=pl.ANY)
    refined = pl.pallas_call(
        kernel,
        out_shape=jax.ShapeDtypeStruct((cells, CELL, D), BF16),
        in_specs=[any_space] * 3,
        out_specs=any_space,
        scratch_shapes=[
            pltpu.VMEM((SRC, VEC, D), BF16),
            pltpu.VMEM((SRC, 8, VEC), jnp.int32),
            pltpu.VMEM((MINE, CELL, D), BF16),
            pltpu.VMEM((MINE, ROWS, D), BF16),
            pltpu.VMEM((SRC, MINE, VEC), F32),
            pltpu.VMEM((VEC, VEC), BF16),
            pltpu.VMEM((MINE, 8, CELL), F32),
            pltpu.VMEM((MINE, ROWS, CELL), F32),
            pltpu.VMEM((MINE, ROWS, CELL), F32),
            pltpu.VMEM((MINE, ROWS, CELL), F32),
            pltpu.VMEM((SRC, 1, VEC), F32),
            pltpu.VMEM((SRC, 1, VEC), F32),
            pltpu.VMEM((SRC, 1, VEC), F32),
            pltpu.VMEM((MINE, 1, CELL), F32),
            pltpu.VMEM((SIDE, MINE, 1, CELL), F32),
            pltpu.VMEM((2, 6, CELL, D), BF16),
            pltpu.VMEM((8, CELL, D), F32),
            pltpu.VMEM((6, CELL, D), BF16),
            pltpu.VMEM((6, CELL, D), BF16),
            pltpu.VMEM((QUARTER, CELL, D), BF16),
            dma((3,)),
            dma((4,)),
            dma((2, 20)),
            dma((2, 20)),
            dma((2, 16)),
            dma((2, 16)),
            dma((4,)),
            dma((2, 6)),
            dma((2, 6)),
            dma((4,)),
            dma((4, 4)),
            dma((4, 4)),
            dma((4, 4)),
            dma((4, 4)),
            dma((4,)),
        ],
        compiler_params=pltpu.CompilerParams(
            collective_id=0, has_side_effects=True, vmem_limit_bytes=56 * 1024 * 1024
        ),
        name="refine",
    )(vectors, candidates.T, centroids.reshape(cells, CELL, D))
    return refined.reshape(cells * CELL, D)


def solution(mesh):
    placed = (P(("grp", "own"), None), P(("grp", "own"), None), P("own", None))
    return jax.shard_map(
        body, mesh=mesh, in_specs=placed, out_specs=P("own", None), check_vma=False
    )
```

```python
import functools

import jax
import jax.numpy as jnp
from jax import lax
from jax.experimental import pallas as pl
from jax.experimental.pallas import tpu as pltpu
from jax.sharding import PartitionSpec as P

MESH = pl.DeviceIdType.MESH
F32 = jnp.float32
BF16 = jnp.bfloat16

CELL = 128
SLOTS = 8
VEC = 256
D = 768
SIDE = 4
PLANE = SIDE * SIDE
SRC = 2 * PLANE
MINE = 16
QUARTER = MINE // SIDE
ROWS = SRC * SLOTS
PRIOR_MASS = 1.0
LOW = -1e30
HIGH = 1e30

HALF = VEC // 2
FOURTH = VEC // 4


BUDGET = 1.0
SPOTS = (
    (0, 0), (1, 0), (-1, 0), (0, 1), (0, -1), (1, 1), (1, -1), (-1, 1), (-1, -1),
    (2, 0), (0, 2), (2, 1), (2, -1), (1, 2), (-1, 2), (2, 2),
)
GROUPS = ((0, 5), (5, 6), (11, 5))


def mirrored(place):
    dx, dy = (0 if v == 0 else 2 if v == 2 else -v for v in SPOTS[place])
    return SPOTS.index((dx, dy))


def ring(i):
    return lax.rem(i + 2 * SIDE, SIDE)


def kernel(
    vec, cand, cents, out,
    X, CD, C, R, RK, H, U, SQ, L, LB, LVS, PV, LV2, MS, MR, S, SF, RN, RP,
    load_sem, cand_send, cand_recv, ag_send, ag_recv, sib_send, sib_recv, lse_sem,
    rs_send, rs_recv, mass_sem, og_send, og_recv, os_send, os_recv,
):
    grp = lax.axis_index("grp")
    own = lax.axis_index("own")
    z, k = lax.div(grp, 2), lax.rem(grp, 2)
    y, x = lax.div(own, SIDE), lax.rem(own, SIDE)
    sibling = (z * 2 + 1 - k, own)
    z_next = (ring(z + 1) * 2 + k, own)
    z_prev = (ring(z - 1) * 2 + k, own)
    z_far = (ring(z + 2) * 2 + k, own)
    me = k * PLANE + own
    both = (0, 1)
    last = (((1,), (1,)), ((), ()))

    def at(dx, dy):
        return ring(y + dy) * SIDE + ring(x + dx)

    def remote(src, dst, send, recv, device):
        return pltpu.make_async_remote_copy(
            src_ref=src, dst_ref=dst, send_sem=send, recv_sem=recv,
            device_id=device, device_id_type=MESH,
        )

    loads = [
        pltpu.make_async_copy(vec, X.at[me], load_sem.at[0]),
        pltpu.make_async_copy(cand, CD.at[me], load_sem.at[1]),
        pltpu.make_async_copy(cents.at[pl.ds(k * MINE, MINE)], C, load_sem.at[2]),
    ]
    for load in loads:
        load.start()
    x_next, x_prev = (grp, at(1, 0)), (grp, at(-1, 0))
    y_next, y_prev = (grp, at(0, 1)), (grp, at(0, -1))
    x_far, y_far = (grp, at(2, 0)), (grp, at(0, 2))
    near = (x_next, x_prev, x_far, y_next, y_prev, y_far, sibling, z_next, z_prev, z_far)
    barrier = pltpu.get_barrier_semaphore()
    for device in near:
        pl.semaphore_signal(barrier, inc=1, device_id=device, device_id_type=MESH)
    pl.semaphore_wait(barrier, len(near))

    def block(h, first, second):
        return at(first, second) if h == 0 else at(second, first)

    def axis_peer(h, stage, step):
        along_x = (h == 0) == (stage == 1)
        return (grp, at(step, 0) if along_x else at(0, step))

    def rows_of(h, part):
        if part == 2:
            return pl.ds(h * HALF, HALF)
        return pl.ds(h * HALF + part * FOURTH, FOURTH)

    def message(h, stage, d, kind):
        place = 0 if stage == 1 else 1 + d % 4
        number = 4 * place + kind
        step = 1 if kind in (0, 2) else -1
        back = 0 if kind < 2 else -step
        blk = block(h, back, 0) if stage == 1 else block(h, d, back)
        ref = X.at[k * PLANE + blk, rows_of(h, 2 if kind < 2 else kind - 2)]
        return remote(
            ref, ref, ag_send.at[h, number], ag_recv.at[h, number], axis_peer(h, stage, step)
        )

    def start(stage, d, kinds):
        for kind in kinds:
            for h in both:
                message(h, stage, d, kind).start()

    def to_sibling(h, place):
        ref = X.at[k * PLANE + at(*SPOTS[place]), rows_of(h, 2)]
        return remote(ref, ref, sib_send.at[h, place], sib_recv.at[h, place], sibling)

    def pass_on(h, first, second):
        to_sibling(h, SPOTS.index((first, second) if h == 0 else (second, first))).start()

    def arrive(stage, d, kinds, h):
        for kind in kinds:
            message(h, stage, d, kind).wait_recv()
            if kind < 2:
                side = -1 if kind == 0 else 1
                message(h, stage, d, 2 + kind).start()
                if stage == 1:
                    pass_on(h, side, 0)
                else:
                    pass_on(h, d, side)
        if kinds[-1] == 3:
            if stage == 1:
                pass_on(h, 2, 0)
            else:
                pass_on(h, d, 2)

    def take(places):
        for place in places:
            for h in both:
                to_sibling(h, place).wait_recv()

    def cand_message(number):
        if number < 3:
            ref = CD.at[pl.ds(k * PLANE + own, 1)]
            device = (x_next, x_prev, x_far)[number]
        else:
            ref = CD.at[pl.ds(k * PLANE + y * SIDE, SIDE)]
            device = (y_next, y_prev, y_far)[number - 3]
        return remote(ref, ref, cand_send.at[number], cand_recv.at[number], device)

    group_cand = CD.at[pl.ds(k * PLANE, PLANE)]
    cand_over = remote(group_cand, group_cand, cand_send.at[6], cand_recv.at[6], sibling)

    def cand_start(numbers):
        for number in numbers:
            cand_message(number).start()

    def cand_arrive(numbers):
        for number in numbers:
            cand_message(number).wait_recv()

    def norms():
        loads[2].wait()
        ones = jnp.ones((8, D), BF16)

        def one(c, carry):
            value = C[c].astype(F32)
            square = value * value
            high = square.astype(BF16)
            low = (square - high.astype(F32)).astype(BF16)
            SQ[c] = lax.dot_general(
                ones, high, last, preferred_element_type=F32
            ) + lax.dot_general(ones, low, last, preferred_element_type=F32)
            return carry

        lax.fori_loop(0, MINE, one, 0)

    def triangle():
        U[...] = jnp.where(
            lax.broadcasted_iota(jnp.int32, (VEC, VEC), 0)
            < lax.broadcasted_iota(jnp.int32, (VEC, VEC), 1),
            1.0,
            0.0,
        ).astype(BF16)

    def ranks(kk):
        labels = lax.broadcasted_iota(jnp.int32, (MINE, VEC), 0) + (own * 2 + k) * MINE
        for place, spot in enumerate(SPOTS):
            named = CD[kk * PLANE + at(*spot)]
            hit = named[0:1] == labels
            for i in range(1, 8):
                hit = hit | (named[i : i + 1] == labels)
            H[place * MINE : (place + 1) * MINE] = jnp.where(hit, 1.0, 0.0).astype(BF16)
        hits = H[...]
        rank = jnp.dot(hits, U[...], preferred_element_type=F32)
        slot = jnp.where(hits.astype(F32) > 0.5, rank, -1.0)
        RK[:, kk] = slot.reshape(PLANE, MINE, VEC)

    def numbers(count):
        return lax.broadcasted_iota(jnp.int32, (count, SLOTS, VEC), 1).astype(F32)

    def slot_mask(place, kk):
        return RK[place, kk][:, None, :] == numbers(MINE)

    def place_rows(place):
        parts = []
        for kk in both:
            pick = jnp.where(slot_mask(place, kk), 1.0, 0.0).reshape(MINE * SLOTS, VEC)
            rows = jnp.dot(
                pick.astype(BF16), X[kk * PLANE + at(*SPOTS[place])], preferred_element_type=F32
            )
            parts.append(rows.reshape(MINE, SLOTS, D))
        base = place * 2 * SLOTS
        R[:, base : base + 2 * SLOTS, :] = jnp.concatenate(parts, axis=1).astype(BF16)

    def logits(group, first_cell, cells):
        first, count = GROUPS[group]
        slots = slice(first * 2 * SLOTS, (first + count) * 2 * SLOTS)
        for c in range(first_cell, first_cell + cells):
            products = lax.dot_general(R[c, slots], C[c], last, preferred_element_type=F32)
            value = (2.0 * products - SQ[c][0:1]) * D**-0.5
            L[c, slots] = value
            top = jnp.max(value, axis=1, keepdims=True)
            total = jnp.sum(jnp.exp(value - top), axis=1, keepdims=True)
            LB[c, slots] = jnp.broadcast_to(top + jnp.log(total), (count * 2 * SLOTS, CELL))

    def partial(place):
        for kk in both:
            base = (place * 2 + kk) * SLOTS
            part = LB[:, base : base + SLOTS, :]
            wide = jnp.concatenate([part, part], axis=2)
            mask = slot_mask(place, kk)
            known = jnp.where(mask, wide, LOW)
            top = jnp.max(jnp.max(known, axis=0), axis=0, keepdims=True)
            terms = jnp.where(mask, jnp.exp(known - top[None]), 0.0)
            total = jnp.sum(jnp.sum(terms, axis=0), axis=0, keepdims=True)
            LVS[2 * place + kk] = top + jnp.log(jnp.maximum(total, 1e-30))
            if place:
                send_partial(2 * place + kk, (z * 2 + kk, at(*SPOTS[place])))
        if not place:
            PV[me] = LVS[k]
            send_partial(1 - k, sibling)

    def send_partial(number, device):
        remote(LVS.at[number], PV.at[me], lse_sem.at[0], lse_sem.at[1], device).start()

    loads[1].wait()
    cand_start((0, 1, 2))
    loads[0].wait()
    start(1, 0, (0, 1))
    for h in both:
        pass_on(h, 0, 0)
    triangle()
    cand_arrive((0, 1, 2))
    cand_start((3, 4, 5))
    start(2, 0, (0, 1))
    drained = set()
    norms()

    steps = []
    for h in both:
        steps.append(("", functools.partial(arrive, 1, 0, (0, 1), h)))
    steps.append(("", lambda: (start(2, 1, (0, 1)), start(2, -1, (0, 1)))))
    steps.append(("", lambda: cand_arrive((3, 4, 5))))
    steps.append(("cand", cand_over.start))
    for h in both:
        steps.append(("", functools.partial(arrive, 1, 0, (2, 3), h)))
    steps.append(("", lambda: start(2, 2, (0, 1))))
    steps.append(("over", None))
    for h in both:
        steps.append(("ring1" if h else "", functools.partial(arrive, 2, 0, (0, 1), h)))
    for d in (1, -1):
        for h in both:
            for kinds in ((0,), (1,)):
                steps.append(("ring2" if h and d < 0 and kinds[0] else "", functools.partial(arrive, 2, d, kinds, h)))
    for h in both:
        steps.append(("far1" if h else "", functools.partial(arrive, 2, 0, (2, 3), h)))
    for h in both:
        for kinds in ((0,), (1,)):
            steps.append(("", functools.partial(arrive, 2, 2, kinds, h)))
    for d in (1, -1):
        for h in both:
            steps.append(("far2" if h and d < 0 else "", functools.partial(arrive, 2, d, (2, 3), h)))
    for h in both:
        steps.append(("end" if h else "", functools.partial(arrive, 2, 2, (2, 3), h)))

    works = []

    def ranks_of_other():
        cand_over.wait_recv()
        ranks(1 - k)

    works.append(("cand", lambda: ranks(k), 1.0))
    works.append(("over", ranks_of_other, 1.0))

    def placed(places, ready):
        works.append((ready, functools.partial(take, places), 0.0))
        for place in places:
            works.append((ready, functools.partial(place_rows, place), 0.4))

    def scored(group, ready):
        for c in range(0, MINE, 4):
            works.append((ready, functools.partial(logits, group, c, 4), 0.8))
        first, count = GROUPS[group]
        for place in range(first, first + count):
            works.append((ready, functools.partial(partial, place), 0.4))

    placed((0, 1, 2, 3, 4), "ring1")
    scored(0, "ring1")
    placed((5, 6, 7, 8), "ring2")
    placed((9, 10), "far1")
    scored(1, "far1")
    placed((11, 12, 13, 14), "far2")
    placed((15,), "end")

    done = set()
    for name, step in steps:
        if step is not None:
            step()
        done.add(name)
        spent = 0.0
        while works and works[0][0] in done and spent < BUDGET:
            spent += works[0][2]
            works.pop(0)[1]()
    for _, work, _ in works:
        work()
    scored_now = len(GROUPS) - 1
    logits(scored_now, 0, MINE)
    for place in range(GROUPS[-1][0], PLANE):
        partial(place)

    others = PV.at[pl.ds(0, SRC - 1)]
    pltpu.make_async_copy(others, others, lse_sem.at[1]).wait()
    parts = PV[...]
    top = jnp.max(parts, axis=0, keepdims=True)
    LV2[pl.ds(k, 1)] = top + jnp.log(jnp.sum(jnp.exp(parts - top), axis=0, keepdims=True))

    def send_total(place, device):
        remote(
            LV2.at[k], LV2.at[2 * mirrored(place) + k], lse_sem.at[2], lse_sem.at[3], device
        ).start()

    send_total(0, sibling)
    for place in range(1, PLANE):
        for kk in both:
            send_total(place, (z * 2 + kk, at(*SPOTS[place])))
    others = LV2.at[pl.ds(0, SRC - 1)]
    pltpu.make_async_copy(others, others, lse_sem.at[3]).wait()

    def cell_sum(c):
        rank = RK[:, :, pl.ds(c, 1), :].reshape(SRC, 1, VEC)
        found = jnp.where(rank == numbers(SRC), LV2[...], HIGH)
        shift = jnp.min(found, axis=2, keepdims=True).reshape(ROWS, 1)
        weights = jnp.exp(L[c] - shift).astype(BF16)
        MS[c] = jnp.sum(weights.astype(F32), axis=0, keepdims=True)
        return lax.dot_general(
            weights, R[c], (((0,), (0,)), ((), ())), preferred_element_type=F32
        )

    def cell_of(step, i):
        return ring(z + step) * QUARTER + i

    landing = (RN, RP)
    toward = (z_next, z_prev)

    def reduce_message(way, number):
        return remote(
            S.at[way, number], landing[way].at[number],
            rs_send.at[way, number], rs_recv.at[way, number], toward[way],
        )

    for i in (0, 1):
        for way in (0, 1):
            S[way, i] = cell_sum(cell_of(2, i + 2 * way)).astype(BF16)
            reduce_message(way, i).start()
    for i in (0, 1):
        for way in (0, 1):
            number = 2 + i + (2 - 2 * way)
            step = 1 - 2 * way
            S[way, number] = cell_sum(cell_of(step, number - 2)).astype(BF16)
            reduce_message(way, number).start()
    for i in (0, 1):
        for way in (0, 1):
            SF[2 * i + way] = cell_sum(cell_of(1 - 2 * way, i + 2 * way))

    def own_sum(i, carry):
        SF[4 + i] = cell_sum(z * QUARTER + i)
        return carry

    lax.fori_loop(0, QUARTER, own_sum, 0)
    MR[z] = MS[...]
    for j, device in enumerate((z_next, z_prev, z_far)):
        remote(MS, MR.at[z], mass_sem.at[j], mass_sem.at[3], device).start()
    for i in (0, 1):
        for way in (0, 1):
            number = 2 + i + 2 * way
            reduce_message(way, i).wait_recv()
            S[way, number] = (SF[2 * i + way] + landing[way][i].astype(F32)).astype(BF16)
            reduce_message(way, number).start()
    others = MR.at[pl.ds(0, SIDE - 1)]
    pltpu.make_async_copy(others, others, mass_sem.at[3]).wait()

    def out_cell(step, i):
        return out.at[k * MINE + cell_of(step, i)]

    def out_message(kind, i):
        ref = out_cell((0, 0, -1, 1)[kind], i)
        return remote(ref, ref, og_send.at[kind, i], og_recv.at[kind, i], toward[kind % 2])

    def out_sibling(step, i):
        ref = out_cell(step, i)
        return remote(ref, ref, os_send.at[step % 4, i], os_recv.at[step % 4, i], sibling)

    diagonal = lax.broadcasted_iota(jnp.int32, (CELL, CELL), 0) == lax.broadcasted_iota(
        jnp.int32, (CELL, CELL), 1
    )
    order = (0, 2, 1, 3)
    for i in order:
        reduce_message(0, 2 + i).wait_recv()
        reduce_message(1, 2 + i).wait_recv()
        c = z * QUARTER + i
        mass = MR[0, c] + MR[1, c] + MR[2, c] + MR[3, c]
        column = jnp.sum(
            jnp.where(diagonal, jnp.broadcast_to(mass, (CELL, CELL)), 0.0), axis=1, keepdims=True
        )
        total = SF[4 + i] + RN[2 + i].astype(F32) + RP[2 + i].astype(F32)
        out[k * MINE + c] = (
            (total + PRIOR_MASS * C[c].astype(F32)) / (column + PRIOR_MASS)
        ).astype(BF16)
        out_message(0, i).start()
        out_message(1, i).start()
        out_sibling(0, i).start()
    for i in order:
        for kind in (0, 1):
            out_message(kind, i).wait_recv()
            if i // 2 == kind:
                out_message(2 + kind, i).start()
            out_sibling(-1 if kind == 0 else 1, i).start()
    for i in order:
        out_message(2 + i // 2, i).wait_recv()
        out_sibling(2, i).start()
    for step in (0, -1, 1, 2):
        for i in order:
            out_sibling(step, i).wait_recv()

    for h in both:
        for stage, d in ((1, 0), (2, 0), (2, 1), (2, -1), (2, 2)):
            for kind in range(4):
                if (stage, d, kind) not in drained:
                    message(h, stage, d, kind).wait_send()
        for place in range(PLANE):
            to_sibling(h, place).wait_send()
    for number in range(6):
        cand_message(number).wait_send()
    cand_over.wait_send()
    sent = PV.at[pl.ds(0, SRC - 1)]
    pltpu.make_async_copy(sent, sent, lse_sem.at[0]).wait()
    pltpu.make_async_copy(sent, sent, lse_sem.at[2]).wait()
    for way in (0, 1):
        for number in range(6):
            reduce_message(way, number).wait_send()
    for j, device in enumerate((z_next, z_prev, z_far)):
        remote(MS, MR.at[z], mass_sem.at[j], mass_sem.at[3], device).wait_send()
    for i in range(QUARTER):
        out_message(0, i).wait_send()
        out_message(1, i).wait_send()
        out_message(2 + i // 2, i).wait_send()
        for step in (0, -1, 1, 2):
            out_sibling(step, i).wait_send()


def body(vectors, candidates, centroids):
    cells = centroids.shape[0] // CELL
    dma = pltpu.SemaphoreType.DMA
    any_space = pl.BlockSpec(memory_space=pl.ANY)
    refined = pl.pallas_call(
        kernel,
        out_shape=pltpu.VMEM((cells, CELL, D), BF16),
        in_specs=[any_space] * 3,
        out_specs=pl.BlockSpec(memory_space=pltpu.VMEM),
        scratch_shapes=[
            pltpu.VMEM((SRC, VEC, D), BF16),
            pltpu.VMEM((SRC, 8, VEC), jnp.int32),
            pltpu.VMEM((MINE, CELL, D), BF16),
            pltpu.VMEM((MINE, ROWS, D), BF16),
            pltpu.VMEM((PLANE, 2, MINE, VEC), F32),
            pltpu.VMEM((PLANE * MINE, VEC), BF16),
            pltpu.VMEM((VEC, VEC), BF16),
            pltpu.VMEM((MINE, 8, CELL), F32),
            pltpu.VMEM((MINE, ROWS, CELL), F32),
            pltpu.VMEM((MINE, ROWS, CELL), F32),
            pltpu.VMEM((SRC, 1, VEC), F32),
            pltpu.VMEM((SRC, 1, VEC), F32),
            pltpu.VMEM((SRC, 1, VEC), F32),
            pltpu.VMEM((MINE, 1, CELL), F32),
            pltpu.VMEM((SIDE, MINE, 1, CELL), F32),
            pltpu.VMEM((2, 6, CELL, D), BF16),
            pltpu.VMEM((8, CELL, D), F32),
            pltpu.VMEM((6, CELL, D), BF16),
            pltpu.VMEM((6, CELL, D), BF16),
            dma((3,)),
            dma((7,)),
            dma((7,)),
            dma((2, 20)),
            dma((2, 20)),
            dma((2, 16)),
            dma((2, 16)),
            dma((4,)),
            dma((2, 6)),
            dma((2, 6)),
            dma((4,)),
            dma((4, 4)),
            dma((4, 4)),
            dma((4, 4)),
            dma((4, 4)),
        ],
        compiler_params=pltpu.CompilerParams(
            collective_id=0, has_side_effects=True, vmem_limit_bytes=48 * 1024 * 1024
        ),
        name="refine",
    )(vectors, candidates.T, centroids.reshape(cells, CELL, D))
    return refined.reshape(cells * CELL, D)


def solution(mesh):
    placed = (P(("grp", "own"), None), P(("grp", "own"), None), P("own", None))
    return jax.shard_map(
        body, mesh=mesh, in_specs=placed, out_specs=P("own", None), check_vma=False
    )
```

```python
import functools

import jax
import jax.numpy as jnp
from jax import lax
from jax.experimental import pallas as pl
from jax.experimental.pallas import tpu as pltpu
from jax.sharding import PartitionSpec as P

MESH = pl.DeviceIdType.MESH
F32 = jnp.float32
BF16 = jnp.bfloat16

CELL = 128
SLOTS = 8
VEC = 256
D = 768
SIDE = 4
PLANE = SIDE * SIDE
SRC = 2 * PLANE
MINE = 16
QUARTER = MINE // SIDE
ROWS = SRC * SLOTS
ROUTED = 2
PRIOR_MASS = 1.0
LOW = -1e30
HIGH = 1e30

HALF = VEC // 2
FOURTH = VEC // 4


BUDGET = 1.0
SPOTS = (
    (0, 0), (1, 0), (-1, 0), (0, 1), (0, -1), (1, 1), (1, -1), (-1, 1), (-1, -1),
    (2, 0), (0, 2), (2, 1), (2, -1), (1, 2), (-1, 2), (2, 2),
)
GROUPS = ((0, 5), (5, 6), (11, 5))


def mirrored(place):
    dx, dy = (0 if v == 0 else 2 if v == 2 else -v for v in SPOTS[place])
    return SPOTS.index((dx, dy))


def ring(i):
    return lax.rem(i + 2 * SIDE, SIDE)


def kernel(
    vec, cand, cents, out,
    X, CD, C, R, RK, H, U, SQ, L, LB, LVS, PV, LV2, MS, MR, S, SF, RN, RP,
    R3, SHR, SHZ, SQC,
    rows_send, rows_recv, shift_send, shift_recv, load_sem, cand_send, cand_recv, ag_send, ag_recv, sib_send, sib_recv, lse_sem,
    rs_send, rs_recv, mass_sem, og_send, og_recv, os_send, os_recv,
):
    grp = lax.axis_index("grp")
    own = lax.axis_index("own")
    z, k = lax.div(grp, 2), lax.rem(grp, 2)
    y, x = lax.div(own, SIDE), lax.rem(own, SIDE)
    sibling = (z * 2 + 1 - k, own)
    z_next = (ring(z + 1) * 2 + k, own)
    z_prev = (ring(z - 1) * 2 + k, own)
    z_far = (ring(z + 2) * 2 + k, own)
    me = k * PLANE + own
    both = (0, 1)
    last = (((1,), (1,)), ((), ()))

    def at(dx, dy):
        return ring(y + dy) * SIDE + ring(x + dx)

    def remote(src, dst, send, recv, device):
        return pltpu.make_async_remote_copy(
            src_ref=src, dst_ref=dst, send_sem=send, recv_sem=recv,
            device_id=device, device_id_type=MESH,
        )

    loads = [
        pltpu.make_async_copy(vec, X.at[me], load_sem.at[0]),
        pltpu.make_async_copy(cand, CD.at[me], load_sem.at[1]),
        pltpu.make_async_copy(cents.at[pl.ds(k * MINE, MINE)], C, load_sem.at[2]),
    ]
    for load in loads:
        load.start()
    x_next, x_prev = (grp, at(1, 0)), (grp, at(-1, 0))
    y_next, y_prev = (grp, at(0, 1)), (grp, at(0, -1))
    x_far, y_far = (grp, at(2, 0)), (grp, at(0, 2))
    near = (x_next, x_prev, x_far, y_next, y_prev, y_far, sibling, z_next, z_prev, z_far)
    barrier = pltpu.get_barrier_semaphore()
    for device in near:
        pl.semaphore_signal(barrier, inc=1, device_id=device, device_id_type=MESH)
    pl.semaphore_wait(barrier, len(near))

    def block(h, first, second):
        return at(first, second) if h == 0 else at(second, first)

    def axis_peer(h, stage, step):
        along_x = (h == 0) == (stage == 1)
        return (grp, at(step, 0) if along_x else at(0, step))

    def rows_of(h, part):
        if part == 2:
            return pl.ds(h * HALF, HALF)
        return pl.ds(h * HALF + part * FOURTH, FOURTH)

    def message(h, stage, d, kind):
        place = 0 if stage == 1 else 1 + d % 4
        number = 4 * place + kind
        step = 1 if kind in (0, 2) else -1
        back = 0 if kind < 2 else -step
        blk = block(h, back, 0) if stage == 1 else block(h, d, back)
        ref = X.at[k * PLANE + blk, rows_of(h, 2 if kind < 2 else kind - 2)]
        return remote(
            ref, ref, ag_send.at[h, number], ag_recv.at[h, number], axis_peer(h, stage, step)
        )

    def start(stage, d, kinds):
        for kind in kinds:
            for h in both:
                message(h, stage, d, kind).start()

    def to_sibling(h, place):
        ref = X.at[k * PLANE + at(*SPOTS[place]), rows_of(h, 2)]
        return remote(ref, ref, sib_send.at[h, place], sib_recv.at[h, place], sibling)

    def pass_on(h, first, second):
        to_sibling(h, SPOTS.index((first, second) if h == 0 else (second, first))).start()

    def arrive(stage, d, kinds, h):
        for kind in kinds:
            message(h, stage, d, kind).wait_recv()
            if kind < 2:
                side = -1 if kind == 0 else 1
                message(h, stage, d, 2 + kind).start()
                if stage == 1:
                    pass_on(h, side, 0)
                else:
                    pass_on(h, d, side)
        if kinds[-1] == 3:
            if stage == 1:
                pass_on(h, 2, 0)
            else:
                pass_on(h, d, 2)

    def take(places):
        for place in places:
            for h in both:
                to_sibling(h, place).wait_recv()

    def cand_message(number):
        if number < 3:
            ref = CD.at[pl.ds(k * PLANE + own, 1)]
            device = (x_next, x_prev, x_far)[number]
        else:
            ref = CD.at[pl.ds(k * PLANE + y * SIDE, SIDE)]
            device = (y_next, y_prev, y_far)[number - 3]
        return remote(ref, ref, cand_send.at[number], cand_recv.at[number], device)

    group_cand = CD.at[pl.ds(k * PLANE, PLANE)]
    cand_over = remote(group_cand, group_cand, cand_send.at[6], cand_recv.at[6], sibling)

    def cand_start(numbers):
        for number in numbers:
            cand_message(number).start()

    def cand_arrive(numbers):
        for number in numbers:
            cand_message(number).wait_recv()

    column = (z_next, z_prev, z_far)
    column_step = (1, -1, 2)

    def rows_message(group, j):
        first, count = GROUPS[group]
        slots = pl.ds(first * 2 * SLOTS, count * 2 * SLOTS)
        cells = pl.ds(ring(z + column_step[j]) * QUARTER + (QUARTER - ROUTED), ROUTED)
        return remote(
            R.at[cells, slots], R3.at[j, :, slots], rows_send.at[j, group], rows_recv.at[j, group],
            column[j],
        )

    def rows_start(group):
        for j in (2, 0, 1):
            rows_message(group, j).start()

    def shift_message(j):
        return remote(SHR.at[j], SHZ.at[j], shift_send.at[j], shift_recv.at[j], column[j])

    def norms():
        loads[2].wait()
        ones = jnp.ones((8, D), BF16)

        def one(c, carry):
            value = C[c].astype(F32)
            square = value * value
            high = square.astype(BF16)
            low = (square - high.astype(F32)).astype(BF16)
            SQ[c] = lax.dot_general(
                ones, high, last, preferred_element_type=F32
            ) + lax.dot_general(ones, low, last, preferred_element_type=F32)
            return carry

        lax.fori_loop(0, MINE, one, 0)
        for j in range(ROUTED):
            value = C[z * QUARTER + (QUARTER - ROUTED) + j].astype(F32)
            SQC[j] = jnp.broadcast_to(
                jnp.sum(value * value, axis=1, keepdims=True), (CELL, CELL)
            )

    def triangle():
        U[...] = jnp.where(
            lax.broadcasted_iota(jnp.int32, (VEC, VEC), 0)
            < lax.broadcasted_iota(jnp.int32, (VEC, VEC), 1),
            1.0,
            0.0,
        ).astype(BF16)

    def ranks(kk):
        labels = lax.broadcasted_iota(jnp.int32, (MINE, VEC), 0) + (own * 2 + k) * MINE
        for place, spot in enumerate(SPOTS):
            named = CD[kk * PLANE + at(*spot)]
            hit = named[0:1] == labels
            for i in range(1, 8):
                hit = hit | (named[i : i + 1] == labels)
            H[place * MINE : (place + 1) * MINE] = jnp.where(hit, 1.0, 0.0).astype(BF16)
        hits = H[...]
        rank = jnp.dot(hits, U[...], preferred_element_type=F32)
        slot = jnp.where(hits.astype(F32) > 0.5, rank, -1.0)
        RK[:, kk] = slot.reshape(PLANE, MINE, VEC)

    def numbers(count):
        return lax.broadcasted_iota(jnp.int32, (count, SLOTS, VEC), 1).astype(F32)

    def slot_mask(place, kk):
        return RK[place, kk][:, None, :] == numbers(MINE)

    def place_rows(place):
        parts = []
        for kk in both:
            pick = jnp.where(slot_mask(place, kk), 1.0, 0.0).reshape(MINE * SLOTS, VEC)
            rows = jnp.dot(
                pick.astype(BF16), X[kk * PLANE + at(*SPOTS[place])], preferred_element_type=F32
            )
            parts.append(rows.reshape(MINE, SLOTS, D))
        base = place * 2 * SLOTS
        R[:, base : base + 2 * SLOTS, :] = jnp.concatenate(parts, axis=1).astype(BF16)

    def logits(group, first_cell, cells):
        first, count = GROUPS[group]
        slots = slice(first * 2 * SLOTS, (first + count) * 2 * SLOTS)
        for c in range(first_cell, first_cell + cells):
            products = lax.dot_general(R[c, slots], C[c], last, preferred_element_type=F32)
            value = (2.0 * products - SQ[c][0:1]) * D**-0.5
            L[c, slots] = value
            top = jnp.max(value, axis=1, keepdims=True)
            total = jnp.sum(jnp.exp(value - top), axis=1, keepdims=True)
            LB[c, slots] = jnp.broadcast_to(top + jnp.log(total), (count * 2 * SLOTS, CELL))

    def partial(place):
        for kk in both:
            base = (place * 2 + kk) * SLOTS
            part = LB[:, base : base + SLOTS, :]
            wide = jnp.concatenate([part, part], axis=2)
            mask = slot_mask(place, kk)
            known = jnp.where(mask, wide, LOW)
            top = jnp.max(jnp.max(known, axis=0), axis=0, keepdims=True)
            terms = jnp.where(mask, jnp.exp(known - top[None]), 0.0)
            total = jnp.sum(jnp.sum(terms, axis=0), axis=0, keepdims=True)
            LVS[2 * place + kk] = top + jnp.log(jnp.maximum(total, 1e-30))
            if place:
                send_partial(2 * place + kk, (z * 2 + kk, at(*SPOTS[place])))
        if not place:
            PV[me] = LVS[k]
            send_partial(1 - k, sibling)

    def send_partial(number, device):
        remote(LVS.at[number], PV.at[me], lse_sem.at[0], lse_sem.at[1], device).start()

    loads[1].wait()
    cand_start((0, 1, 2))
    loads[0].wait()
    start(1, 0, (0, 1))
    for h in both:
        pass_on(h, 0, 0)
    triangle()
    cand_arrive((0, 1, 2))
    cand_start((3, 4, 5))
    start(2, 0, (0, 1))
    drained = set()
    norms()

    steps = []
    for h in both:
        steps.append(("", functools.partial(arrive, 1, 0, (0, 1), h)))
    steps.append(("", lambda: (start(2, 1, (0, 1)), start(2, -1, (0, 1)))))
    steps.append(("", lambda: cand_arrive((3, 4, 5))))
    steps.append(("cand", cand_over.start))
    for h in both:
        steps.append(("", functools.partial(arrive, 1, 0, (2, 3), h)))
    steps.append(("", lambda: start(2, 2, (0, 1))))
    steps.append(("over", None))
    for h in both:
        steps.append(("ring1" if h else "", functools.partial(arrive, 2, 0, (0, 1), h)))
    for d in (1, -1):
        for h in both:
            for kinds in ((0,), (1,)):
                steps.append(("ring2" if h and d < 0 and kinds[0] else "", functools.partial(arrive, 2, d, kinds, h)))
    for h in both:
        steps.append(("far1" if h else "", functools.partial(arrive, 2, 0, (2, 3), h)))
    for h in both:
        for kinds in ((0,), (1,)):
            steps.append(("", functools.partial(arrive, 2, 2, kinds, h)))
    for d in (1, -1):
        for h in both:
            steps.append(("far2" if h and d < 0 else "", functools.partial(arrive, 2, d, (2, 3), h)))
    for h in both:
        steps.append(("end" if h else "", functools.partial(arrive, 2, 2, (2, 3), h)))

    works = []

    def ranks_of_other():
        cand_over.wait_recv()
        ranks(1 - k)

    works.append(("cand", lambda: ranks(k), 1.0))
    works.append(("over", ranks_of_other, 1.0))

    def placed(places, ready):
        works.append((ready, functools.partial(take, places), 0.0))
        for place in places:
            works.append((ready, functools.partial(place_rows, place), 0.4))

    def scored(group, ready):
        for c in range(0, MINE, 4):
            works.append((ready, functools.partial(logits, group, c, 4), 0.8))
        first, count = GROUPS[group]
        for place in range(first, first + count):
            works.append((ready, functools.partial(partial, place), 0.4))

    placed((0, 1, 2, 3, 4), "ring1")
    works.append(("ring1", functools.partial(rows_start, 0), 0.0))
    scored(0, "ring1")
    placed((5, 6, 7, 8), "ring2")
    placed((9, 10), "far1")
    works.append(("far1", functools.partial(rows_start, 1), 0.0))
    scored(1, "far1")
    placed((11, 12, 13, 14), "far2")
    placed((15,), "end")

    done = set()
    for name, step in steps:
        if step is not None:
            step()
        done.add(name)
        spent = 0.0
        while works and works[0][0] in done and spent < BUDGET:
            spent += works[0][2]
            works.pop(0)[1]()
    for _, work, _ in works:
        work()
    rows_start(2)
    scored_now = len(GROUPS) - 1
    logits(scored_now, 0, MINE)
    for place in range(GROUPS[-1][0], PLANE):
        partial(place)

    others = PV.at[pl.ds(0, SRC - 1)]
    pltpu.make_async_copy(others, others, lse_sem.at[1]).wait()
    parts = PV[...]
    top = jnp.max(parts, axis=0, keepdims=True)
    LV2[pl.ds(k, 1)] = top + jnp.log(jnp.sum(jnp.exp(parts - top), axis=0, keepdims=True))

    def send_total(place, device):
        remote(
            LV2.at[k], LV2.at[2 * mirrored(place) + k], lse_sem.at[2], lse_sem.at[3], device
        ).start()

    send_total(0, sibling)
    for place in range(1, PLANE):
        for kk in both:
            send_total(place, (z * 2 + kk, at(*SPOTS[place])))
    others = LV2.at[pl.ds(0, SRC - 1)]
    pltpu.make_async_copy(others, others, lse_sem.at[3]).wait()

    def cell_shift(c):
        rank = RK[:, :, pl.ds(c, 1), :].reshape(SRC, 1, VEC)
        found = jnp.where(rank == numbers(SRC), LV2[...], HIGH)
        return jnp.min(found, axis=2, keepdims=True).reshape(ROWS, 1)

    def cell_sum(c):
        weights = jnp.exp(L[c] - cell_shift(c)).astype(BF16)
        MS[c] = jnp.sum(weights.astype(F32), axis=0, keepdims=True)
        return lax.dot_general(
            weights, R[c], (((0,), (0,)), ((), ())), preferred_element_type=F32
        )

    def cell_of(step, i):
        return ring(z + step) * QUARTER + i

    landing = (RN, RP)
    toward = (z_next, z_prev)

    def reduce_message(way, number):
        return remote(
            S.at[way, number], landing[way].at[number],
            rs_send.at[way, number], rs_recv.at[way, number], toward[way],
        )

    def out_cell(step, i):
        return out.at[k * MINE + cell_of(step, i)]

    def out_message(kind, i):
        ref = out_cell((0, 0, -1, 1)[kind], i)
        return remote(ref, ref, og_send.at[kind, i], og_recv.at[kind, i], toward[kind % 2])

    def out_sibling(step, i):
        ref = out_cell(step, i)
        return remote(ref, ref, os_send.at[step % 4, i], os_recv.at[step % 4, i], sibling)

    diagonal = lax.broadcasted_iota(jnp.int32, (CELL, CELL), 0) == lax.broadcasted_iota(
        jnp.int32, (CELL, CELL), 1
    )

    def finish(i, total, mass_row, mass):
        c = z * QUARTER + i
        mass = mass + jnp.sum(
            jnp.where(diagonal, jnp.broadcast_to(mass_row, (CELL, CELL)), 0.0),
            axis=1,
            keepdims=True,
        )
        out[k * MINE + c] = (
            (total + PRIOR_MASS * C[c].astype(F32)) / (mass + PRIOR_MASS)
        ).astype(BF16)
        out_message(0, i).start()
        out_message(1, i).start()
        out_sibling(0, i).start()

    for way in both:
        S[way, 0] = cell_sum(cell_of(2, way)).astype(BF16)
        reduce_message(way, 0).start()
    for way in both:
        S[way, 1] = cell_sum(cell_of(1 - 2 * way, 1 - way)).astype(BF16)
        reduce_message(way, 1).start()

    eye = lax.broadcasted_iota(jnp.int32, (ROWS, ROWS), 0) == lax.broadcasted_iota(
        jnp.int32, (ROWS, ROWS), 1
    )
    for j in (2, 0, 1):
        for i in range(ROUTED):
            shift = cell_shift(cell_of(column_step[j], QUARTER - ROUTED + i))
            wide = jnp.where(eye, jnp.broadcast_to(shift, (ROWS, ROWS)), 0.0)
            SHR[j, i] = jnp.sum(wide, axis=0, keepdims=True)
        shift_message(j).start()

    for way in both:
        SF[way] = cell_sum(cell_of(1 - 2 * way, way))

    def own_sum(i, carry):
        SF[2 + i] = cell_sum(z * QUARTER + i)
        return carry

    lax.fori_loop(0, QUARTER, own_sum, 0)
    MR[z] = MS[...]
    for j, device in enumerate((z_next, z_prev, z_far)):
        remote(MS, MR.at[z], mass_sem.at[j], mass_sem.at[3], device).start()
    for j in range(3):
        shift_message(j).wait_recv()
        for group in range(len(GROUPS)):
            rows_message(group, j).wait_recv()
    def finish_rows(i):
        c = z * QUARTER + (QUARTER - ROUTED) + i
        mass = 0.0
        total = SF[2 + QUARTER - ROUTED + i]
        for j in range(3):
            rows = R3[j, i]
            products = lax.dot_general(C[c], rows, last, preferred_element_type=F32)
            value = (2.0 * products - SQC[i][:, 0:1]) * D**-0.5
            weights = jnp.exp(value - SHZ[j, i]).astype(BF16)
            mass = mass + jnp.sum(weights.astype(F32), axis=1, keepdims=True)
            total = total + jnp.dot(weights, rows, preferred_element_type=F32)
        finish(QUARTER - ROUTED + i, total, MS[c], mass)

    finish_rows(0)
    for way in both:
        reduce_message(way, 0).wait_recv()
        S[way, 2] = (SF[way] + landing[way][0].astype(F32)).astype(BF16)
        reduce_message(way, 2).start()
    finish_rows(1)
    others = MR.at[pl.ds(0, SIDE - 1)]
    pltpu.make_async_copy(others, others, mass_sem.at[3]).wait()

    def out_arrive(i):
        for kind in both:
            out_message(kind, i).wait_recv()
            if i % 2 == kind:
                out_message(2 + kind, i).start()
            out_sibling(-1 if kind == 0 else 1, i).start()

    out_arrive(2)
    for i in both:
        reduce_message(0, 2 - i).wait_recv()
        reduce_message(1, 1 + i).wait_recv()
        c = z * QUARTER + i
        total = SF[2 + i] + RN[2 - i].astype(F32) + RP[1 + i].astype(F32)
        finish(i, total, MR[0, c] + MR[1, c] + MR[2, c] + MR[3, c], 0.0)

    for i in (3, 0, 1):
        out_arrive(i)
    for i in (2, 3, 0, 1):
        out_message(2 + i % 2, i).wait_recv()
        out_sibling(2, i).start()
    for step in (0, -1, 1, 2):
        for i in range(QUARTER):
            out_sibling(step, i).wait_recv()

    for h in both:
        for stage, d in ((1, 0), (2, 0), (2, 1), (2, -1), (2, 2)):
            for kind in range(4):
                if (stage, d, kind) not in drained:
                    message(h, stage, d, kind).wait_send()
        for place in range(PLANE):
            to_sibling(h, place).wait_send()
    for number in range(6):
        cand_message(number).wait_send()
    cand_over.wait_send()
    for j in range(3):
        shift_message(j).wait_send()
        for group in range(len(GROUPS)):
            rows_message(group, j).wait_send()
    sent = PV.at[pl.ds(0, SRC - 1)]
    pltpu.make_async_copy(sent, sent, lse_sem.at[0]).wait()
    pltpu.make_async_copy(sent, sent, lse_sem.at[2]).wait()
    for way in (0, 1):
        for number in range(3):
            reduce_message(way, number).wait_send()
    for j, device in enumerate((z_next, z_prev, z_far)):
        remote(MS, MR.at[z], mass_sem.at[j], mass_sem.at[3], device).wait_send()
    for i in range(QUARTER):
        out_message(0, i).wait_send()
        out_message(1, i).wait_send()
        out_message(2 + i % 2, i).wait_send()
        for step in (0, -1, 1, 2):
            out_sibling(step, i).wait_send()


def body(vectors, candidates, centroids):
    cells = centroids.shape[0] // CELL
    dma = pltpu.SemaphoreType.DMA
    any_space = pl.BlockSpec(memory_space=pl.ANY)
    refined = pl.pallas_call(
        kernel,
        out_shape=pltpu.VMEM((cells, CELL, D), BF16),
        in_specs=[any_space] * 3,
        out_specs=pl.BlockSpec(memory_space=pltpu.VMEM),
        scratch_shapes=[
            pltpu.VMEM((SRC, VEC, D), BF16),
            pltpu.VMEM((SRC, 8, VEC), jnp.int32),
            pltpu.VMEM((MINE, CELL, D), BF16),
            pltpu.VMEM((MINE, ROWS, D), BF16),
            pltpu.VMEM((PLANE, 2, MINE, VEC), F32),
            pltpu.VMEM((PLANE * MINE, VEC), BF16),
            pltpu.VMEM((VEC, VEC), BF16),
            pltpu.VMEM((MINE, 8, CELL), F32),
            pltpu.VMEM((MINE, ROWS, CELL), F32),
            pltpu.VMEM((MINE, ROWS, CELL), F32),
            pltpu.VMEM((SRC, 1, VEC), F32),
            pltpu.VMEM((SRC, 1, VEC), F32),
            pltpu.VMEM((SRC, 1, VEC), F32),
            pltpu.VMEM((MINE, 1, CELL), F32),
            pltpu.VMEM((SIDE, MINE, 1, CELL), F32),
            pltpu.VMEM((2, 3, CELL, D), BF16),
            pltpu.VMEM((2 + QUARTER, CELL, D), F32),
            pltpu.VMEM((3, CELL, D), BF16),
            pltpu.VMEM((3, CELL, D), BF16),
            pltpu.VMEM((3, ROUTED, ROWS, D), BF16),
            pltpu.VMEM((3, ROUTED, 1, ROWS), F32),
            pltpu.VMEM((3, ROUTED, 1, ROWS), F32),
            pltpu.VMEM((ROUTED, CELL, CELL), F32),
            dma((3, 3)),
            dma((3, 3)),
            dma((3,)),
            dma((3,)),
            dma((3,)),
            dma((7,)),
            dma((7,)),
            dma((2, 20)),
            dma((2, 20)),
            dma((2, 16)),
            dma((2, 16)),
            dma((4,)),
            dma((2, 3)),
            dma((2, 3)),
            dma((4,)),
            dma((4, 4)),
            dma((4, 4)),
            dma((4, 4)),
            dma((4, 4)),
        ],
        compiler_params=pltpu.CompilerParams(
            collective_id=0, has_side_effects=True, vmem_limit_bytes=48 * 1024 * 1024
        ),
        name="refine",
    )(vectors, candidates.T, centroids.reshape(cells, CELL, D))
    return refined.reshape(cells * CELL, D)


def solution(mesh):
    placed = (P(("grp", "own"), None), P(("grp", "own"), None), P("own", None))
    return jax.shard_map(
        body, mesh=mesh, in_specs=placed, out_specs=P("own", None), check_vma=False
    )
```

```python
import functools

import jax
import jax.numpy as jnp
from jax import lax
from jax.experimental import pallas as pl
from jax.experimental.pallas import tpu as pltpu
from jax.sharding import PartitionSpec as P

MESH = pl.DeviceIdType.MESH
F32 = jnp.float32
BF16 = jnp.bfloat16

CELL = 128
SLOTS = 8
VEC = 256
D = 768
SIDE = 4
PLANE = SIDE * SIDE
SRC = 2 * PLANE
MINE = 16
QUARTER = MINE // SIDE
ROWS = SRC * SLOTS
ROUTED = 2
PRIOR_MASS = 1.0
LOW = -1e30
HIGH = 1e30

HALF = VEC // 2
FOURTH = VEC // 4


BUDGET = 1.0
SPOTS = (
    (0, 0), (1, 0), (-1, 0), (0, 1), (0, -1), (1, 1), (2, 0), (0, 2),
    (1, -1), (-1, 1), (-1, -1), (2, 1), (1, 2), (2, -1), (-1, 2), (2, 2),
)
GROUPS = ((0, 5), (5, 6), (11, 5))


def mirrored(place):
    dx, dy = (0 if v == 0 else 2 if v == 2 else -v for v in SPOTS[place])
    return SPOTS.index((dx, dy))


def ring(i):
    return lax.rem(i + 2 * SIDE, SIDE)


def kernel(
    vec, cand, cents, out,
    X, CD, C, CT, R, RK, H, U, SQ, L, LB, LVS, PV, LV2, MS, MR, S, SF, RN, RP,
    R3, SHR, SHZ, SQC,
    rows_send, rows_recv, shift_send, shift_recv, load_sem, cand_send, cand_recv, ag_send, ag_recv, sib_send, sib_recv, lse_sem,
    rs_send, rs_recv, mass_sem, og_send, og_recv, os_send, os_recv,
):
    grp = lax.axis_index("grp")
    own = lax.axis_index("own")
    z, k = lax.div(grp, 2), lax.rem(grp, 2)
    y, x = lax.div(own, SIDE), lax.rem(own, SIDE)
    sibling = (z * 2 + 1 - k, own)
    z_next = (ring(z + 1) * 2 + k, own)
    z_prev = (ring(z - 1) * 2 + k, own)
    z_far = (ring(z + 2) * 2 + k, own)
    me = k * PLANE + own
    both = (0, 1)
    last = (((1,), (1,)), ((), ()))

    def at(dx, dy):
        return ring(y + dy) * SIDE + ring(x + dx)

    def remote(src, dst, send, recv, device):
        return pltpu.make_async_remote_copy(
            src_ref=src, dst_ref=dst, send_sem=send, recv_sem=recv,
            device_id=device, device_id_type=MESH,
        )

    loads = [
        pltpu.make_async_copy(vec, X.at[me], load_sem.at[0]),
        pltpu.make_async_copy(cand, CD.at[me], load_sem.at[1]),
        pltpu.make_async_copy(cents.at[pl.ds(k * MINE, MINE)], C, load_sem.at[2]),
    ]
    for load in loads:
        load.start()
    x_next, x_prev = (grp, at(1, 0)), (grp, at(-1, 0))
    y_next, y_prev = (grp, at(0, 1)), (grp, at(0, -1))
    x_far, y_far = (grp, at(2, 0)), (grp, at(0, 2))
    near = (x_next, x_prev, x_far, y_next, y_prev, y_far, sibling, z_next, z_prev, z_far)
    barrier = pltpu.get_barrier_semaphore()
    for device in near:
        pl.semaphore_signal(barrier, inc=1, device_id=device, device_id_type=MESH)
    pl.semaphore_wait(barrier, len(near))

    def block(h, first, second):
        return at(first, second) if h == 0 else at(second, first)

    def axis_peer(h, stage, step):
        along_x = (h == 0) == (stage == 1)
        return (grp, at(step, 0) if along_x else at(0, step))

    def rows_of(h, part):
        if part == 2:
            return pl.ds(h * HALF, HALF)
        return pl.ds(h * HALF + part * FOURTH, FOURTH)

    def message(h, stage, d, kind):
        place = 0 if stage == 1 else 1 + d % 4
        number = 4 * place + kind
        step = 1 if kind in (0, 2) else -1
        back = 0 if kind < 2 else -step
        blk = block(h, back, 0) if stage == 1 else block(h, d, back)
        ref = X.at[k * PLANE + blk, rows_of(h, 2 if kind < 2 else kind - 2)]
        return remote(
            ref, ref, ag_send.at[h, number], ag_recv.at[h, number], axis_peer(h, stage, step)
        )

    def start(stage, d, kinds):
        for kind in kinds:
            for h in both:
                message(h, stage, d, kind).start()

    def to_sibling(h, place):
        ref = X.at[k * PLANE + at(*SPOTS[place]), rows_of(h, 2)]
        return remote(ref, ref, sib_send.at[h, place], sib_recv.at[h, place], sibling)

    def pass_on(h, first, second):
        to_sibling(h, SPOTS.index((first, second) if h == 0 else (second, first))).start()

    def arrive(stage, d, kinds, h):
        for kind in kinds:
            message(h, stage, d, kind).wait_recv()
            if kind < 2:
                side = -1 if kind == 0 else 1
                message(h, stage, d, 2 + kind).start()
                if stage == 1:
                    pass_on(h, side, 0)
                else:
                    pass_on(h, d, side)
        if kinds[-1] == 3:
            if stage == 1:
                pass_on(h, 2, 0)
            else:
                pass_on(h, d, 2)

    def take(places):
        for place in places:
            for h in both:
                to_sibling(h, place).wait_recv()

    def cand_message(number):
        if number < 3:
            ref = CD.at[pl.ds(k * PLANE + own, 1)]
            device = (x_next, x_prev, x_far)[number]
        else:
            ref = CD.at[pl.ds(k * PLANE + y * SIDE, SIDE)]
            device = (y_next, y_prev, y_far)[number - 3]
        return remote(ref, ref, cand_send.at[number], cand_recv.at[number], device)

    group_cand = CD.at[pl.ds(k * PLANE, PLANE)]
    cand_over = remote(group_cand, group_cand, cand_send.at[6], cand_recv.at[6], sibling)

    def cand_start(numbers):
        for number in numbers:
            cand_message(number).start()

    def cand_arrive(numbers):
        for number in numbers:
            cand_message(number).wait_recv()

    column = (z_next, z_prev, z_far)
    column_step = (1, -1, 2)

    def rows_message(place, j):
        slots = pl.ds(place * 2 * SLOTS, 2 * SLOTS)
        cells = pl.ds(ring(z + column_step[j]) * QUARTER + (QUARTER - ROUTED), ROUTED)
        return remote(
            R.at[cells, slots], R3.at[j, :, slots], rows_send.at[j, place], rows_recv.at[j, place],
            column[j],
        )

    def shift_message(j):
        return remote(SHR.at[j], SHZ.at[j], shift_send.at[j], shift_recv.at[j], column[j])

    def turned(first, count):
        if not first:
            loads[2].wait()
        for c in range(first, first + count):
            block_t = C[c].T
            CT[c] = block_t
            value = block_t.astype(F32)
            SQ[c] = jnp.broadcast_to(jnp.sum(value * value, axis=0, keepdims=True), (8, CELL))

    def own_norms():
        for j in range(ROUTED):
            value = C[z * QUARTER + (QUARTER - ROUTED) + j].astype(F32)
            SQC[j] = jnp.broadcast_to(
                jnp.sum(value * value, axis=1, keepdims=True), (CELL, CELL)
            )

    def triangle():
        U[...] = jnp.where(
            lax.broadcasted_iota(jnp.int32, (VEC, VEC), 0)
            < lax.broadcasted_iota(jnp.int32, (VEC, VEC), 1),
            1.0,
            0.0,
        ).astype(BF16)

    def ranks(kk):
        labels = lax.broadcasted_iota(jnp.int32, (MINE, VEC), 0) + (own * 2 + k) * MINE
        for place, spot in enumerate(SPOTS):
            named = CD[kk * PLANE + at(*spot)]
            hit = named[0:1] == labels
            for i in range(1, 8):
                hit = hit | (named[i : i + 1] == labels)
            H[place * MINE : (place + 1) * MINE] = jnp.where(hit, 1.0, 0.0).astype(BF16)
        hits = H[...]
        rank = jnp.dot(hits, U[...], preferred_element_type=F32)
        slot = jnp.where(hits.astype(F32) > 0.5, rank, -1.0)
        RK[:, kk] = slot.reshape(PLANE, MINE, VEC)

    def numbers(count):
        return lax.broadcasted_iota(jnp.int32, (count, SLOTS, VEC), 1).astype(F32)

    def slot_mask(place, kk):
        return RK[place, kk][:, None, :] == numbers(MINE)

    def place_rows(place):
        parts = []
        for kk in both:
            pick = jnp.where(slot_mask(place, kk), 1.0, 0.0).reshape(MINE * SLOTS, VEC)
            rows = jnp.dot(
                pick.astype(BF16), X[kk * PLANE + at(*SPOTS[place])], preferred_element_type=F32
            )
            parts.append(rows.reshape(MINE, SLOTS, D))
        base = place * 2 * SLOTS
        R[:, base : base + 2 * SLOTS, :] = jnp.concatenate(parts, axis=1).astype(BF16)
        for j in (2, 0, 1):
            rows_message(place, j).start()

    def logits(group, first_cell, cells):
        first, count = GROUPS[group]
        slots = slice(first * 2 * SLOTS, (first + count) * 2 * SLOTS)
        for c in range(first_cell, first_cell + cells):
            products = jnp.dot(R[c, slots], CT[c], preferred_element_type=F32)
            value = (2.0 * products - SQ[c][0:1]) * D**-0.5
            L[c, slots] = value
            top = jnp.max(value, axis=1, keepdims=True)
            total = jnp.sum(jnp.exp(value - top), axis=1, keepdims=True)
            LB[c, slots] = jnp.broadcast_to(top + jnp.log(total), (count * 2 * SLOTS, CELL))

    def partial(place):
        for kk in both:
            base = (place * 2 + kk) * SLOTS
            part = LB[:, base : base + SLOTS, :]
            wide = jnp.concatenate([part, part], axis=2)
            mask = slot_mask(place, kk)
            known = jnp.where(mask, wide, LOW)
            top = jnp.max(jnp.max(known, axis=0), axis=0, keepdims=True)
            terms = jnp.where(mask, jnp.exp(known - top[None]), 0.0)
            total = jnp.sum(jnp.sum(terms, axis=0), axis=0, keepdims=True)
            LVS[2 * place + kk] = top + jnp.log(jnp.maximum(total, 1e-30))
            if place:
                send_partial(2 * place + kk, (z * 2 + kk, at(*SPOTS[place])))
        if not place:
            PV[me] = LVS[k]
            send_partial(1 - k, sibling)

    def send_partial(number, device):
        remote(LVS.at[number], PV.at[me], lse_sem.at[0], lse_sem.at[1], device).start()

    loads[1].wait()
    cand_start((0, 1, 2))
    loads[0].wait()
    start(1, 0, (0, 1))
    for h in both:
        pass_on(h, 0, 0)
    triangle()
    cand_arrive((0, 1, 2))
    cand_start((3, 4, 5))
    start(2, 0, (0, 1))
    drained = set()

    steps = []
    for h in both:
        steps.append(("", functools.partial(arrive, 1, 0, (0, 1), h)))
    steps.append(("", lambda: start(2, 1, (0, 1))))
    steps.append(("", lambda: cand_arrive((3, 4, 5))))
    steps.append(("cand", cand_over.start))
    for h in both:
        steps.append(("ring1" if h else "", functools.partial(arrive, 2, 0, (0, 1), h)))
    steps.append(("over", lambda: start(2, -1, (0, 1))))
    for h in both:
        steps.append(("", functools.partial(arrive, 1, 0, (2, 3), h)))
    steps.append(("", lambda: start(2, 2, (0, 1))))
    for h in both:
        for kinds in ((0,), (1,)):
            name = "ring2" if h and kinds[0] else ""
            steps.append((name, functools.partial(arrive, 2, 1, kinds, h)))
    for h in both:
        steps.append(("far1" if h else "", functools.partial(arrive, 2, 0, (2, 3), h)))
    for h in both:
        for kinds in ((0,), (1,)):
            name = "ring3" if h and kinds[0] else ""
            steps.append((name, functools.partial(arrive, 2, -1, kinds, h)))
    for h in both:
        for kinds in ((0,), (1,)):
            steps.append(("", functools.partial(arrive, 2, 2, kinds, h)))
    for d in (1, -1):
        for h in both:
            name = "" if not h else "far2" if d > 0 else "far3"
            steps.append((name, functools.partial(arrive, 2, d, (2, 3), h)))
    for h in both:
        steps.append(("end" if h else "", functools.partial(arrive, 2, 2, (2, 3), h)))

    placing, scoring = [], []
    for c in range(0, MINE, 2):
        scoring.append(("", functools.partial(turned, c, 2), 0.5))
    scoring.append(("", own_norms, 0.3))

    def ranks_of_other():
        cand_over.wait_recv()
        ranks(1 - k)

    placing.append(("cand", lambda: ranks(k), 1.0))
    placing.append(("over", ranks_of_other, 1.0))

    def placed(places, ready):
        placing.append((ready, functools.partial(take, places), 0.0))
        for place in places:
            placing.append((ready, functools.partial(place_rows, place), 0.4))

    def scored(group, ready):
        for c in range(0, MINE, 4):
            scoring.append((ready, functools.partial(logits, group, c, 4), 0.3))
        first, count = GROUPS[group]
        for place in range(first, first + count):
            scoring.append((ready, functools.partial(partial, place), 0.2))

    placed((0,), "over")
    placed((1, 2, 3, 4), "ring1")
    placed((5,), "ring2")
    placed((6, 7), "far1")
    placed((8, 9, 10), "ring3")
    placed((11, 12), "far2")
    placed((13, 14), "far3")
    placed((15,), "end")
    scored(0, ("placed", 4))
    scored(1, ("placed", 10))

    done = {""}

    def advance(works, spent):
        while works and works[0][0] in done and spent < BUDGET:
            _, work, cost = works.pop(0)
            work()
            spent += cost
            if work.__class__ is functools.partial and work.func is place_rows:
                done.add(("placed", work.args[0]))
        return spent

    for name, step in steps:
        if step is not None:
            step()
        done.add(name)
        advance(scoring, advance(placing, 0.0))
    for works in (placing, scoring):
        for _, work, _ in works:
            work()
    scored_now = len(GROUPS) - 1
    logits(scored_now, 0, MINE)
    for place in range(GROUPS[-1][0], PLANE):
        partial(place)

    others = PV.at[pl.ds(0, SRC - 1)]
    pltpu.make_async_copy(others, others, lse_sem.at[1]).wait()
    parts = PV[...]
    top = jnp.max(parts, axis=0, keepdims=True)
    LV2[pl.ds(k, 1)] = top + jnp.log(jnp.sum(jnp.exp(parts - top), axis=0, keepdims=True))

    def send_total(place, device):
        remote(
            LV2.at[k], LV2.at[2 * mirrored(place) + k], lse_sem.at[2], lse_sem.at[3], device
        ).start()

    send_total(0, sibling)
    for place in range(1, PLANE):
        for kk in both:
            send_total(place, (z * 2 + kk, at(*SPOTS[place])))
    others = LV2.at[pl.ds(0, SRC - 1)]
    pltpu.make_async_copy(others, others, lse_sem.at[3]).wait()

    def cell_shift(c):
        rank = RK[:, :, pl.ds(c, 1), :].reshape(SRC, 1, VEC)
        found = jnp.where(rank == numbers(SRC), LV2[...], HIGH)
        return jnp.min(found, axis=2, keepdims=True).reshape(ROWS, 1)

    def cell_sum(c):
        weights = jnp.exp(L[c] - cell_shift(c)).astype(BF16)
        MS[c] = jnp.sum(weights.astype(F32), axis=0, keepdims=True)
        return lax.dot_general(
            weights, R[c], (((0,), (0,)), ((), ())), preferred_element_type=F32
        )

    def cell_of(step, i):
        return ring(z + step) * QUARTER + i

    landing = (RN, RP)
    toward = (z_next, z_prev)

    def reduce_message(way, number):
        return remote(
            S.at[way, number], landing[way].at[number],
            rs_send.at[way, number], rs_recv.at[way, number], toward[way],
        )

    def out_cell(step, i):
        return out.at[k * MINE + cell_of(step, i)]

    def out_message(kind, i):
        ref = out_cell((0, 0, -1, 1)[kind], i)
        return remote(ref, ref, og_send.at[kind, i], og_recv.at[kind, i], toward[kind % 2])

    def out_sibling(step, i):
        ref = out_cell(step, i)
        return remote(ref, ref, os_send.at[step % 4, i], os_recv.at[step % 4, i], sibling)

    diagonal = lax.broadcasted_iota(jnp.int32, (CELL, CELL), 0) == lax.broadcasted_iota(
        jnp.int32, (CELL, CELL), 1
    )

    def finish(i, total, mass_row, mass):
        c = z * QUARTER + i
        mass = mass + jnp.sum(
            jnp.where(diagonal, jnp.broadcast_to(mass_row, (CELL, CELL)), 0.0),
            axis=1,
            keepdims=True,
        )
        out[k * MINE + c] = (
            (total + PRIOR_MASS * C[c].astype(F32)) / (mass + PRIOR_MASS)
        ).astype(BF16)
        out_message(0, i).start()
        out_message(1, i).start()
        out_sibling(0, i).start()

    eye = lax.broadcasted_iota(jnp.int32, (ROWS, ROWS), 0) == lax.broadcasted_iota(
        jnp.int32, (ROWS, ROWS), 1
    )
    for j in (2, 0, 1):
        for i in range(ROUTED):
            shift = cell_shift(cell_of(column_step[j], QUARTER - ROUTED + i))
            wide = jnp.where(eye, jnp.broadcast_to(shift, (ROWS, ROWS)), 0.0)
            SHR[j, i] = jnp.sum(wide, axis=0, keepdims=True)
        shift_message(j).start()

    for way in both:
        S[way, 0] = cell_sum(cell_of(2, way)).astype(BF16)
        reduce_message(way, 0).start()
    for way in both:
        S[way, 1] = cell_sum(cell_of(1 - 2 * way, 1 - way)).astype(BF16)
        reduce_message(way, 1).start()

    for way in both:
        SF[way] = cell_sum(cell_of(1 - 2 * way, way))

    def own_sum(i, carry):
        SF[2 + i] = cell_sum(z * QUARTER + i)
        return carry

    lax.fori_loop(0, QUARTER, own_sum, 0)
    MR[z] = MS[...]
    for j, device in enumerate((z_next, z_prev, z_far)):
        remote(MS, MR.at[z], mass_sem.at[j], mass_sem.at[3], device).start()
    for j in range(3):
        shift_message(j).wait_recv()
        for place in range(PLANE):
            rows_message(place, j).wait_recv()
    def finish_rows(i):
        c = z * QUARTER + (QUARTER - ROUTED) + i
        mass = 0.0
        total = SF[2 + QUARTER - ROUTED + i]
        for j in range(3):
            rows = R3[j, i]
            products = lax.dot_general(C[c], rows, last, preferred_element_type=F32)
            value = (2.0 * products - SQC[i][:, 0:1]) * D**-0.5
            weights = jnp.exp(value - SHZ[j, i]).astype(BF16)
            mass = mass + jnp.sum(weights.astype(F32), axis=1, keepdims=True)
            total = total + jnp.dot(weights, rows, preferred_element_type=F32)
        finish(QUARTER - ROUTED + i, total, MS[c], mass)

    finish_rows(0)
    for way in both:
        reduce_message(way, 0).wait_recv()
        S[way, 2] = (SF[way] + landing[way][0].astype(F32)).astype(BF16)
        reduce_message(way, 2).start()
    finish_rows(1)
    others = MR.at[pl.ds(0, SIDE - 1)]
    pltpu.make_async_copy(others, others, mass_sem.at[3]).wait()

    def out_arrive(i):
        for kind in both:
            out_message(kind, i).wait_recv()
            if i % 2 == kind:
                out_message(2 + kind, i).start()
            out_sibling(-1 if kind == 0 else 1, i).start()

    out_arrive(2)
    for i in both:
        reduce_message(0, 2 - i).wait_recv()
        reduce_message(1, 1 + i).wait_recv()
        c = z * QUARTER + i
        total = SF[2 + i] + RN[2 - i].astype(F32) + RP[1 + i].astype(F32)
        finish(i, total, MR[0, c] + MR[1, c] + MR[2, c] + MR[3, c], 0.0)

    for i in (3, 0, 1):
        out_arrive(i)
    for i in (2, 3, 0, 1):
        out_message(2 + i % 2, i).wait_recv()
        out_sibling(2, i).start()
    for step in (0, -1, 1, 2):
        for i in range(QUARTER):
            out_sibling(step, i).wait_recv()

    for h in both:
        for stage, d in ((1, 0), (2, 0), (2, 1), (2, -1), (2, 2)):
            for kind in range(4):
                if (stage, d, kind) not in drained:
                    message(h, stage, d, kind).wait_send()
        for place in range(PLANE):
            to_sibling(h, place).wait_send()
    for number in range(6):
        cand_message(number).wait_send()
    cand_over.wait_send()
    for j in range(3):
        shift_message(j).wait_send()
        for place in range(PLANE):
            rows_message(place, j).wait_send()
    sent = PV.at[pl.ds(0, SRC - 1)]
    pltpu.make_async_copy(sent, sent, lse_sem.at[0]).wait()
    pltpu.make_async_copy(sent, sent, lse_sem.at[2]).wait()
    for way in (0, 1):
        for number in range(3):
            reduce_message(way, number).wait_send()
    for j, device in enumerate((z_next, z_prev, z_far)):
        remote(MS, MR.at[z], mass_sem.at[j], mass_sem.at[3], device).wait_send()
    for i in range(QUARTER):
        out_message(0, i).wait_send()
        out_message(1, i).wait_send()
        out_message(2 + i % 2, i).wait_send()
        for step in (0, -1, 1, 2):
            out_sibling(step, i).wait_send()


def body(vectors, candidates, centroids):
    cells = centroids.shape[0] // CELL
    dma = pltpu.SemaphoreType.DMA
    any_space = pl.BlockSpec(memory_space=pl.ANY)
    refined = pl.pallas_call(
        kernel,
        out_shape=pltpu.VMEM((cells, CELL, D), BF16),
        in_specs=[any_space] * 3,
        out_specs=pl.BlockSpec(memory_space=pltpu.VMEM),
        scratch_shapes=[
            pltpu.VMEM((SRC, VEC, D), BF16),
            pltpu.VMEM((SRC, 8, VEC), jnp.int32),
            pltpu.VMEM((MINE, CELL, D), BF16),
            pltpu.VMEM((MINE, D, CELL), BF16),
            pltpu.VMEM((MINE, ROWS, D), BF16),
            pltpu.VMEM((PLANE, 2, MINE, VEC), F32),
            pltpu.VMEM((PLANE * MINE, VEC), BF16),
            pltpu.VMEM((VEC, VEC), BF16),
            pltpu.VMEM((MINE, 8, CELL), F32),
            pltpu.VMEM((MINE, ROWS, CELL), F32),
            pltpu.VMEM((MINE, ROWS, CELL), F32),
            pltpu.VMEM((SRC, 1, VEC), F32),
            pltpu.VMEM((SRC, 1, VEC), F32),
            pltpu.VMEM((SRC, 1, VEC), F32),
            pltpu.VMEM((MINE, 1, CELL), F32),
            pltpu.VMEM((SIDE, MINE, 1, CELL), F32),
            pltpu.VMEM((2, 3, CELL, D), BF16),
            pltpu.VMEM((2 + QUARTER, CELL, D), F32),
            pltpu.VMEM((3, CELL, D), BF16),
            pltpu.VMEM((3, CELL, D), BF16),
            pltpu.VMEM((3, ROUTED, ROWS, D), BF16),
            pltpu.VMEM((3, ROUTED, 1, ROWS), F32),
            pltpu.VMEM((3, ROUTED, 1, ROWS), F32),
            pltpu.VMEM((ROUTED, CELL, CELL), F32),
            dma((3, 16)),
            dma((3, 16)),
            dma((3,)),
            dma((3,)),
            dma((3,)),
            dma((7,)),
            dma((7,)),
            dma((2, 20)),
            dma((2, 20)),
            dma((2, 16)),
            dma((2, 16)),
            dma((4,)),
            dma((2, 3)),
            dma((2, 3)),
            dma((4,)),
            dma((4, 4)),
            dma((4, 4)),
            dma((4, 4)),
            dma((4, 4)),
        ],
        compiler_params=pltpu.CompilerParams(
            collective_id=0, has_side_effects=True, vmem_limit_bytes=48 * 1024 * 1024
        ),
        name="refine",
    )(vectors, candidates.T, centroids.reshape(cells, CELL, D))
    return refined.reshape(cells * CELL, D)


def solution(mesh):
    placed = (P(("grp", "own"), None), P(("grp", "own"), None), P("own", None))
    return jax.shard_map(
        body, mesh=mesh, in_specs=placed, out_specs=P("own", None), check_vma=False
    )
```

```python
import functools

import jax
import jax.numpy as jnp
from jax import lax
from jax.experimental import pallas as pl
from jax.experimental.pallas import tpu as pltpu
from jax.sharding import PartitionSpec as P

MESH = pl.DeviceIdType.MESH
F32 = jnp.float32
BF16 = jnp.bfloat16

CELL = 128
SLOTS = 8
VEC = 256
D = 768
SIDE = 4
PLANE = SIDE * SIDE
SRC = 2 * PLANE
MINE = 16
QUARTER = MINE // SIDE
ROWS = SRC * SLOTS
ROUTED = 2
PRIOR_MASS = 1.0
LOW = -1e30
HIGH = 1e30

HALF = VEC // 2
FOURTH = VEC // 4


BUDGET = 1.0
SPOTS = (
    (0, 0), (1, 0), (-1, 0), (0, 1), (0, -1), (1, 1), (2, 0), (0, 2),
    (1, -1), (-1, 1), (-1, -1), (2, 1), (1, 2), (2, -1), (-1, 2), (2, 2),
)
GROUPS = ((0, 5), (5, 6), (11, 2), (13, 3))
LATE = 13
FRESH = 2 * (PLANE - LATE)


def mirrored(place):
    dx, dy = (0 if v == 0 else 2 if v == 2 else -v for v in SPOTS[place])
    return SPOTS.index((dx, dy))


def behind(place, late):
    dx, dy = ((a - b + 5) % 4 - 1 for a, b in zip(SPOTS[place], SPOTS[late]))
    return SPOTS.index((dx, dy))


def ring(i):
    return lax.rem(i + 2 * SIDE, SIDE)


def kernel(
    vec, cand, cents, out,
    X, CD, CE, C, CT, R, RK, H, U, SQ, L, LB, LVS, PV, LV2, LT, MS, MR, S, SF, RN, RP,
    R3, SHR, SHZ, SQC,
    rows_send, rows_recv, shift_send, shift_recv, load_sem, cand_send, cand_recv, ag_send, ag_recv, sib_send, sib_recv, lse_sem,
    rs_send, rs_recv, mass_sem, og_send, og_recv, os_send, os_recv,
):
    grp = lax.axis_index("grp")
    own = lax.axis_index("own")
    z, k = lax.div(grp, 2), lax.rem(grp, 2)
    y, x = lax.div(own, SIDE), lax.rem(own, SIDE)
    sibling = (z * 2 + 1 - k, own)
    z_next = (ring(z + 1) * 2 + k, own)
    z_prev = (ring(z - 1) * 2 + k, own)
    z_far = (ring(z + 2) * 2 + k, own)
    me = k * PLANE + own
    both = (0, 1)
    last = (((1,), (1,)), ((), ()))

    def at(dx, dy):
        return ring(y + dy) * SIDE + ring(x + dx)

    def remote(src, dst, send, recv, device):
        return pltpu.make_async_remote_copy(
            src_ref=src, dst_ref=dst, send_sem=send, recv_sem=recv,
            device_id=device, device_id_type=MESH,
        )

    loads = [
        pltpu.make_async_copy(vec, X.at[me], load_sem.at[0]),
        pltpu.make_async_copy(cand, CD.at[me], load_sem.at[1]),
        pltpu.make_async_copy(cents.at[pl.ds(k * MINE, MINE)], C, load_sem.at[2]),
    ]
    for load in loads:
        load.start()
    x_next, x_prev = (grp, at(1, 0)), (grp, at(-1, 0))
    y_next, y_prev = (grp, at(0, 1)), (grp, at(0, -1))
    x_far, y_far = (grp, at(2, 0)), (grp, at(0, 2))
    near = (x_next, x_prev, x_far, y_next, y_prev, y_far, sibling, z_next, z_prev, z_far)
    barrier = pltpu.get_barrier_semaphore()
    for device in near:
        pl.semaphore_signal(barrier, inc=1, device_id=device, device_id_type=MESH)
    pl.semaphore_wait(barrier, len(near))

    def block(h, first, second):
        return at(first, second) if h == 0 else at(second, first)

    def axis_peer(h, stage, step):
        along_x = (h == 0) == (stage == 1)
        return (grp, at(step, 0) if along_x else at(0, step))

    def rows_of(h, part):
        if part == 2:
            return pl.ds(h * HALF, HALF)
        return pl.ds(h * HALF + part * FOURTH, FOURTH)

    def message(h, stage, d, kind):
        place = 0 if stage == 1 else 1 + d % 4
        number = 4 * place + kind
        step = 1 if kind in (0, 2) else -1
        back = 0 if kind < 2 else -step
        blk = block(h, back, 0) if stage == 1 else block(h, d, back)
        ref = X.at[k * PLANE + blk, rows_of(h, 2 if kind < 2 else kind - 2)]
        return remote(
            ref, ref, ag_send.at[h, number], ag_recv.at[h, number], axis_peer(h, stage, step)
        )

    def start(stage, d, kinds):
        for kind in kinds:
            for h in both:
                message(h, stage, d, kind).start()

    def to_sibling(h, place):
        ref = X.at[k * PLANE + at(*SPOTS[place]), rows_of(h, 2)]
        return remote(ref, ref, sib_send.at[h, place], sib_recv.at[h, place], sibling)

    def pass_on(h, first, second):
        to_sibling(h, SPOTS.index((first, second) if h == 0 else (second, first))).start()

    def arrive(stage, d, kinds, h):
        for kind in kinds:
            message(h, stage, d, kind).wait_recv()
            if kind < 2:
                side = -1 if kind == 0 else 1
                message(h, stage, d, 2 + kind).start()
                if stage == 1:
                    pass_on(h, side, 0)
                else:
                    pass_on(h, d, side)
        if kinds[-1] == 3:
            if stage == 1:
                pass_on(h, 2, 0)
            else:
                pass_on(h, d, 2)

    def take(places):
        for place in places:
            for h in both:
                to_sibling(h, place).wait_recv()

    def cand_message(number):
        if number < 3:
            ref = CD.at[pl.ds(k * PLANE + own, 1)]
            device = (x_next, x_prev, x_far)[number]
        else:
            ref = CD.at[pl.ds(k * PLANE + y * SIDE, SIDE)]
            device = (y_next, y_prev, y_far)[number - 3]
        return remote(ref, ref, cand_send.at[number], cand_recv.at[number], device)

    group_cand = CD.at[pl.ds(k * PLANE, PLANE)]
    cand_over = remote(group_cand, group_cand, cand_send.at[6], cand_recv.at[6], sibling)

    cand_near = remote(CD.at[me], CE, cand_send.at[7], cand_recv.at[7], sibling)

    def cand_start(numbers):
        for number in numbers:
            cand_message(number).start()

    def cand_arrive(numbers):
        for number in numbers:
            cand_message(number).wait_recv()

    column = (z_next, z_prev, z_far)
    column_step = (1, -1, 2)

    def rows_message(place, j):
        slots = pl.ds(place * 2 * SLOTS, 2 * SLOTS)
        cells = pl.ds(ring(z + column_step[j]) * QUARTER + (QUARTER - ROUTED), ROUTED)
        return remote(
            R.at[cells, slots], R3.at[j, :, slots], rows_send.at[j, place], rows_recv.at[j, place],
            column[j],
        )

    def shift_message(j):
        return remote(SHR.at[j], SHZ.at[j], shift_send.at[j], shift_recv.at[j], column[j])

    def turned(first, count):
        if not first:
            loads[2].wait()
        for c in range(first, first + count):
            block_t = C[c].T
            CT[c] = block_t
            value = block_t.astype(F32)
            SQ[c] = jnp.broadcast_to(jnp.sum(value * value, axis=0, keepdims=True), (8, CELL))

    def own_norms():
        for j in range(ROUTED):
            value = C[z * QUARTER + (QUARTER - ROUTED) + j].astype(F32)
            SQC[j] = jnp.broadcast_to(
                jnp.sum(value * value, axis=1, keepdims=True), (CELL, CELL)
            )

    def triangle():
        U[...] = jnp.where(
            lax.broadcasted_iota(jnp.int32, (VEC, VEC), 0)
            < lax.broadcasted_iota(jnp.int32, (VEC, VEC), 1),
            1.0,
            0.0,
        ).astype(BF16)

    def ranks(kk):
        labels = lax.broadcasted_iota(jnp.int32, (MINE, VEC), 0) + (own * 2 + k) * MINE
        for place, spot in enumerate(SPOTS):
            named = CD[kk * PLANE + at(*spot)]
            hit = named[0:1] == labels
            for i in range(1, 8):
                hit = hit | (named[i : i + 1] == labels)
            H[place * MINE : (place + 1) * MINE] = jnp.where(hit, 1.0, 0.0).astype(BF16)
        hits = H[...]
        rank = jnp.dot(hits, U[...], preferred_element_type=F32)
        slot = jnp.where(hits.astype(F32) > 0.5, rank, -1.0)
        RK[:, kk] = slot.reshape(PLANE, MINE, VEC)

    def own_ranks():
        labels = lax.broadcasted_iota(jnp.int32, (MINE, VEC), 0) + (own * 2 + k) * MINE
        for j, named in enumerate((CD[me], CE[...])):
            hit = named[0:1] == labels
            for i in range(1, 8):
                hit = hit | (named[i : i + 1] == labels)
            H[j * MINE : (j + 1) * MINE] = jnp.where(hit, 1.0, 0.0).astype(BF16)
        hits = H[0 : 2 * MINE]
        rank = jnp.dot(hits, U[...], preferred_element_type=F32)
        slot = jnp.where(hits.astype(F32) > 0.5, rank, -1.0)
        RK[0, k] = slot[0:MINE]
        RK[0, 1 - k] = slot[MINE:]

    def numbers(count):
        return lax.broadcasted_iota(jnp.int32, (count, SLOTS, VEC), 1).astype(F32)

    def slot_mask(place, kk):
        return RK[place, kk][:, None, :] == numbers(MINE)

    def place_rows(place):
        parts = []
        for kk in both:
            pick = jnp.where(slot_mask(place, kk), 1.0, 0.0).reshape(MINE * SLOTS, VEC)
            rows = jnp.dot(
                pick.astype(BF16), X[kk * PLANE + at(*SPOTS[place])], preferred_element_type=F32
            )
            parts.append(rows.reshape(MINE, SLOTS, D))
        base = place * 2 * SLOTS
        R[:, base : base + 2 * SLOTS, :] = jnp.concatenate(parts, axis=1).astype(BF16)
        for j in (2, 0, 1):
            rows_message(place, j).start()

    def logits(group, first_cell, cells):
        first, count = GROUPS[group]
        slots = slice(first * 2 * SLOTS, (first + count) * 2 * SLOTS)
        for c in range(first_cell, first_cell + cells):
            products = jnp.dot(R[c, slots], CT[c], preferred_element_type=F32)
            value = (2.0 * products - SQ[c][0:1]) * D**-0.5
            L[c, slots] = value
            top = jnp.max(value, axis=1, keepdims=True)
            total = jnp.sum(jnp.exp(value - top), axis=1, keepdims=True)
            LB[c, slots] = jnp.broadcast_to(top + jnp.log(total), (count * 2 * SLOTS, CELL))

    def partial(place):
        for kk in both:
            base = (place * 2 + kk) * SLOTS
            part = LB[:, base : base + SLOTS, :]
            wide = jnp.concatenate([part, part], axis=2)
            mask = slot_mask(place, kk)
            known = jnp.where(mask, wide, LOW)
            top = jnp.max(jnp.max(known, axis=0), axis=0, keepdims=True)
            terms = jnp.where(mask, jnp.exp(known - top[None]), 0.0)
            total = jnp.sum(jnp.sum(terms, axis=0), axis=0, keepdims=True)
            LVS[2 * place + kk] = top + jnp.log(jnp.maximum(total, 1e-30))
            if 0 < place < LATE:
                device = (z * 2 + kk, at(*SPOTS[place]))
                send_partial(2 * place + kk, 2 * place + k, device)
        if not place:
            PV[k] = LVS[k]
            send_partial(1 - k, k, sibling)

    def send_partial(number, there, device):
        remote(LVS.at[number], PV.at[there], lse_sem.at[0], lse_sem.at[1], device).start()

    def announce(src, dst, send, recv):
        for place in range(PLANE - 1, 0, -1):
            for kk in both:
                device = (z * 2 + kk, at(*SPOTS[place]))
                remote(src, dst.at[2 * mirrored(place) + k], send, recv, device).start()
        remote(src, dst.at[k], send, recv, sibling).start()

    loads[1].wait()
    cand_start((0, 1, 2))
    cand_near.start()
    loads[0].wait()
    start(1, 0, (0, 1))
    for h in both:
        pass_on(h, 0, 0)
    triangle()
    cand_arrive((0, 1, 2))
    cand_start((3, 4, 5))
    start(2, 0, (0, 1))
    cand_near.wait_recv()
    own_ranks()
    take((0,))
    place_rows(0)

    steps = []
    for h in both:
        steps.append(("", functools.partial(arrive, 1, 0, (0, 1), h)))
    steps.append(("", lambda: start(2, 1, (0, 1))))
    steps.append(("", lambda: cand_arrive((3, 4, 5))))
    steps.append(("cand", cand_over.start))
    for h in both:
        steps.append(("ring1" if h else "", functools.partial(arrive, 2, 0, (0, 1), h)))
    steps.append(("over", lambda: start(2, -1, (0, 1))))
    for h in both:
        steps.append(("", functools.partial(arrive, 1, 0, (2, 3), h)))
    steps.append(("", lambda: start(2, 2, (0, 1))))
    for h in both:
        for kinds in ((0,), (1,)):
            name = "ring2" if h and kinds[0] else ""
            steps.append((name, functools.partial(arrive, 2, 1, kinds, h)))
    for h in both:
        steps.append(("far1" if h else "", functools.partial(arrive, 2, 0, (2, 3), h)))
    for h in both:
        for kinds in ((0,), (1,)):
            name = "ring3" if h and kinds[0] else ""
            steps.append((name, functools.partial(arrive, 2, -1, kinds, h)))
    for h in both:
        for kinds in ((0,), (1,)):
            steps.append(("", functools.partial(arrive, 2, 2, kinds, h)))
    for d in (1, -1):
        for h in both:
            name = "" if not h else "far2" if d > 0 else "far3"
            steps.append((name, functools.partial(arrive, 2, d, (2, 3), h)))
    for h in both:
        steps.append(("end" if h else "", functools.partial(arrive, 2, 2, (2, 3), h)))

    placing, scoring = [], []
    for c in range(0, MINE, 2):
        scoring.append(("", functools.partial(turned, c, 2), 0.5))
    scoring.append(("", own_norms, 0.3))

    def ranks_of_other():
        cand_over.wait_recv()
        ranks(1 - k)

    placing.append(("cand", lambda: ranks(k), 1.0))
    placing.append(("over", ranks_of_other, 1.0))

    def placed(places, ready):
        placing.append((ready, functools.partial(take, places), 0.0))
        for place in places:
            placing.append((ready, functools.partial(place_rows, place), 0.4))

    def scored(group, ready):
        for c in range(0, MINE, 4):
            scoring.append((ready, functools.partial(logits, group, c, 4), 0.3))
        first, count = GROUPS[group]
        for place in range(first, first + count):
            scoring.append((ready, functools.partial(partial, place), 0.2))

    done = {"", ("placed", 0)}
    placed((1, 2, 3, 4), "ring1")
    placed((5,), "ring2")
    placed((6, 7), "far1")
    placed((8, 9, 10), "ring3")
    placed((11, 12), "far2")
    placed((13, 14), "far3")
    placed((15,), "end")
    scored(0, ("placed", 4))
    scored(1, ("placed", 10))
    scored(2, ("placed", 12))


    def advance(works, spent):
        while works and works[0][0] in done and spent < BUDGET:
            _, work, cost = works.pop(0)
            work()
            spent += cost
            if work.__class__ is functools.partial and work.func is place_rows:
                done.add(("placed", work.args[0]))
        return spent

    for name, step in steps:
        if step is not None:
            step()
        done.add(name)
        advance(scoring, advance(placing, 0.0))
    for works in (placing, scoring):
        for _, work, _ in works:
            work()
    logits(len(GROUPS) - 1, 0, MINE)
    for place in range(LATE, PLANE):
        partial(place)

    others = PV.at[pl.ds(0, 2 * LATE - 1)]
    pltpu.make_async_copy(others, others, lse_sem.at[1]).wait()
    parts = PV[...]
    top = jnp.max(parts, axis=0, keepdims=True)
    LVS[SRC : SRC + 1] = top + jnp.log(jnp.sum(jnp.exp(parts - top), axis=0, keepdims=True))
    LT[k] = LVS[SRC - FRESH :]
    announce(LVS.at[pl.ds(SRC - FRESH, FRESH + 1)], LT, lse_sem.at[2], lse_sem.at[3])
    others = LT.at[pl.ds(0, SRC - 1)]
    pltpu.make_async_copy(others, others, lse_sem.at[3]).wait()
    for place in range(PLANE):
        for kk in both:
            terms = [LT[2 * place + kk, FRESH]]
            for late in range(LATE, PLANE):
                for core in both:
                    terms.append(LT[2 * behind(place, late) + core, 2 * (late - LATE) + kk])
            top = functools.reduce(jnp.maximum, terms)
            LV2[2 * place + kk] = top + jnp.log(sum(jnp.exp(v - top) for v in terms))

    def cell_shift(c):
        rank = RK[:, :, pl.ds(c, 1), :].reshape(SRC, 1, VEC)
        found = jnp.where(rank == numbers(SRC), LV2[...], HIGH)
        return jnp.min(found, axis=2, keepdims=True).reshape(ROWS, 1)

    def cell_sum(c):
        weights = jnp.exp(L[c] - cell_shift(c)).astype(BF16)
        MS[c] = jnp.sum(weights.astype(F32), axis=0, keepdims=True)
        return lax.dot_general(
            weights, R[c], (((0,), (0,)), ((), ())), preferred_element_type=F32
        )

    def cell_of(step, i):
        return ring(z + step) * QUARTER + i

    landing = (RN, RP)
    toward = (z_next, z_prev)

    def reduce_message(way, number):
        return remote(
            S.at[way, number], landing[way].at[number],
            rs_send.at[way, number], rs_recv.at[way, number], toward[way],
        )

    def out_cell(step, i):
        return out.at[k * MINE + cell_of(step, i)]

    def out_message(kind, i):
        ref = out_cell((0, 0, -1, 1)[kind], i)
        return remote(ref, ref, og_send.at[kind, i], og_recv.at[kind, i], toward[kind % 2])

    def out_sibling(step, i):
        ref = out_cell(step, i)
        return remote(ref, ref, os_send.at[step % 4, i], os_recv.at[step % 4, i], sibling)

    diagonal = lax.broadcasted_iota(jnp.int32, (CELL, CELL), 0) == lax.broadcasted_iota(
        jnp.int32, (CELL, CELL), 1
    )

    def finish(i, total, mass_row, mass):
        c = z * QUARTER + i
        mass = mass + jnp.sum(
            jnp.where(diagonal, jnp.broadcast_to(mass_row, (CELL, CELL)), 0.0),
            axis=1,
            keepdims=True,
        )
        out[k * MINE + c] = (
            (total + PRIOR_MASS * C[c].astype(F32)) / (mass + PRIOR_MASS)
        ).astype(BF16)
        out_message(0, i).start()
        out_message(1, i).start()
        out_sibling(0, i).start()

    eye = lax.broadcasted_iota(jnp.int32, (ROWS, ROWS), 0) == lax.broadcasted_iota(
        jnp.int32, (ROWS, ROWS), 1
    )
    for j in (2, 0, 1):
        for i in range(ROUTED):
            shift = cell_shift(cell_of(column_step[j], QUARTER - ROUTED + i))
            wide = jnp.where(eye, jnp.broadcast_to(shift, (ROWS, ROWS)), 0.0)
            SHR[j, i] = jnp.sum(wide, axis=0, keepdims=True)
        shift_message(j).start()

    for way in both:
        S[way, 0] = cell_sum(cell_of(2, way)).astype(BF16)
        reduce_message(way, 0).start()
    for way in both:
        S[way, 1] = cell_sum(cell_of(1 - 2 * way, 1 - way)).astype(BF16)
        reduce_message(way, 1).start()

    for way in both:
        SF[way] = cell_sum(cell_of(1 - 2 * way, way))

    def own_sum(i, carry):
        SF[2 + i] = cell_sum(z * QUARTER + i)
        return carry

    lax.fori_loop(0, QUARTER, own_sum, 0)
    MR[z] = MS[...]
    for j, device in enumerate((z_next, z_prev, z_far)):
        remote(MS, MR.at[z], mass_sem.at[j], mass_sem.at[3], device).start()
    for j in range(3):
        shift_message(j).wait_recv()
        for place in range(PLANE):
            rows_message(place, j).wait_recv()
    def finish_rows(i):
        c = z * QUARTER + (QUARTER - ROUTED) + i
        mass = 0.0
        total = SF[2 + QUARTER - ROUTED + i]
        for j in range(3):
            rows = R3[j, i]
            products = lax.dot_general(C[c], rows, last, preferred_element_type=F32)
            value = (2.0 * products - SQC[i][:, 0:1]) * D**-0.5
            weights = jnp.exp(value - SHZ[j, i]).astype(BF16)
            mass = mass + jnp.sum(weights.astype(F32), axis=1, keepdims=True)
            total = total + jnp.dot(weights, rows, preferred_element_type=F32)
        finish(QUARTER - ROUTED + i, total, MS[c], mass)

    finish_rows(0)
    for way in both:
        reduce_message(way, 0).wait_recv()
        S[way, 2] = (SF[way] + landing[way][0].astype(F32)).astype(BF16)
        reduce_message(way, 2).start()
    finish_rows(1)
    others = MR.at[pl.ds(0, SIDE - 1)]
    pltpu.make_async_copy(others, others, mass_sem.at[3]).wait()

    def out_arrive(i):
        for kind in both:
            out_message(kind, i).wait_recv()
            if i % 2 == kind:
                out_message(2 + kind, i).start()
            out_sibling(-1 if kind == 0 else 1, i).start()

    for h in both:
        for stage, d in ((1, 0), (2, 0), (2, 1), (2, -1), (2, 2)):
            for kind in range(4):
                message(h, stage, d, kind).wait_send()
        for place in range(PLANE):
            to_sibling(h, place).wait_send()
    for number in range(6):
        cand_message(number).wait_send()
    cand_over.wait_send()
    cand_near.wait_send()
    for j in range(3):
        shift_message(j).wait_send()
        for place in range(PLANE):
            rows_message(place, j).wait_send()
    sent = PV.at[pl.ds(0, 2 * LATE - 1)]
    pltpu.make_async_copy(sent, sent, lse_sem.at[0]).wait()
    sent = LT.at[pl.ds(0, SRC - 1)]
    pltpu.make_async_copy(sent, sent, lse_sem.at[2]).wait()
    out_arrive(2)
    for i in both:
        reduce_message(0, 2 - i).wait_recv()
        reduce_message(1, 1 + i).wait_recv()
        c = z * QUARTER + i
        total = SF[2 + i] + RN[2 - i].astype(F32) + RP[1 + i].astype(F32)
        finish(i, total, MR[0, c] + MR[1, c] + MR[2, c] + MR[3, c], 0.0)

    out_arrive(3)
    for way in both:
        for number in range(3):
            reduce_message(way, number).wait_send()
    for j, device in enumerate((z_next, z_prev, z_far)):
        remote(MS, MR.at[z], mass_sem.at[j], mass_sem.at[3], device).wait_send()
    for i in both:
        out_arrive(i)
    for i in (2, 3):
        out_message(2 + i % 2, i).wait_recv()
        out_sibling(2, i).start()
    for i in range(QUARTER):
        out_message(0, i).wait_send()
        out_message(1, i).wait_send()
        for step in (0, -1, 1):
            out_sibling(step, i).wait_send()
            out_sibling(step, i).wait_recv()
    for i in both:
        out_message(2 + i % 2, i).wait_recv()
        out_sibling(2, i).start()
    for i in (2, 3, 0, 1):
        out_message(2 + i % 2, i).wait_send()
        out_sibling(2, i).wait_send()
        out_sibling(2, i).wait_recv()


def body(vectors, candidates, centroids):
    cells = centroids.shape[0] // CELL
    dma = pltpu.SemaphoreType.DMA
    any_space = pl.BlockSpec(memory_space=pl.ANY)
    refined = pl.pallas_call(
        kernel,
        out_shape=pltpu.VMEM((cells, CELL, D), BF16),
        in_specs=[any_space] * 3,
        out_specs=pl.BlockSpec(memory_space=pltpu.VMEM),
        scratch_shapes=[
            pltpu.VMEM((SRC, VEC, D), BF16),
            pltpu.VMEM((SRC, 8, VEC), jnp.int32),
            pltpu.VMEM((8, VEC), jnp.int32),
            pltpu.VMEM((MINE, CELL, D), BF16),
            pltpu.VMEM((MINE, D, CELL), BF16),
            pltpu.VMEM((MINE, ROWS, D), BF16),
            pltpu.VMEM((PLANE, 2, MINE, VEC), F32),
            pltpu.VMEM((PLANE * MINE, VEC), BF16),
            pltpu.VMEM((VEC, VEC), BF16),
            pltpu.VMEM((MINE, 8, CELL), F32),
            pltpu.VMEM((MINE, ROWS, CELL), F32),
            pltpu.VMEM((MINE, ROWS, CELL), F32),
            pltpu.VMEM((SRC + 1, 1, VEC), F32),
            pltpu.VMEM((2 * LATE, 1, VEC), F32),
            pltpu.VMEM((SRC, 1, VEC), F32),
            pltpu.VMEM((SRC, FRESH + 1, 1, VEC), F32),
            pltpu.VMEM((MINE, 1, CELL), F32),
            pltpu.VMEM((SIDE, MINE, 1, CELL), F32),
            pltpu.VMEM((2, 3, CELL, D), BF16),
            pltpu.VMEM((2 + QUARTER, CELL, D), F32),
            pltpu.VMEM((3, CELL, D), BF16),
            pltpu.VMEM((3, CELL, D), BF16),
            pltpu.VMEM((3, ROUTED, ROWS, D), BF16),
            pltpu.VMEM((3, ROUTED, 1, ROWS), F32),
            pltpu.VMEM((3, ROUTED, 1, ROWS), F32),
            pltpu.VMEM((ROUTED, CELL, CELL), F32),
            dma((3, 16)),
            dma((3, 16)),
            dma((3,)),
            dma((3,)),
            dma((3,)),
            dma((8,)),
            dma((8,)),
            dma((2, 20)),
            dma((2, 20)),
            dma((2, 16)),
            dma((2, 16)),
            dma((4,)),
            dma((2, 3)),
            dma((2, 3)),
            dma((4,)),
            dma((4, 4)),
            dma((4, 4)),
            dma((4, 4)),
            dma((4, 4)),
        ],
        compiler_params=pltpu.CompilerParams(
            collective_id=0, has_side_effects=True, vmem_limit_bytes=48 * 1024 * 1024
        ),
        name="refine",
    )(vectors, candidates.T, centroids.reshape(cells, CELL, D))
    return refined.reshape(cells * CELL, D)


def solution(mesh):
    placed = (P(("grp", "own"), None), P(("grp", "own"), None), P("own", None))
    return jax.shard_map(
        body, mesh=mesh, in_specs=placed, out_specs=P("own", None), check_vma=False
    )
```

```python
import functools

import jax
import jax.numpy as jnp
from jax import lax
from jax.experimental import pallas as pl
from jax.experimental.pallas import tpu as pltpu
from jax.sharding import PartitionSpec as P

MESH = pl.DeviceIdType.MESH
F32 = jnp.float32
BF16 = jnp.bfloat16

CELL = 128
SLOTS = 8
VEC = 256
D = 768
SIDE = 4
PLANE = SIDE * SIDE
SRC = 2 * PLANE
MINE = 16
QUARTER = MINE // SIDE
ROWS = SRC * SLOTS
ROUTED = 2
PRIOR_MASS = 1.0
LOW = -1e30
HIGH = 1e30

HALF = VEC // 2
FOURTH = VEC // 4


BUDGET = 1.6
SPOTS = (
    (0, 0), (1, 0), (-1, 0), (0, 1), (0, -1), (1, 1), (2, 0), (0, 2),
    (1, -1), (-1, 1), (-1, -1), (2, 1), (1, 2), (2, -1), (-1, 2), (2, 2),
)
GROUPS = ((0, 5), (5, 6), (11, 2), (13, 3))
LATE = 13
FRESH = 2 * (PLANE - LATE)


def mirrored(place):
    dx, dy = (0 if v == 0 else 2 if v == 2 else -v for v in SPOTS[place])
    return SPOTS.index((dx, dy))


def behind(place, late):
    dx, dy = ((a - b + 5) % 4 - 1 for a, b in zip(SPOTS[place], SPOTS[late]))
    return SPOTS.index((dx, dy))


def ring(i):
    return lax.rem(i + 2 * SIDE, SIDE)


def kernel(
    vec, cand, cents, out,
    X, CD, CE, C, CT, R, RK, H, U, SQ, L, LB, LVS, PV, LV2, LT, MS, MR, S, SF, RN, RP,
    R3, SHR, SHZ, SQC,
    rows_send, rows_recv, shift_send, shift_recv, load_sem, cand_send, cand_recv, ag_send, ag_recv, sib_send, sib_recv, lse_sem,
    rs_send, rs_recv, mass_sem, og_send, og_recv, os_send, os_recv,
):
    grp = lax.axis_index("grp")
    own = lax.axis_index("own")
    z, k = lax.div(grp, 2), lax.rem(grp, 2)
    y, x = lax.div(own, SIDE), lax.rem(own, SIDE)
    sibling = (z * 2 + 1 - k, own)
    z_next = (ring(z + 1) * 2 + k, own)
    z_prev = (ring(z - 1) * 2 + k, own)
    z_far = (ring(z + 2) * 2 + k, own)
    me = k * PLANE + own
    both = (0, 1)
    last = (((1,), (1,)), ((), ()))

    def at(dx, dy):
        return ring(y + dy) * SIDE + ring(x + dx)

    def remote(src, dst, send, recv, device):
        return pltpu.make_async_remote_copy(
            src_ref=src, dst_ref=dst, send_sem=send, recv_sem=recv,
            device_id=device, device_id_type=MESH,
        )

    loads = [
        pltpu.make_async_copy(vec, X.at[me], load_sem.at[0]),
        pltpu.make_async_copy(cand, CD.at[me], load_sem.at[1]),
        pltpu.make_async_copy(cents.at[pl.ds(k * MINE, MINE)], C, load_sem.at[2]),
    ]
    for load in loads:
        load.start()
    x_next, x_prev = (grp, at(1, 0)), (grp, at(-1, 0))
    y_next, y_prev = (grp, at(0, 1)), (grp, at(0, -1))
    x_far, y_far = (grp, at(2, 0)), (grp, at(0, 2))
    near = (x_next, x_prev, x_far, y_next, y_prev, y_far, sibling, z_next, z_prev, z_far)
    barrier = pltpu.get_barrier_semaphore()
    for device in near:
        pl.semaphore_signal(barrier, inc=1, device_id=device, device_id_type=MESH)
    pl.semaphore_wait(barrier, len(near))

    def block(h, first, second):
        return at(first, second) if h == 0 else at(second, first)

    def axis_peer(h, stage, step):
        along_x = (h == 0) == (stage == 1)
        return (grp, at(step, 0) if along_x else at(0, step))

    def rows_of(h, part):
        if part == 2:
            return pl.ds(h * HALF, HALF)
        return pl.ds(h * HALF + part * FOURTH, FOURTH)

    def message(h, stage, d, kind):
        place = 0 if stage == 1 else 1 + d % 4
        number = 4 * place + kind if kind < 4 else 16 + kind
        step = 1 if kind % 2 == 0 else -1
        back = -step if kind in (2, 3) else 0
        part = (2, 2, 0, 1)[kind] if d != 2 else (0, 1, 0, 1, 1, 0)[kind]
        blk = block(h, back, 0) if stage == 1 else block(h, d, back)
        ref = X.at[k * PLANE + blk, rows_of(h, part)]
        return remote(
            ref, ref, ag_send.at[h, number], ag_recv.at[h, number], axis_peer(h, stage, step)
        )

    def start(stage, d, kinds):
        for kind in kinds:
            for h in both:
                message(h, stage, d, kind).start()

    def to_sibling(h, place):
        ref = X.at[k * PLANE + at(*SPOTS[place]), rows_of(h, 2)]
        return remote(ref, ref, sib_send.at[h, place], sib_recv.at[h, place], sibling)

    def pass_on(h, first, second):
        to_sibling(h, SPOTS.index((first, second) if h == 0 else (second, first))).start()

    def arrive(stage, d, kinds, h):
        for kind in kinds:
            message(h, stage, d, kind).wait_recv()
            if kind < 2:
                side = -1 if kind == 0 else 1
                message(h, stage, d, 2 + kind).start()
                if stage == 1:
                    pass_on(h, side, 0)
                elif d != 2:
                    pass_on(h, d, side)
            elif kind > 3:
                pass_on(h, d, -1 if kind == 4 else 1)
        if kinds[-1] == 3:
            if stage == 1:
                pass_on(h, 2, 0)
            else:
                pass_on(h, d, 2)

    def take(places):
        for place in places:
            for h in both:
                to_sibling(h, place).wait_recv()

    def cand_message(number):
        if number < 3:
            ref = CD.at[pl.ds(k * PLANE + own, 1)]
            device = (x_next, x_prev, x_far)[number]
        else:
            ref = CD.at[pl.ds(k * PLANE + y * SIDE, SIDE)]
            device = (y_next, y_prev, y_far)[number - 3]
        return remote(ref, ref, cand_send.at[number], cand_recv.at[number], device)

    group_cand = CD.at[pl.ds(k * PLANE, PLANE)]
    cand_over = remote(group_cand, group_cand, cand_send.at[6], cand_recv.at[6], sibling)

    cand_near = remote(CD.at[me], CE, cand_send.at[7], cand_recv.at[7], sibling)

    def cand_start(numbers):
        for number in numbers:
            cand_message(number).start()

    def cand_arrive(numbers):
        for number in numbers:
            cand_message(number).wait_recv()

    column = (z_next, z_prev, z_far)
    column_step = (1, -1, 2)

    def rows_message(place, j):
        slots = pl.ds(place * 2 * SLOTS, 2 * SLOTS)
        cells = pl.ds(ring(z + column_step[j]) * QUARTER + (QUARTER - ROUTED), ROUTED)
        return remote(
            R.at[cells, slots], R3.at[j, :, slots], rows_send.at[j, place], rows_recv.at[j, place],
            column[j],
        )

    def shift_message(j):
        return remote(SHR.at[j], SHZ.at[j], shift_send.at[j], shift_recv.at[j], column[j])

    def turned(first, count):
        if not first:
            loads[2].wait()
        for c in range(first, first + count):
            block_t = C[c].T
            CT[c] = block_t
            value = block_t.astype(F32)
            SQ[c] = jnp.broadcast_to(jnp.sum(value * value, axis=0, keepdims=True), (8, CELL))

    def own_norms():
        for j in range(ROUTED):
            value = C[z * QUARTER + (QUARTER - ROUTED) + j].astype(F32)
            SQC[j] = jnp.broadcast_to(
                jnp.sum(value * value, axis=1, keepdims=True), (CELL, CELL)
            )

    def triangle():
        U[...] = jnp.where(
            lax.broadcasted_iota(jnp.int32, (VEC, VEC), 0)
            < lax.broadcasted_iota(jnp.int32, (VEC, VEC), 1),
            1.0,
            0.0,
        ).astype(BF16)

    def ranks(kk):
        labels = lax.broadcasted_iota(jnp.int32, (MINE, VEC), 0) + (own * 2 + k) * MINE
        for place, spot in enumerate(SPOTS):
            named = CD[kk * PLANE + at(*spot)]
            hit = named[0:1] == labels
            for i in range(1, 8):
                hit = hit | (named[i : i + 1] == labels)
            H[place * MINE : (place + 1) * MINE] = jnp.where(hit, 1.0, 0.0).astype(BF16)
        hits = H[...]
        rank = jnp.dot(hits, U[...], preferred_element_type=F32)
        slot = jnp.where(hits.astype(F32) > 0.5, rank, -1.0)
        RK[:, kk] = slot.reshape(PLANE, MINE, VEC)

    def own_ranks():
        labels = lax.broadcasted_iota(jnp.int32, (MINE, VEC), 0) + (own * 2 + k) * MINE
        for j, named in enumerate((CD[me], CE[...])):
            hit = named[0:1] == labels
            for i in range(1, 8):
                hit = hit | (named[i : i + 1] == labels)
            H[j * MINE : (j + 1) * MINE] = jnp.where(hit, 1.0, 0.0).astype(BF16)
        hits = H[0 : 2 * MINE]
        rank = jnp.dot(hits, U[...], preferred_element_type=F32)
        slot = jnp.where(hits.astype(F32) > 0.5, rank, -1.0)
        RK[0, k] = slot[0:MINE]
        RK[0, 1 - k] = slot[MINE:]

    def numbers(count):
        return lax.broadcasted_iota(jnp.int32, (count, SLOTS, VEC), 1).astype(F32)

    def slot_mask(place, kk):
        return RK[place, kk][:, None, :] == numbers(MINE)

    def place_rows(place):
        parts = []
        for kk in both:
            pick = jnp.where(slot_mask(place, kk), 1.0, 0.0).reshape(MINE * SLOTS, VEC)
            rows = jnp.dot(
                pick.astype(BF16), X[kk * PLANE + at(*SPOTS[place])], preferred_element_type=F32
            )
            parts.append(rows.reshape(MINE, SLOTS, D))
        base = place * 2 * SLOTS
        R[:, base : base + 2 * SLOTS, :] = jnp.concatenate(parts, axis=1).astype(BF16)
        for j in (2, 0, 1):
            rows_message(place, j).start()

    def logits(group, first_cell, cells):
        first, count = GROUPS[group]
        slots = slice(first * 2 * SLOTS, (first + count) * 2 * SLOTS)
        for c in range(first_cell, first_cell + cells):
            products = jnp.dot(R[c, slots], CT[c], preferred_element_type=F32)
            value = (2.0 * products - SQ[c][0:1]) * D**-0.5
            L[c, slots] = value
            top = jnp.max(value, axis=1, keepdims=True)
            total = jnp.sum(jnp.exp(value - top), axis=1, keepdims=True)
            LB[c, slots] = jnp.broadcast_to(top + jnp.log(total), (count * 2 * SLOTS, CELL))

    def partial(place):
        for kk in both:
            base = (place * 2 + kk) * SLOTS
            part = LB[:, base : base + SLOTS, :]
            wide = jnp.concatenate([part, part], axis=2)
            mask = slot_mask(place, kk)
            known = jnp.where(mask, wide, LOW)
            top = jnp.max(jnp.max(known, axis=0), axis=0, keepdims=True)
            terms = jnp.where(mask, jnp.exp(known - top[None]), 0.0)
            total = jnp.sum(jnp.sum(terms, axis=0), axis=0, keepdims=True)
            LVS[2 * place + kk] = top + jnp.log(jnp.maximum(total, 1e-30))
            if 0 < place < LATE:
                device = (z * 2 + kk, at(*SPOTS[place]))
                send_partial(2 * place + kk, 2 * place + k, device)
        if not place:
            PV[k] = LVS[k]
            send_partial(1 - k, k, sibling)

    def send_partial(number, there, device):
        remote(LVS.at[number], PV.at[there], lse_sem.at[0], lse_sem.at[1], device).start()

    def announce(src, dst, send, recv):
        for place in range(PLANE - 1, 0, -1):
            for kk in both:
                device = (z * 2 + kk, at(*SPOTS[place]))
                remote(src, dst.at[2 * mirrored(place) + k], send, recv, device).start()
        remote(src, dst.at[k], send, recv, sibling).start()

    loads[1].wait()
    cand_start((0, 1, 2))
    cand_near.start()
    loads[0].wait()
    start(1, 0, (0, 1))
    for h in both:
        pass_on(h, 0, 0)
    triangle()
    cand_arrive((0, 1, 2))
    cand_start((3, 4, 5))
    start(2, 0, (0, 1))
    cand_near.wait_recv()
    own_ranks()
    take((0,))
    place_rows(0)

    steps = []
    for h in both:
        steps.append(("", functools.partial(arrive, 1, 0, (0, 1), h)))
    steps.append(("", lambda: start(2, 1, (0, 1))))
    steps.append(("", lambda: cand_arrive((3, 4, 5))))
    steps.append(("cand", cand_over.start))
    steps.append(("over", None))
    for h in both:
        steps.append(("", functools.partial(arrive, 2, 0, (0, 1), h)))
    steps.append(("ring1", lambda: start(2, -1, (0, 1))))
    for h in both:
        steps.append(("", functools.partial(arrive, 1, 0, (2, 3), h)))
    steps.append(("", lambda: start(2, 2, (0, 1, 4, 5))))
    for h in both:
        for kinds in ((0,), (1,)):
            name = "ring2" if h and kinds[0] else ""
            steps.append((name, functools.partial(arrive, 2, 1, kinds, h)))
    for h in both:
        steps.append(("far1" if h else "", functools.partial(arrive, 2, 0, (2, 3), h)))
    for h in both:
        for kinds in ((0,), (1,)):
            name = "ring3" if h and kinds[0] else ""
            steps.append((name, functools.partial(arrive, 2, -1, kinds, h)))
    for h in both:
        for kinds in ((0,), (1,)):
            steps.append(("", functools.partial(arrive, 2, 2, kinds, h)))
    for h in both:
        steps.append(("", functools.partial(arrive, 2, 2, (4, 5), h)))
    for d in (1, -1):
        for h in both:
            name = "" if not h else "far2" if d > 0 else "far3"
            steps.append((name, functools.partial(arrive, 2, d, (2, 3), h)))
    for h in both:
        steps.append(("end" if h else "", functools.partial(arrive, 2, 2, (2, 3), h)))

    placing, scoring = [], []
    for c in range(0, MINE, 2):
        scoring.append(("ring1", functools.partial(turned, c, 2), 0.5))
    scoring.append(("ring1", own_norms, 0.3))

    def ranks_of_other():
        cand_over.wait_recv()
        ranks(1 - k)

    placing.append(("cand", lambda: ranks(k), 1.0))
    placing.append(("over", ranks_of_other, 1.0))

    def placed(places, ready):
        placing.append((ready, functools.partial(take, places), 0.0))
        for place in places:
            placing.append((ready, functools.partial(place_rows, place), 0.4))

    def scored(group, ready):
        for c in range(0, MINE, 4):
            scoring.append((ready, functools.partial(logits, group, c, 4), 0.3))
        first, count = GROUPS[group]
        for place in range(first, first + count):
            scoring.append((ready, functools.partial(partial, place), 0.2))

    done = {"", ("placed", 0)}
    placed((1, 2, 3, 4), "ring1")
    placed((5,), "ring2")
    placed((6, 7), "far1")
    placed((8, 9, 10), "ring3")
    placed((11, 12), "far2")
    placed((13, 14), "far3")
    placed((15,), "end")
    scored(0, ("placed", 4))
    scored(1, ("placed", 10))
    scored(2, ("placed", 12))


    def advance(works, spent):
        while works and works[0][0] in done and spent < BUDGET:
            _, work, cost = works.pop(0)
            work()
            spent += cost
            if work.__class__ is functools.partial and work.func is place_rows:
                done.add(("placed", work.args[0]))
        return spent

    for name, step in steps:
        if step is not None:
            step()
        done.add(name)
        advance(scoring, advance(placing, -1.0 if name == "ring1" else 0.0))
    for works in (placing, scoring):
        for _, work, _ in works:
            work()
    logits(len(GROUPS) - 1, 0, MINE)
    for place in range(LATE, PLANE):
        partial(place)

    others = PV.at[pl.ds(0, 2 * LATE - 1)]
    pltpu.make_async_copy(others, others, lse_sem.at[1]).wait()
    parts = PV[...]
    top = jnp.max(parts, axis=0, keepdims=True)
    LVS[SRC : SRC + 1] = top + jnp.log(jnp.sum(jnp.exp(parts - top), axis=0, keepdims=True))
    LT[k] = LVS[SRC - FRESH :]
    announce(LVS.at[pl.ds(SRC - FRESH, FRESH + 1)], LT, lse_sem.at[2], lse_sem.at[3])
    others = LT.at[pl.ds(0, SRC - 1)]
    pltpu.make_async_copy(others, others, lse_sem.at[3]).wait()
    for place in range(PLANE):
        for kk in both:
            terms = [LT[2 * place + kk, FRESH]]
            for late in range(LATE, PLANE):
                for core in both:
                    terms.append(LT[2 * behind(place, late) + core, 2 * (late - LATE) + kk])
            top = functools.reduce(jnp.maximum, terms)
            LV2[2 * place + kk] = top + jnp.log(sum(jnp.exp(v - top) for v in terms))

    def cell_shift(c):
        rank = RK[:, :, pl.ds(c, 1), :].reshape(SRC, 1, VEC)
        found = jnp.where(rank == numbers(SRC), LV2[...], HIGH)
        return jnp.min(found, axis=2, keepdims=True).reshape(ROWS, 1)

    def cell_sum(c):
        weights = jnp.exp(L[c] - cell_shift(c)).astype(BF16)
        MS[c] = jnp.sum(weights.astype(F32), axis=0, keepdims=True)
        return lax.dot_general(
            weights, R[c], (((0,), (0,)), ((), ())), preferred_element_type=F32
        )

    def cell_of(step, i):
        return ring(z + step) * QUARTER + i

    landing = (RN, RP)
    toward = (z_next, z_prev)

    def reduce_message(way, number):
        return remote(
            S.at[way, number], landing[way].at[number],
            rs_send.at[way, number], rs_recv.at[way, number], toward[way],
        )

    def out_cell(step, i):
        return out.at[k * MINE + cell_of(step, i)]

    def out_message(kind, i):
        ref = out_cell((0, 0, -1, 1)[kind], i)
        return remote(ref, ref, og_send.at[kind, i], og_recv.at[kind, i], toward[kind % 2])

    def out_sibling(step, i):
        ref = out_cell(step, i)
        return remote(ref, ref, os_send.at[step % 4, i], os_recv.at[step % 4, i], sibling)

    diagonal = lax.broadcasted_iota(jnp.int32, (CELL, CELL), 0) == lax.broadcasted_iota(
        jnp.int32, (CELL, CELL), 1
    )

    def finish(i, total, mass_row, mass):
        c = z * QUARTER + i
        mass = mass + jnp.sum(
            jnp.where(diagonal, jnp.broadcast_to(mass_row, (CELL, CELL)), 0.0),
            axis=1,
            keepdims=True,
        )
        out[k * MINE + c] = (
            (total + PRIOR_MASS * C[c].astype(F32)) / (mass + PRIOR_MASS)
        ).astype(BF16)
        out_message(0, i).start()
        out_message(1, i).start()
        out_sibling(0, i).start()

    eye = lax.broadcasted_iota(jnp.int32, (ROWS, ROWS), 0) == lax.broadcasted_iota(
        jnp.int32, (ROWS, ROWS), 1
    )
    for j in (2, 0, 1):
        for i in range(ROUTED):
            shift = cell_shift(cell_of(column_step[j], QUARTER - ROUTED + i))
            wide = jnp.where(eye, jnp.broadcast_to(shift, (ROWS, ROWS)), 0.0)
            SHR[j, i] = jnp.sum(wide, axis=0, keepdims=True)
        shift_message(j).start()

    for way in both:
        S[way, 0] = cell_sum(cell_of(2, way)).astype(BF16)
        reduce_message(way, 0).start()
    for way in both:
        S[way, 1] = cell_sum(cell_of(1 - 2 * way, 1 - way)).astype(BF16)
        reduce_message(way, 1).start()

    for way in both:
        SF[way] = cell_sum(cell_of(1 - 2 * way, way))

    def own_sum(i, carry):
        SF[2 + i] = cell_sum(z * QUARTER + i)
        return carry

    lax.fori_loop(0, QUARTER, own_sum, 0)
    MR[z] = MS[...]
    for j, device in enumerate((z_next, z_prev, z_far)):
        remote(MS, MR.at[z], mass_sem.at[j], mass_sem.at[3], device).start()
    for j in range(3):
        shift_message(j).wait_recv()
        for place in range(PLANE):
            rows_message(place, j).wait_recv()
    def finish_rows(i):
        c = z * QUARTER + (QUARTER - ROUTED) + i
        mass = 0.0
        total = SF[2 + QUARTER - ROUTED + i]
        for j in range(3):
            rows = R3[j, i]
            products = lax.dot_general(C[c], rows, last, preferred_element_type=F32)
            value = (2.0 * products - SQC[i][:, 0:1]) * D**-0.5
            weights = jnp.exp(value - SHZ[j, i]).astype(BF16)
            mass = mass + jnp.sum(weights.astype(F32), axis=1, keepdims=True)
            total = total + jnp.dot(weights, rows, preferred_element_type=F32)
        finish(QUARTER - ROUTED + i, total, MS[c], mass)

    finish_rows(0)
    for way in both:
        reduce_message(way, 0).wait_recv()
        S[way, 2] = (SF[way] + landing[way][0].astype(F32)).astype(BF16)
        reduce_message(way, 2).start()
    finish_rows(1)
    others = MR.at[pl.ds(0, SIDE - 1)]
    pltpu.make_async_copy(others, others, mass_sem.at[3]).wait()

    def out_arrive(i):
        for kind in both:
            out_message(kind, i).wait_recv()
            if i % 2 == kind:
                out_message(2 + kind, i).start()
            out_sibling(-1 if kind == 0 else 1, i).start()

    for h in both:
        for stage, d in ((1, 0), (2, 0), (2, 1), (2, -1), (2, 2)):
            for kind in range(6 if d == 2 else 4):
                message(h, stage, d, kind).wait_send()
        for place in range(PLANE):
            to_sibling(h, place).wait_send()
    for number in range(6):
        cand_message(number).wait_send()
    cand_over.wait_send()
    cand_near.wait_send()
    for j in range(3):
        shift_message(j).wait_send()
        for place in range(PLANE):
            rows_message(place, j).wait_send()
    sent = PV.at[pl.ds(0, 2 * LATE - 1)]
    pltpu.make_async_copy(sent, sent, lse_sem.at[0]).wait()
    sent = LT.at[pl.ds(0, SRC - 1)]
    pltpu.make_async_copy(sent, sent, lse_sem.at[2]).wait()
    out_arrive(2)
    for i in both:
        reduce_message(0, 2 - i).wait_recv()
        reduce_message(1, 1 + i).wait_recv()
        c = z * QUARTER + i
        total = SF[2 + i] + RN[2 - i].astype(F32) + RP[1 + i].astype(F32)
        finish(i, total, MR[0, c] + MR[1, c] + MR[2, c] + MR[3, c], 0.0)

    out_arrive(3)
    for way in both:
        for number in range(3):
            reduce_message(way, number).wait_send()
    for j, device in enumerate((z_next, z_prev, z_far)):
        remote(MS, MR.at[z], mass_sem.at[j], mass_sem.at[3], device).wait_send()
    for i in both:
        out_arrive(i)
    for i in (2, 3):
        out_message(2 + i % 2, i).wait_recv()
        out_sibling(2, i).start()
    for i in range(QUARTER):
        out_message(0, i).wait_send()
        out_message(1, i).wait_send()
        for step in (0, -1, 1):
            out_sibling(step, i).wait_send()
            out_sibling(step, i).wait_recv()
    for i in both:
        out_message(2 + i % 2, i).wait_recv()
        out_sibling(2, i).start()
    for i in (2, 3, 0, 1):
        out_message(2 + i % 2, i).wait_send()
        out_sibling(2, i).wait_send()
        out_sibling(2, i).wait_recv()


def body(vectors, candidates, centroids):
    cells = centroids.shape[0] // CELL
    dma = pltpu.SemaphoreType.DMA
    any_space = pl.BlockSpec(memory_space=pl.ANY)
    refined = pl.pallas_call(
        kernel,
        out_shape=pltpu.VMEM((cells, CELL, D), BF16),
        in_specs=[any_space] * 3,
        out_specs=pl.BlockSpec(memory_space=pltpu.VMEM),
        scratch_shapes=[
            pltpu.VMEM((SRC, VEC, D), BF16),
            pltpu.VMEM((SRC, 8, VEC), jnp.int32),
            pltpu.VMEM((8, VEC), jnp.int32),
            pltpu.VMEM((MINE, CELL, D), BF16),
            pltpu.VMEM((MINE, D, CELL), BF16),
            pltpu.VMEM((MINE, ROWS, D), BF16),
            pltpu.VMEM((PLANE, 2, MINE, VEC), F32),
            pltpu.VMEM((PLANE * MINE, VEC), BF16),
            pltpu.VMEM((VEC, VEC), BF16),
            pltpu.VMEM((MINE, 8, CELL), F32),
            pltpu.VMEM((MINE, ROWS, CELL), F32),
            pltpu.VMEM((MINE, ROWS, CELL), F32),
            pltpu.VMEM((SRC + 1, 1, VEC), F32),
            pltpu.VMEM((2 * LATE, 1, VEC), F32),
            pltpu.VMEM((SRC, 1, VEC), F32),
            pltpu.VMEM((SRC, FRESH + 1, 1, VEC), F32),
            pltpu.VMEM((MINE, 1, CELL), F32),
            pltpu.VMEM((SIDE, MINE, 1, CELL), F32),
            pltpu.VMEM((2, 3, CELL, D), BF16),
            pltpu.VMEM((2 + QUARTER, CELL, D), F32),
            pltpu.VMEM((3, CELL, D), BF16),
            pltpu.VMEM((3, CELL, D), BF16),
            pltpu.VMEM((3, ROUTED, ROWS, D), BF16),
            pltpu.VMEM((3, ROUTED, 1, ROWS), F32),
            pltpu.VMEM((3, ROUTED, 1, ROWS), F32),
            pltpu.VMEM((ROUTED, CELL, CELL), F32),
            dma((3, 16)),
            dma((3, 16)),
            dma((3,)),
            dma((3,)),
            dma((3,)),
            dma((8,)),
            dma((8,)),
            dma((2, 22)),
            dma((2, 22)),
            dma((2, 16)),
            dma((2, 16)),
            dma((4,)),
            dma((2, 3)),
            dma((2, 3)),
            dma((4,)),
            dma((4, 4)),
            dma((4, 4)),
            dma((4, 4)),
            dma((4, 4)),
        ],
        compiler_params=pltpu.CompilerParams(
            collective_id=0, has_side_effects=True, vmem_limit_bytes=48 * 1024 * 1024
        ),
        name="refine",
    )(vectors, candidates.T, centroids.reshape(cells, CELL, D))
    return refined.reshape(cells * CELL, D)


def solution(mesh):
    placed = (P(("grp", "own"), None), P(("grp", "own"), None), P("own", None))
    return jax.shard_map(
        body, mesh=mesh, in_specs=placed, out_specs=P("own", None), check_vma=False
    )
```

```python
import functools

import jax
import jax.numpy as jnp
from jax import lax
from jax.experimental import pallas as pl
from jax.experimental.pallas import tpu as pltpu
from jax.sharding import PartitionSpec as P

MESH = pl.DeviceIdType.MESH
F32 = jnp.float32
BF16 = jnp.bfloat16

CELL = 128
SLOTS = 8
VEC = 256
D = 768
SIDE = 4
PLANE = SIDE * SIDE
SRC = 2 * PLANE
MINE = 16
QUARTER = MINE // SIDE
ROWS = SRC * SLOTS
ROUTED = 2
PRIOR_MASS = 1.0
LOW = -1e30
HIGH = 1e30

HALF = VEC // 2
FOURTH = VEC // 4


BUDGET = 1.6
SPOTS = (
    (0, 0), (1, 0), (-1, 0), (0, 1), (0, -1), (1, 1), (2, 0), (0, 2),
    (1, -1), (-1, 1), (-1, -1), (2, 1), (1, 2), (2, -1), (-1, 2), (2, 2),
)
GROUPS = ((0, 5), (5, 6), (11, 2), (13, 3))
LATE = 13
FRESH = 2 * (PLANE - LATE)


def mirrored(place):
    dx, dy = (0 if v == 0 else 2 if v == 2 else -v for v in SPOTS[place])
    return SPOTS.index((dx, dy))


def behind(place, late):
    dx, dy = ((a - b + 5) % 4 - 1 for a, b in zip(SPOTS[place], SPOTS[late]))
    return SPOTS.index((dx, dy))


def ring(i):
    return lax.rem(i + 2 * SIDE, SIDE)


def kernel(
    vec, cand, cents, out,
    X, CD, CE, C, CT, R, RK, H, U, SQ, L, LB, LVS, PV, LV2, LT, MS, MR, S, SF, RN, RP,
    R3, SHR, SHZ, SQC,
    rows_send, rows_recv, shift_send, shift_recv, load_sem, cand_send, cand_recv, ag_send, ag_recv, sib_send, sib_recv, lse_sem,
    rs_send, rs_recv, mass_sem, og_send, og_recv, os_send, os_recv,
):
    grp = lax.axis_index("grp")
    own = lax.axis_index("own")
    z, k = lax.div(grp, 2), lax.rem(grp, 2)
    y, x = lax.div(own, SIDE), lax.rem(own, SIDE)
    sibling = (z * 2 + 1 - k, own)
    z_next = (ring(z + 1) * 2 + k, own)
    z_prev = (ring(z - 1) * 2 + k, own)
    z_far = (ring(z + 2) * 2 + k, own)
    me = k * PLANE + own
    both = (0, 1)
    last = (((1,), (1,)), ((), ()))

    def at(dx, dy):
        return ring(y + dy) * SIDE + ring(x + dx)

    def remote(src, dst, send, recv, device):
        return pltpu.make_async_remote_copy(
            src_ref=src, dst_ref=dst, send_sem=send, recv_sem=recv,
            device_id=device, device_id_type=MESH,
        )

    loads = [
        pltpu.make_async_copy(vec, X.at[me], load_sem.at[0]),
        pltpu.make_async_copy(cand, CD.at[me], load_sem.at[1]),
        pltpu.make_async_copy(cents.at[pl.ds(k * MINE, MINE)], C, load_sem.at[2]),
    ]
    for load in loads:
        load.start()
    x_next, x_prev = (grp, at(1, 0)), (grp, at(-1, 0))
    y_next, y_prev = (grp, at(0, 1)), (grp, at(0, -1))
    x_far, y_far = (grp, at(2, 0)), (grp, at(0, 2))
    near = (x_next, x_prev, x_far, y_next, y_prev, y_far, sibling, z_next, z_prev, z_far)
    barrier = pltpu.get_barrier_semaphore()
    for device in near:
        pl.semaphore_signal(barrier, inc=1, device_id=device, device_id_type=MESH)
    pl.semaphore_wait(barrier, len(near))

    def block(h, first, second):
        return at(first, second) if h == 0 else at(second, first)

    def axis_peer(h, stage, step):
        along_x = (h == 0) == (stage == 1)
        return (grp, at(step, 0) if along_x else at(0, step))

    def rows_of(h, part):
        if part == 2:
            return pl.ds(h * HALF, HALF)
        return pl.ds(h * HALF + part * FOURTH, FOURTH)

    def message(h, stage, d, kind):
        place = 0 if stage == 1 else 1 + d % 4
        number = 4 * place + kind if kind < 4 else 16 + kind
        step = 1 if kind % 2 == 0 else -1
        back = -step if kind in (2, 3) else 0
        part = (2, 2, 0, 1)[kind] if d != 2 else (0, 1, 0, 1, 1, 0)[kind]
        blk = block(h, back, 0) if stage == 1 else block(h, d, back)
        ref = X.at[k * PLANE + blk, rows_of(h, part)]
        return remote(
            ref, ref, ag_send.at[h, number], ag_recv.at[h, number], axis_peer(h, stage, step)
        )

    def start(stage, d, kinds):
        for kind in kinds:
            for h in both:
                message(h, stage, d, kind).start()

    def to_sibling(h, place):
        ref = X.at[k * PLANE + at(*SPOTS[place]), rows_of(h, 2)]
        return remote(ref, ref, sib_send.at[h, place], sib_recv.at[h, place], sibling)

    def pass_on(h, first, second):
        to_sibling(h, SPOTS.index((first, second) if h == 0 else (second, first))).start()

    def arrive(stage, d, kinds, h):
        for kind in kinds:
            message(h, stage, d, kind).wait_recv()
            if kind < 2:
                side = -1 if kind == 0 else 1
                message(h, stage, d, 2 + kind).start()
                if stage == 1:
                    pass_on(h, side, 0)
                elif d != 2:
                    pass_on(h, d, side)
            elif kind > 3:
                pass_on(h, d, -1 if kind == 4 else 1)
        if kinds[-1] == 3:
            if stage == 1:
                pass_on(h, 2, 0)
            else:
                pass_on(h, d, 2)

    def take(places):
        for place in places:
            for h in both:
                to_sibling(h, place).wait_recv()

    def cand_message(number):
        if number < 3:
            ref = CD.at[pl.ds(k * PLANE + own, 1)]
            device = (x_next, x_prev, x_far)[number]
        else:
            ref = CD.at[pl.ds(k * PLANE + y * SIDE, SIDE)]
            device = (y_next, y_prev, y_far)[number - 3]
        return remote(ref, ref, cand_send.at[number], cand_recv.at[number], device)

    group_cand = CD.at[pl.ds(k * PLANE, PLANE)]
    cand_over = remote(group_cand, group_cand, cand_send.at[6], cand_recv.at[6], sibling)

    cand_near = remote(CD.at[me], CE, cand_send.at[7], cand_recv.at[7], sibling)

    def cand_start(numbers):
        for number in numbers:
            cand_message(number).start()

    def cand_arrive(numbers):
        for number in numbers:
            cand_message(number).wait_recv()

    column = (z_next, z_prev, z_far)
    column_step = (1, -1, 2)

    def rows_message(place, j):
        slots = pl.ds(place * 2 * SLOTS, 2 * SLOTS)
        cells = pl.ds(ring(z + column_step[j]) * QUARTER + (QUARTER - ROUTED), ROUTED)
        return remote(
            R.at[cells, slots], R3.at[j, :, slots], rows_send.at[j, place], rows_recv.at[j, place],
            column[j],
        )

    def shift_message(j):
        return remote(SHR.at[j], SHZ.at[j], shift_send.at[j], shift_recv.at[j], column[j])

    def turned(first, count):
        if not first:
            loads[2].wait()
        for c in range(first, first + count):
            block_t = C[c].T
            CT[c] = block_t
            value = block_t.astype(F32)
            SQ[c] = jnp.broadcast_to(jnp.sum(value * value, axis=0, keepdims=True), (8, CELL))

    def own_norms():
        for j in range(ROUTED):
            value = C[z * QUARTER + (QUARTER - ROUTED) + j].astype(F32)
            SQC[j] = jnp.broadcast_to(
                jnp.sum(value * value, axis=1, keepdims=True), (CELL, CELL)
            )

    def triangle():
        U[...] = jnp.where(
            lax.broadcasted_iota(jnp.int32, (VEC, VEC), 0)
            < lax.broadcasted_iota(jnp.int32, (VEC, VEC), 1),
            1.0,
            0.0,
        ).astype(BF16)

    def ranks(kk):
        labels = lax.broadcasted_iota(jnp.int32, (MINE, VEC), 0) + (own * 2 + k) * MINE
        for place, spot in enumerate(SPOTS):
            named = CD[kk * PLANE + at(*spot)]
            hit = named[0:1] == labels
            for i in range(1, 8):
                hit = hit | (named[i : i + 1] == labels)
            H[place * MINE : (place + 1) * MINE] = jnp.where(hit, 1.0, 0.0).astype(BF16)
        hits = H[...]
        rank = jnp.dot(hits, U[...], preferred_element_type=F32)
        slot = jnp.where(hits.astype(F32) > 0.5, rank, -1.0)
        RK[:, kk] = slot.reshape(PLANE, MINE, VEC)

    def own_ranks():
        labels = lax.broadcasted_iota(jnp.int32, (MINE, VEC), 0) + (own * 2 + k) * MINE
        for j, named in enumerate((CD[me], CE[...])):
            hit = named[0:1] == labels
            for i in range(1, 8):
                hit = hit | (named[i : i + 1] == labels)
            H[j * MINE : (j + 1) * MINE] = jnp.where(hit, 1.0, 0.0).astype(BF16)
        hits = H[0 : 2 * MINE]
        rank = jnp.dot(hits, U[...], preferred_element_type=F32)
        slot = jnp.where(hits.astype(F32) > 0.5, rank, -1.0)
        RK[0, k] = slot[0:MINE]
        RK[0, 1 - k] = slot[MINE:]

    def numbers(count):
        return lax.broadcasted_iota(jnp.int32, (count, SLOTS, VEC), 1).astype(F32)

    def slot_mask(place, kk):
        return RK[place, kk][:, None, :] == numbers(MINE)

    def place_rows(place):
        parts = []
        for kk in both:
            pick = jnp.where(slot_mask(place, kk), 1.0, 0.0).reshape(MINE * SLOTS, VEC)
            rows = jnp.dot(
                pick.astype(BF16), X[kk * PLANE + at(*SPOTS[place])], preferred_element_type=F32
            )
            parts.append(rows.reshape(MINE, SLOTS, D))
        base = place * 2 * SLOTS
        R[:, base : base + 2 * SLOTS, :] = jnp.concatenate(parts, axis=1).astype(BF16)
        for j in (2, 0, 1):
            rows_message(place, j).start()

    def logits(group, first_cell, cells):
        first, count = GROUPS[group]
        slots = slice(first * 2 * SLOTS, (first + count) * 2 * SLOTS)
        for c in range(first_cell, first_cell + cells):
            products = jnp.dot(R[c, slots], CT[c], preferred_element_type=F32)
            value = (2.0 * products - SQ[c][0:1]) * D**-0.5
            L[c, slots] = value
            top = jnp.max(value, axis=1, keepdims=True)
            total = jnp.sum(jnp.exp(value - top), axis=1, keepdims=True)
            LB[c, slots] = jnp.broadcast_to(top + jnp.log(total), (count * 2 * SLOTS, CELL))

    def partial(place):
        for kk in both:
            base = (place * 2 + kk) * SLOTS
            part = LB[:, base : base + SLOTS, :]
            wide = jnp.concatenate([part, part], axis=2)
            mask = slot_mask(place, kk)
            known = jnp.where(mask, wide, LOW)
            top = jnp.max(jnp.max(known, axis=0), axis=0, keepdims=True)
            terms = jnp.where(mask, jnp.exp(known - top[None]), 0.0)
            total = jnp.sum(jnp.sum(terms, axis=0), axis=0, keepdims=True)
            LVS[2 * place + kk] = top + jnp.log(jnp.maximum(total, 1e-30))
            if 0 < place < LATE:
                device = (z * 2 + kk, at(*SPOTS[place]))
                send_partial(2 * place + kk, 2 * place + k, device)
        if not place:
            PV[k] = LVS[k]
            send_partial(1 - k, k, sibling)

    def send_partial(number, there, device):
        remote(LVS.at[number], PV.at[there], lse_sem.at[0], lse_sem.at[1], device).start()

    def announce(src, dst, send, recv):
        for place in range(PLANE - 1, 0, -1):
            for kk in both:
                device = (z * 2 + kk, at(*SPOTS[place]))
                remote(src, dst.at[2 * mirrored(place) + k], send, recv, device).start()
        remote(src, dst.at[k], send, recv, sibling).start()

    loads[1].wait()
    cand_start((0, 1, 2))
    cand_near.start()
    loads[0].wait()
    start(1, 0, (0, 1))
    for h in both:
        pass_on(h, 0, 0)
    triangle()
    cand_arrive((0, 1, 2))
    cand_start((3, 4, 5))
    start(2, 0, (0, 1))
    cand_near.wait_recv()
    own_ranks()
    take((0,))
    place_rows(0)

    steps = []
    for h in both:
        steps.append(("", functools.partial(arrive, 1, 0, (0, 1), h)))
    steps.append(("", lambda: start(2, 1, (0, 1))))
    steps.append(("", lambda: cand_arrive((3, 4, 5))))
    steps.append(("cand", cand_over.start))
    steps.append(("over", None))
    for h in both:
        steps.append(("", functools.partial(arrive, 2, 0, (0, 1), h)))
    steps.append(("ring1", lambda: start(2, -1, (0, 1))))
    for h in both:
        steps.append(("", functools.partial(arrive, 1, 0, (2, 3), h)))
    steps.append(("", lambda: start(2, 2, (0, 1, 4, 5))))
    for h in both:
        for kinds in ((0,), (1,)):
            name = "ring2" if h and kinds[0] else ""
            steps.append((name, functools.partial(arrive, 2, 1, kinds, h)))
    for h in both:
        steps.append(("far1" if h else "", functools.partial(arrive, 2, 0, (2, 3), h)))
    for h in both:
        for kinds in ((0,), (1,)):
            name = "ring3" if h and kinds[0] else ""
            steps.append((name, functools.partial(arrive, 2, -1, kinds, h)))
    for h in both:
        for kinds in ((0,), (1,)):
            steps.append(("", functools.partial(arrive, 2, 2, kinds, h)))
    for h in both:
        steps.append(("", functools.partial(arrive, 2, 2, (4, 5), h)))
    for d in (1, -1):
        for h in both:
            name = "" if not h else "far2" if d > 0 else "far3"
            steps.append((name, functools.partial(arrive, 2, d, (2, 3), h)))
    for h in both:
        steps.append(("end" if h else "", functools.partial(arrive, 2, 2, (2, 3), h)))

    placing, scoring = [], []
    for c in range(0, MINE, 2):
        scoring.append(("ring1", functools.partial(turned, c, 2), 0.5))
    scoring.append(("ring1", own_norms, 0.3))

    def ranks_of_other():
        cand_over.wait_recv()
        ranks(1 - k)

    placing.append(("cand", lambda: ranks(k), 1.0))
    placing.append(("over", ranks_of_other, 1.0))

    def placed(places, ready):
        placing.append((ready, functools.partial(take, places), 0.0))
        for place in places:
            placing.append((ready, functools.partial(place_rows, place), 0.4))

    def scored(group, ready):
        for c in range(0, MINE, 4):
            scoring.append((ready, functools.partial(logits, group, c, 4), 0.3))
        first, count = GROUPS[group]
        for place in range(first, first + count):
            scoring.append((ready, functools.partial(partial, place), 0.2))

    done = {"", ("placed", 0)}
    placed((1, 2, 3, 4), "ring1")
    placed((5,), "ring2")
    placed((6, 7), "far1")
    placed((8, 9, 10), "ring3")
    placed((11, 12), "far2")
    placed((13, 14), "far3")
    placed((15,), "end")
    scored(0, ("placed", 4))
    scored(1, ("placed", 10))
    scored(2, ("placed", 12))


    def advance(works, spent):
        while works and works[0][0] in done and spent < BUDGET:
            _, work, cost = works.pop(0)
            work()
            spent += cost
            if work.__class__ is functools.partial and work.func is place_rows:
                done.add(("placed", work.args[0]))
        return spent

    for name, step in steps:
        if step is not None:
            step()
        done.add(name)
        advance(scoring, advance(placing, -1.0 if name == "ring1" else 0.0))
    for works in (placing, scoring):
        for _, work, _ in works:
            work()
    logits(len(GROUPS) - 1, 0, MINE)
    for place in range(LATE, PLANE):
        partial(place)

    others = PV.at[pl.ds(0, 2 * LATE - 1)]
    pltpu.make_async_copy(others, others, lse_sem.at[1]).wait()
    parts = PV[...]
    top = jnp.max(parts, axis=0, keepdims=True)
    LVS[SRC : SRC + 1] = top + jnp.log(jnp.sum(jnp.exp(parts - top), axis=0, keepdims=True))
    LT[k] = LVS[SRC - FRESH :]
    announce(LVS.at[pl.ds(SRC - FRESH, FRESH + 1)], LT, lse_sem.at[2], lse_sem.at[3])
    others = LT.at[pl.ds(0, SRC - 1)]
    pltpu.make_async_copy(others, others, lse_sem.at[3]).wait()
    for place in range(PLANE):
        for kk in both:
            terms = [LT[2 * place + kk, FRESH]]
            for late in range(LATE, PLANE):
                for core in both:
                    terms.append(LT[2 * behind(place, late) + core, 2 * (late - LATE) + kk])
            top = functools.reduce(jnp.maximum, terms)
            LV2[2 * place + kk] = top + jnp.log(sum(jnp.exp(v - top) for v in terms))

    def cell_shift(c):
        rank = RK[:, :, pl.ds(c, 1), :].reshape(SRC, 1, VEC)
        found = jnp.where(rank == numbers(SRC), LV2[...], HIGH)
        return jnp.min(found, axis=2, keepdims=True).reshape(ROWS, 1)

    def cell_sum(c):
        weights = jnp.exp(L[c] - cell_shift(c)).astype(BF16)
        MS[c] = jnp.sum(weights.astype(F32), axis=0, keepdims=True)
        return lax.dot_general(
            weights, R[c], (((0,), (0,)), ((), ())), preferred_element_type=F32
        )

    def cell_of(step, i):
        return ring(z + step) * QUARTER + i

    landing = (RN, RP)
    toward = (z_next, z_prev)

    def reduce_message(way, number):
        return remote(
            S.at[way, number], landing[way].at[number],
            rs_send.at[way, number], rs_recv.at[way, number], toward[way],
        )

    def out_cell(step, i):
        return out.at[k * MINE + cell_of(step, i)]

    def out_message(kind, i):
        ref = out_cell((0, 0, -1, 1)[kind], i)
        return remote(ref, ref, og_send.at[kind, i], og_recv.at[kind, i], toward[kind % 2])

    def out_sibling(step, i):
        ref = out_cell(step, i)
        return remote(ref, ref, os_send.at[step % 4, i], os_recv.at[step % 4, i], sibling)

    diagonal = lax.broadcasted_iota(jnp.int32, (CELL, CELL), 0) == lax.broadcasted_iota(
        jnp.int32, (CELL, CELL), 1
    )

    def finish(i, total, mass_row, mass):
        c = z * QUARTER + i
        mass = mass + jnp.sum(
            jnp.where(diagonal, jnp.broadcast_to(mass_row, (CELL, CELL)), 0.0),
            axis=1,
            keepdims=True,
        )
        out[k * MINE + c] = (
            (total + PRIOR_MASS * C[c].astype(F32)) / (mass + PRIOR_MASS)
        ).astype(BF16)
        out_message(0, i).start()
        out_message(1, i).start()
        out_sibling(0, i).start()

    eye = lax.broadcasted_iota(jnp.int32, (ROWS, ROWS), 0) == lax.broadcasted_iota(
        jnp.int32, (ROWS, ROWS), 1
    )
    for j in (2, 0, 1):
        for i in range(ROUTED):
            shift = cell_shift(cell_of(column_step[j], QUARTER - ROUTED + i))
            wide = jnp.where(eye, jnp.broadcast_to(shift, (ROWS, ROWS)), 0.0)
            SHR[j, i] = jnp.sum(wide, axis=0, keepdims=True)
        shift_message(j).start()

    for way in both:
        S[way, 0] = cell_sum(cell_of(2, way)).astype(BF16)
        reduce_message(way, 0).start()
    for way in both:
        S[way, 1] = cell_sum(cell_of(1 - 2 * way, 1 - way)).astype(BF16)
        reduce_message(way, 1).start()

    for way in both:
        SF[way] = cell_sum(cell_of(1 - 2 * way, way))

    def own_sum(i, carry):
        SF[2 + i] = cell_sum(z * QUARTER + i)
        return carry

    lax.fori_loop(0, QUARTER, own_sum, 0)
    MR[z] = MS[...]
    for j, device in enumerate((z_next, z_prev, z_far)):
        remote(MS, MR.at[z], mass_sem.at[j], mass_sem.at[3], device).start()
    for j in range(3):
        shift_message(j).wait_recv()
        for place in range(PLANE):
            rows_message(place, j).wait_recv()
    def finish_rows(i):
        c = z * QUARTER + (QUARTER - ROUTED) + i
        mass = 0.0
        total = SF[2 + QUARTER - ROUTED + i]
        for j in range(3):
            rows = R3[j, i]
            products = lax.dot_general(C[c], rows, last, preferred_element_type=F32)
            value = (2.0 * products - SQC[i][:, 0:1]) * D**-0.5
            weights = jnp.exp(value - SHZ[j, i]).astype(BF16)
            mass = mass + jnp.sum(weights.astype(F32), axis=1, keepdims=True)
            total = total + jnp.dot(weights, rows, preferred_element_type=F32)
        finish(QUARTER - ROUTED + i, total, MS[c], mass)

    for way in both:
        reduce_message(way, 0).wait_recv()
        S[way, 2] = (SF[way] + landing[way][0].astype(F32)).astype(BF16)
        reduce_message(way, 2).start()
    finish_rows(0)
    finish_rows(1)
    others = MR.at[pl.ds(0, SIDE - 1)]
    pltpu.make_async_copy(others, others, mass_sem.at[3]).wait()

    def out_arrive(i):
        for kind in both:
            out_message(kind, i).wait_recv()
            if i % 2 == kind:
                out_message(2 + kind, i).start()
            out_sibling(-1 if kind == 0 else 1, i).start()

    for h in both:
        for stage, d in ((1, 0), (2, 0), (2, 1), (2, -1), (2, 2)):
            for kind in range(6 if d == 2 else 4):
                message(h, stage, d, kind).wait_send()
        for place in range(PLANE):
            to_sibling(h, place).wait_send()
    for number in range(6):
        cand_message(number).wait_send()
    cand_over.wait_send()
    cand_near.wait_send()
    for j in range(3):
        shift_message(j).wait_send()
        for place in range(PLANE):
            rows_message(place, j).wait_send()
    sent = PV.at[pl.ds(0, 2 * LATE - 1)]
    pltpu.make_async_copy(sent, sent, lse_sem.at[0]).wait()
    sent = LT.at[pl.ds(0, SRC - 1)]
    pltpu.make_async_copy(sent, sent, lse_sem.at[2]).wait()
    out_arrive(2)
    for i in both:
        reduce_message(0, 2 - i).wait_recv()
        reduce_message(1, 1 + i).wait_recv()
        c = z * QUARTER + i
        total = SF[2 + i] + RN[2 - i].astype(F32) + RP[1 + i].astype(F32)
        finish(i, total, MR[0, c] + MR[1, c] + MR[2, c] + MR[3, c], 0.0)

    out_arrive(3)
    for way in both:
        for number in range(3):
            reduce_message(way, number).wait_send()
    for j, device in enumerate((z_next, z_prev, z_far)):
        remote(MS, MR.at[z], mass_sem.at[j], mass_sem.at[3], device).wait_send()
    for i in both:
        out_arrive(i)
    for i in (2, 3):
        out_message(2 + i % 2, i).wait_recv()
        out_sibling(2, i).start()
    for i in range(QUARTER):
        out_message(0, i).wait_send()
        out_message(1, i).wait_send()
        for step in (0, -1, 1):
            out_sibling(step, i).wait_send()
            out_sibling(step, i).wait_recv()
    for i in both:
        out_message(2 + i % 2, i).wait_recv()
        out_sibling(2, i).start()
    for i in (2, 3, 0, 1):
        out_message(2 + i % 2, i).wait_send()
        out_sibling(2, i).wait_send()
        out_sibling(2, i).wait_recv()


def body(vectors, candidates, centroids):
    cells = centroids.shape[0] // CELL
    dma = pltpu.SemaphoreType.DMA
    any_space = pl.BlockSpec(memory_space=pl.ANY)
    refined = pl.pallas_call(
        kernel,
        out_shape=pltpu.VMEM((cells, CELL, D), BF16),
        in_specs=[any_space] * 3,
        out_specs=pl.BlockSpec(memory_space=pltpu.VMEM),
        scratch_shapes=[
            pltpu.VMEM((SRC, VEC, D), BF16),
            pltpu.VMEM((SRC, 8, VEC), jnp.int32),
            pltpu.VMEM((8, VEC), jnp.int32),
            pltpu.VMEM((MINE, CELL, D), BF16),
            pltpu.VMEM((MINE, D, CELL), BF16),
            pltpu.VMEM((MINE, ROWS, D), BF16),
            pltpu.VMEM((PLANE, 2, MINE, VEC), F32),
            pltpu.VMEM((PLANE * MINE, VEC), BF16),
            pltpu.VMEM((VEC, VEC), BF16),
            pltpu.VMEM((MINE, 8, CELL), F32),
            pltpu.VMEM((MINE, ROWS, CELL), F32),
            pltpu.VMEM((MINE, ROWS, CELL), F32),
            pltpu.VMEM((SRC + 1, 1, VEC), F32),
            pltpu.VMEM((2 * LATE, 1, VEC), F32),
            pltpu.VMEM((SRC, 1, VEC), F32),
            pltpu.VMEM((SRC, FRESH + 1, 1, VEC), F32),
            pltpu.VMEM((MINE, 1, CELL), F32),
            pltpu.VMEM((SIDE, MINE, 1, CELL), F32),
            pltpu.VMEM((2, 3, CELL, D), BF16),
            pltpu.VMEM((2 + QUARTER, CELL, D), F32),
            pltpu.VMEM((3, CELL, D), BF16),
            pltpu.VMEM((3, CELL, D), BF16),
            pltpu.VMEM((3, ROUTED, ROWS, D), BF16),
            pltpu.VMEM((3, ROUTED, 1, ROWS), F32),
            pltpu.VMEM((3, ROUTED, 1, ROWS), F32),
            pltpu.VMEM((ROUTED, CELL, CELL), F32),
            dma((3, 16)),
            dma((3, 16)),
            dma((3,)),
            dma((3,)),
            dma((3,)),
            dma((8,)),
            dma((8,)),
            dma((2, 22)),
            dma((2, 22)),
            dma((2, 16)),
            dma((2, 16)),
            dma((4,)),
            dma((2, 3)),
            dma((2, 3)),
            dma((4,)),
            dma((4, 4)),
            dma((4, 4)),
            dma((4, 4)),
            dma((4, 4)),
        ],
        compiler_params=pltpu.CompilerParams(
            collective_id=0, has_side_effects=True, vmem_limit_bytes=48 * 1024 * 1024
        ),
        name="refine",
    )(vectors, candidates.T, centroids.reshape(cells, CELL, D))
    return refined.reshape(cells * CELL, D)


def solution(mesh):
    placed = (P(("grp", "own"), None), P(("grp", "own"), None), P("own", None))
    return jax.shard_map(
        body, mesh=mesh, in_specs=placed, out_specs=P("own", None), check_vma=False
    )
```

```python
import functools

import jax
import jax.numpy as jnp
from jax import lax
from jax.experimental import pallas as pl
from jax.experimental.pallas import tpu as pltpu
from jax.sharding import PartitionSpec as P

MESH = pl.DeviceIdType.MESH
F32 = jnp.float32
BF16 = jnp.bfloat16

CELL = 128
SLOTS = 8
VEC = 256
D = 768
SIDE = 4
PLANE = SIDE * SIDE
SRC = 2 * PLANE
MINE = 16
QUARTER = MINE // SIDE
ROWS = SRC * SLOTS
ROUTED = 2
PRIOR_MASS = 1.0
LOW = -1e30
HIGH = 1e30

HALF = VEC // 2
FOURTH = VEC // 4


BUDGET = 1.6
SPOTS = (
    (0, 0), (1, 0), (-1, 0), (0, 1), (0, -1), (1, 1), (2, 0), (0, 2),
    (1, -1), (-1, 1), (-1, -1), (2, 1), (1, 2), (2, -1), (-1, 2), (2, 2),
)
GROUPS = ((0, 5), (5, 6), (11, 2), (13, 3))
LATE = 13
FRESH = 2 * (PLANE - LATE)


def mirrored(place):
    dx, dy = (0 if v == 0 else 2 if v == 2 else -v for v in SPOTS[place])
    return SPOTS.index((dx, dy))


def behind(place, late):
    dx, dy = ((a - b + 5) % 4 - 1 for a, b in zip(SPOTS[place], SPOTS[late]))
    return SPOTS.index((dx, dy))


def ring(i):
    return lax.rem(i + 2 * SIDE, SIDE)


def kernel(
    vec, cand, cents, out,
    X, CD, CE, C, CT, R, RK, H, U, SQ, L, LB, LVS, PV, LV2, LT, MS, MR, S, SF, RN, RP,
    R3, SHR, SHZ, SQC,
    rows_send, rows_recv, shift_send, shift_recv, load_sem, cand_send, cand_recv, ag_send, ag_recv, sib_send, sib_recv, lse_sem,
    rs_send, rs_recv, mass_sem, og_send, og_recv, os_send, os_recv,
):
    grp = lax.axis_index("grp")
    own = lax.axis_index("own")
    z, k = lax.div(grp, 2), lax.rem(grp, 2)
    y, x = lax.div(own, SIDE), lax.rem(own, SIDE)
    sibling = (z * 2 + 1 - k, own)
    z_next = (ring(z + 1) * 2 + k, own)
    z_prev = (ring(z - 1) * 2 + k, own)
    z_far = (ring(z + 2) * 2 + k, own)
    me = k * PLANE + own
    both = (0, 1)
    last = (((1,), (1,)), ((), ()))

    def at(dx, dy):
        return ring(y + dy) * SIDE + ring(x + dx)

    def remote(src, dst, send, recv, device):
        return pltpu.make_async_remote_copy(
            src_ref=src, dst_ref=dst, send_sem=send, recv_sem=recv,
            device_id=device, device_id_type=MESH,
        )

    loads = [
        pltpu.make_async_copy(vec, X.at[me], load_sem.at[0]),
        pltpu.make_async_copy(cand, CD.at[me], load_sem.at[1]),
        pltpu.make_async_copy(cents.at[pl.ds(k * MINE, MINE)], C, load_sem.at[2]),
    ]
    for load in loads:
        load.start()
    x_next, x_prev = (grp, at(1, 0)), (grp, at(-1, 0))
    y_next, y_prev = (grp, at(0, 1)), (grp, at(0, -1))
    x_far, y_far = (grp, at(2, 0)), (grp, at(0, 2))
    near = (x_next, x_prev, x_far, y_next, y_prev, y_far, sibling, z_next, z_prev, z_far)
    barrier = pltpu.get_barrier_semaphore()
    for device in near:
        pl.semaphore_signal(barrier, inc=1, device_id=device, device_id_type=MESH)
    pl.semaphore_wait(barrier, len(near))

    def block(h, first, second):
        return at(first, second) if h == 0 else at(second, first)

    def axis_peer(h, stage, step):
        along_x = (h == 0) == (stage == 1)
        return (grp, at(step, 0) if along_x else at(0, step))

    def rows_of(h, part):
        if part == 2:
            return pl.ds(h * HALF, HALF)
        return pl.ds(h * HALF + part * FOURTH, FOURTH)

    def message(h, stage, d, kind):
        place = 0 if stage == 1 else 1 + d % 4
        number = 4 * place + kind if kind < 4 else 16 + kind
        step = 1 if kind % 2 == 0 else -1
        back = -step if kind in (2, 3) else 0
        part = (2, 2, 0, 1)[kind] if d != 2 else (0, 1, 0, 1, 1, 0)[kind]
        blk = block(h, back, 0) if stage == 1 else block(h, d, back)
        ref = X.at[k * PLANE + blk, rows_of(h, part)]
        return remote(
            ref, ref, ag_send.at[h, number], ag_recv.at[h, number], axis_peer(h, stage, step)
        )

    def start(stage, d, kinds):
        for kind in kinds:
            for h in both:
                message(h, stage, d, kind).start()

    def to_sibling(h, place):
        ref = X.at[k * PLANE + at(*SPOTS[place]), rows_of(h, 2)]
        return remote(ref, ref, sib_send.at[h, place], sib_recv.at[h, place], sibling)

    def pass_on(h, first, second):
        to_sibling(h, SPOTS.index((first, second) if h == 0 else (second, first))).start()

    def arrive(stage, d, kinds, h):
        for kind in kinds:
            message(h, stage, d, kind).wait_recv()
            if kind < 2:
                side = -1 if kind == 0 else 1
                message(h, stage, d, 2 + kind).start()
                if stage == 1:
                    pass_on(h, side, 0)
                elif d != 2:
                    pass_on(h, d, side)
            elif kind > 3:
                pass_on(h, d, -1 if kind == 4 else 1)
        if kinds[-1] == 3:
            if stage == 1:
                pass_on(h, 2, 0)
            else:
                pass_on(h, d, 2)

    def take(places):
        for place in places:
            for h in both:
                to_sibling(h, place).wait_recv()

    def cand_message(number):
        if number < 3:
            ref = CD.at[pl.ds(k * PLANE + own, 1)]
            device = (x_next, x_prev, x_far)[number]
        else:
            ref = CD.at[pl.ds(k * PLANE + y * SIDE, SIDE)]
            device = (y_next, y_prev, y_far)[number - 3]
        return remote(ref, ref, cand_send.at[number], cand_recv.at[number], device)

    group_cand = CD.at[pl.ds(k * PLANE, PLANE)]
    cand_over = remote(group_cand, group_cand, cand_send.at[6], cand_recv.at[6], sibling)

    cand_near = remote(CD.at[me], CE, cand_send.at[7], cand_recv.at[7], sibling)

    def cand_start(numbers):
        for number in numbers:
            cand_message(number).start()

    def cand_arrive(numbers):
        for number in numbers:
            cand_message(number).wait_recv()

    column = (z_next, z_prev, z_far)
    column_step = (1, -1, 2)

    def rows_message(place, j):
        slots = pl.ds(place * 2 * SLOTS, 2 * SLOTS)
        cells = pl.ds(ring(z + column_step[j]) * QUARTER + (QUARTER - ROUTED), ROUTED)
        return remote(
            R.at[cells, slots], R3.at[j, :, slots], rows_send.at[j, place], rows_recv.at[j, place],
            column[j],
        )

    def shift_message(j):
        return remote(SHR.at[j], SHZ.at[j], shift_send.at[j], shift_recv.at[j], column[j])

    def turned(first, count):
        if not first:
            loads[2].wait()
        for c in range(first, first + count):
            block_t = C[c].T
            CT[c] = block_t
            value = block_t.astype(F32)
            SQ[c] = jnp.broadcast_to(jnp.sum(value * value, axis=0, keepdims=True), (8, CELL))

    def own_norms():
        for j in range(ROUTED):
            value = C[z * QUARTER + (QUARTER - ROUTED) + j].astype(F32)
            SQC[j] = jnp.broadcast_to(
                jnp.sum(value * value, axis=1, keepdims=True), (CELL, CELL)
            )

    def triangle():
        U[...] = jnp.where(
            lax.broadcasted_iota(jnp.int32, (VEC, VEC), 0)
            < lax.broadcasted_iota(jnp.int32, (VEC, VEC), 1),
            1.0,
            0.0,
        ).astype(BF16)

    def ranks(kk):
        labels = lax.broadcasted_iota(jnp.int32, (MINE, VEC), 0) + (own * 2 + k) * MINE
        for place, spot in enumerate(SPOTS):
            named = CD[kk * PLANE + at(*spot)]
            hit = named[0:1] == labels
            for i in range(1, 8):
                hit = hit | (named[i : i + 1] == labels)
            H[place * MINE : (place + 1) * MINE] = jnp.where(hit, 1.0, 0.0).astype(BF16)
        hits = H[...]
        rank = jnp.dot(hits, U[...], preferred_element_type=F32)
        slot = jnp.where(hits.astype(F32) > 0.5, rank, -1.0)
        RK[:, kk] = slot.reshape(PLANE, MINE, VEC)

    def own_ranks():
        labels = lax.broadcasted_iota(jnp.int32, (MINE, VEC), 0) + (own * 2 + k) * MINE
        for j, named in enumerate((CD[me], CE[...])):
            hit = named[0:1] == labels
            for i in range(1, 8):
                hit = hit | (named[i : i + 1] == labels)
            H[j * MINE : (j + 1) * MINE] = jnp.where(hit, 1.0, 0.0).astype(BF16)
        hits = H[0 : 2 * MINE]
        rank = jnp.dot(hits, U[...], preferred_element_type=F32)
        slot = jnp.where(hits.astype(F32) > 0.5, rank, -1.0)
        RK[0, k] = slot[0:MINE]
        RK[0, 1 - k] = slot[MINE:]

    def numbers(count):
        return lax.broadcasted_iota(jnp.int32, (count, SLOTS, VEC), 1).astype(F32)

    def slot_mask(place, kk):
        return RK[place, kk][:, None, :] == numbers(MINE)

    def place_rows(place):
        parts = []
        for kk in both:
            pick = jnp.where(slot_mask(place, kk), 1.0, 0.0).reshape(MINE * SLOTS, VEC)
            rows = jnp.dot(
                pick.astype(BF16), X[kk * PLANE + at(*SPOTS[place])], preferred_element_type=F32
            )
            parts.append(rows.reshape(MINE, SLOTS, D))
        base = place * 2 * SLOTS
        R[:, base : base + 2 * SLOTS, :] = jnp.concatenate(parts, axis=1).astype(BF16)
        for j in (2, 0, 1):
            rows_message(place, j).start()

    def logits(group, first_cell, cells):
        first, count = GROUPS[group]
        slots = slice(first * 2 * SLOTS, (first + count) * 2 * SLOTS)
        for c in range(first_cell, first_cell + cells):
            products = jnp.dot(R[c, slots], CT[c], preferred_element_type=F32)
            value = (2.0 * products - SQ[c][0:1]) * D**-0.5
            L[c, slots] = value
            top = jnp.max(value, axis=1, keepdims=True)
            total = jnp.sum(jnp.exp(value - top), axis=1, keepdims=True)
            LB[c, slots] = jnp.broadcast_to(top + jnp.log(total), (count * 2 * SLOTS, CELL))

    def partial(place):
        for kk in both:
            base = (place * 2 + kk) * SLOTS
            part = LB[:, base : base + SLOTS, :]
            wide = jnp.concatenate([part, part], axis=2)
            mask = slot_mask(place, kk)
            known = jnp.where(mask, wide, LOW)
            top = jnp.max(jnp.max(known, axis=0), axis=0, keepdims=True)
            terms = jnp.where(mask, jnp.exp(known - top[None]), 0.0)
            total = jnp.sum(jnp.sum(terms, axis=0), axis=0, keepdims=True)
            LVS[2 * place + kk] = top + jnp.log(jnp.maximum(total, 1e-30))
            if 0 < place < LATE:
                device = (z * 2 + kk, at(*SPOTS[place]))
                send_partial(2 * place + kk, 2 * place + k, device)
        if not place:
            PV[k] = LVS[k]
            send_partial(1 - k, k, sibling)

    def send_partial(number, there, device):
        remote(LVS.at[number], PV.at[there], lse_sem.at[0], lse_sem.at[1], device).start()

    def announce(src, dst, send, recv):
        for place in range(PLANE - 1, 0, -1):
            for kk in both:
                device = (z * 2 + kk, at(*SPOTS[place]))
                remote(src, dst.at[2 * mirrored(place) + k], send, recv, device).start()
        remote(src, dst.at[k], send, recv, sibling).start()

    loads[1].wait()
    cand_start((0, 1, 2))
    cand_near.start()
    loads[0].wait()
    start(1, 0, (0, 1))
    for h in both:
        pass_on(h, 0, 0)
    triangle()
    cand_arrive((0, 1, 2))
    cand_start((3, 4, 5))
    start(2, 0, (0, 1))
    cand_near.wait_recv()
    own_ranks()
    take((0,))
    place_rows(0)

    steps = []
    for h in both:
        steps.append(("", functools.partial(arrive, 1, 0, (0, 1), h)))
    steps.append(("", lambda: start(2, 1, (0, 1))))
    steps.append(("", lambda: cand_arrive((3, 4, 5))))
    steps.append(("cand", cand_over.start))
    steps.append(("over", None))
    for h in both:
        steps.append(("", functools.partial(arrive, 2, 0, (0, 1), h)))
    steps.append(("ring1", lambda: start(2, -1, (0, 1))))
    for h in both:
        steps.append(("", functools.partial(arrive, 1, 0, (2, 3), h)))
    steps.append(("", lambda: start(2, 2, (0, 1, 4, 5))))
    for h in both:
        for kinds in ((0,), (1,)):
            name = "ring2" if h and kinds[0] else ""
            steps.append((name, functools.partial(arrive, 2, 1, kinds, h)))
    for h in both:
        steps.append(("far1" if h else "", functools.partial(arrive, 2, 0, (2, 3), h)))
    for h in both:
        for kinds in ((0,), (1,)):
            name = "ring3" if h and kinds[0] else ""
            steps.append((name, functools.partial(arrive, 2, -1, kinds, h)))
    for h in both:
        for kinds in ((0,), (1,)):
            steps.append(("", functools.partial(arrive, 2, 2, kinds, h)))
    for h in both:
        steps.append(("", functools.partial(arrive, 2, 2, (4, 5), h)))
    for d in (1, -1):
        for h in both:
            name = "" if not h else "far2" if d > 0 else "far3"
            steps.append((name, functools.partial(arrive, 2, d, (2, 3), h)))
    for h in both:
        steps.append(("end" if h else "", functools.partial(arrive, 2, 2, (2, 3), h)))

    placing, scoring = [], []
    for c in range(0, MINE, 2):
        scoring.append(("ring1", functools.partial(turned, c, 2), 0.5))
    scoring.append(("ring1", own_norms, 0.3))

    def ranks_of_other():
        cand_over.wait_recv()
        ranks(1 - k)

    placing.append(("cand", lambda: ranks(k), 1.0))
    placing.append(("over", ranks_of_other, 1.0))

    def placed(places, ready):
        placing.append((ready, functools.partial(take, places), 0.0))
        for place in places:
            placing.append((ready, functools.partial(place_rows, place), 0.4))

    def scored(group, ready):
        for c in range(0, MINE, 4):
            scoring.append((ready, functools.partial(logits, group, c, 4), 0.3))
        first, count = GROUPS[group]
        for place in range(first, first + count):
            scoring.append((ready, functools.partial(partial, place), 0.2))

    done = {"", ("placed", 0)}
    placed((1, 2, 3, 4), "ring1")
    placed((5,), "ring2")
    placed((6, 7), "far1")
    placed((8, 9, 10), "ring3")
    placed((11, 12), "far2")
    placed((13, 14), "far3")
    placed((15,), "end")
    scored(0, ("placed", 4))
    scored(1, ("placed", 10))
    scored(2, ("placed", 12))


    def advance(works, spent):
        while works and works[0][0] in done and spent < BUDGET:
            _, work, cost = works.pop(0)
            work()
            spent += cost
            if work.__class__ is functools.partial and work.func is place_rows:
                done.add(("placed", work.args[0]))
        return spent

    for name, step in steps:
        if step is not None:
            step()
        done.add(name)
        advance(scoring, advance(placing, -1.0 if name == "ring1" else 0.0))
    for works in (placing, scoring):
        for _, work, _ in works:
            work()
    logits(len(GROUPS) - 1, 0, MINE)
    for place in range(LATE, PLANE):
        partial(place)

    others = PV.at[pl.ds(0, 2 * LATE - 1)]
    pltpu.make_async_copy(others, others, lse_sem.at[1]).wait()
    parts = PV[...]
    top = jnp.max(parts, axis=0, keepdims=True)
    LVS[SRC : SRC + 1] = top + jnp.log(jnp.sum(jnp.exp(parts - top), axis=0, keepdims=True))
    LT[k] = LVS[SRC - FRESH :]
    announce(LVS.at[pl.ds(SRC - FRESH, FRESH + 1)], LT, lse_sem.at[2], lse_sem.at[3])
    others = LT.at[pl.ds(0, SRC - 1)]
    pltpu.make_async_copy(others, others, lse_sem.at[3]).wait()
    for place in range(PLANE):
        for kk in both:
            terms = [LT[2 * place + kk, FRESH]]
            for late in range(LATE, PLANE):
                for core in both:
                    terms.append(LT[2 * behind(place, late) + core, 2 * (late - LATE) + kk])
            top = functools.reduce(jnp.maximum, terms)
            LV2[2 * place + kk] = top + jnp.log(sum(jnp.exp(v - top) for v in terms))

    def cell_shift(c):
        rank = RK[:, :, pl.ds(c, 1), :].reshape(SRC, 1, VEC)
        found = jnp.where(rank == numbers(SRC), LV2[...], HIGH)
        return jnp.min(found, axis=2, keepdims=True).reshape(ROWS, 1)

    def cell_sum(c):
        weights = jnp.exp(L[c] - cell_shift(c)).astype(BF16)
        MS[c] = jnp.sum(weights.astype(F32), axis=0, keepdims=True)
        return lax.dot_general(
            weights, R[c], (((0,), (0,)), ((), ())), preferred_element_type=F32
        )

    def cell_of(step, i):
        return ring(z + step) * QUARTER + i

    landing = (RN, RP)
    toward = (z_next, z_prev)

    def reduce_message(way, number):
        return remote(
            S.at[way, number], landing[way].at[number],
            rs_send.at[way, number], rs_recv.at[way, number], toward[way],
        )

    def out_cell(step, i):
        return out.at[k * MINE + cell_of(step, i)]

    def out_message(kind, i):
        ref = out_cell((0, 0, -1, 1)[kind], i)
        return remote(ref, ref, og_send.at[kind, i], og_recv.at[kind, i], toward[kind % 2])

    def out_sibling(step, i):
        ref = out_cell(step, i)
        return remote(ref, ref, os_send.at[step % 4, i], os_recv.at[step % 4, i], sibling)

    diagonal = lax.broadcasted_iota(jnp.int32, (CELL, CELL), 0) == lax.broadcasted_iota(
        jnp.int32, (CELL, CELL), 1
    )

    def finish(i, total, mass_row, mass):
        c = z * QUARTER + i
        mass = mass + jnp.sum(
            jnp.where(diagonal, jnp.broadcast_to(mass_row, (CELL, CELL)), 0.0),
            axis=1,
            keepdims=True,
        )
        out[k * MINE + c] = (
            (total + PRIOR_MASS * C[c].astype(F32)) / (mass + PRIOR_MASS)
        ).astype(BF16)
        out_message(0, i).start()
        out_message(1, i).start()
        out_sibling(0, i).start()

    for way in both:
        S[way, 0] = cell_sum(cell_of(2, way)).astype(BF16)
        reduce_message(way, 0).start()

    eye = lax.broadcasted_iota(jnp.int32, (ROWS, ROWS), 0) == lax.broadcasted_iota(
        jnp.int32, (ROWS, ROWS), 1
    )
    for j in (2, 0, 1):
        for i in range(ROUTED):
            shift = cell_shift(cell_of(column_step[j], QUARTER - ROUTED + i))
            wide = jnp.where(eye, jnp.broadcast_to(shift, (ROWS, ROWS)), 0.0)
            SHR[j, i] = jnp.sum(wide, axis=0, keepdims=True)
        shift_message(j).start()

    for way in both:
        S[way, 1] = cell_sum(cell_of(1 - 2 * way, 1 - way)).astype(BF16)
        reduce_message(way, 1).start()

    for way in both:
        SF[way] = cell_sum(cell_of(1 - 2 * way, way))

    def own_sum(i, carry):
        SF[2 + i] = cell_sum(z * QUARTER + i)
        return carry

    lax.fori_loop(0, QUARTER, own_sum, 0)
    MR[z] = MS[...]
    for j, device in enumerate((z_next, z_prev, z_far)):
        remote(MS, MR.at[z], mass_sem.at[j], mass_sem.at[3], device).start()
    for j in range(3):
        shift_message(j).wait_recv()
        for place in range(PLANE):
            rows_message(place, j).wait_recv()
    def finish_rows(i):
        c = z * QUARTER + (QUARTER - ROUTED) + i
        mass = 0.0
        total = SF[2 + QUARTER - ROUTED + i]
        for j in range(3):
            rows = R3[j, i]
            products = lax.dot_general(C[c], rows, last, preferred_element_type=F32)
            value = (2.0 * products - SQC[i][:, 0:1]) * D**-0.5
            weights = jnp.exp(value - SHZ[j, i]).astype(BF16)
            mass = mass + jnp.sum(weights.astype(F32), axis=1, keepdims=True)
            total = total + jnp.dot(weights, rows, preferred_element_type=F32)
        finish(QUARTER - ROUTED + i, total, MS[c], mass)

    finish_rows(0)
    for way in both:
        reduce_message(way, 0).wait_recv()
        S[way, 2] = (SF[way] + landing[way][0].astype(F32)).astype(BF16)
        reduce_message(way, 2).start()
    finish_rows(1)
    others = MR.at[pl.ds(0, SIDE - 1)]
    pltpu.make_async_copy(others, others, mass_sem.at[3]).wait()

    def out_arrive(i):
        for kind in both:
            out_message(kind, i).wait_recv()
            if i % 2 == kind:
                out_message(2 + kind, i).start()
            out_sibling(-1 if kind == 0 else 1, i).start()

    for h in both:
        for stage, d in ((1, 0), (2, 0), (2, 1), (2, -1), (2, 2)):
            for kind in range(6 if d == 2 else 4):
                message(h, stage, d, kind).wait_send()
        for place in range(PLANE):
            to_sibling(h, place).wait_send()
    for number in range(6):
        cand_message(number).wait_send()
    cand_over.wait_send()
    cand_near.wait_send()
    for j in range(3):
        shift_message(j).wait_send()
        for place in range(PLANE):
            rows_message(place, j).wait_send()
    sent = PV.at[pl.ds(0, 2 * LATE - 1)]
    pltpu.make_async_copy(sent, sent, lse_sem.at[0]).wait()
    sent = LT.at[pl.ds(0, SRC - 1)]
    pltpu.make_async_copy(sent, sent, lse_sem.at[2]).wait()
    out_arrive(2)
    for i in both:
        reduce_message(0, 2 - i).wait_recv()
        reduce_message(1, 1 + i).wait_recv()
        c = z * QUARTER + i
        total = SF[2 + i] + RN[2 - i].astype(F32) + RP[1 + i].astype(F32)
        finish(i, total, MR[0, c] + MR[1, c] + MR[2, c] + MR[3, c], 0.0)

    out_arrive(3)
    for way in both:
        for number in range(3):
            reduce_message(way, number).wait_send()
    for j, device in enumerate((z_next, z_prev, z_far)):
        remote(MS, MR.at[z], mass_sem.at[j], mass_sem.at[3], device).wait_send()
    for i in both:
        out_arrive(i)
    for i in (2, 3):
        out_message(2 + i % 2, i).wait_recv()
        out_sibling(2, i).start()
    for i in range(QUARTER):
        out_message(0, i).wait_send()
        out_message(1, i).wait_send()
        for step in (0, -1, 1):
            out_sibling(step, i).wait_send()
            out_sibling(step, i).wait_recv()
    for i in both:
        out_message(2 + i % 2, i).wait_recv()
        out_sibling(2, i).start()
    for i in (2, 3, 0, 1):
        out_message(2 + i % 2, i).wait_send()
        out_sibling(2, i).wait_send()
        out_sibling(2, i).wait_recv()


def body(vectors, candidates, centroids):
    cells = centroids.shape[0] // CELL
    dma = pltpu.SemaphoreType.DMA
    any_space = pl.BlockSpec(memory_space=pl.ANY)
    refined = pl.pallas_call(
        kernel,
        out_shape=pltpu.VMEM((cells, CELL, D), BF16),
        in_specs=[any_space] * 3,
        out_specs=pl.BlockSpec(memory_space=pltpu.VMEM),
        scratch_shapes=[
            pltpu.VMEM((SRC, VEC, D), BF16),
            pltpu.VMEM((SRC, 8, VEC), jnp.int32),
            pltpu.VMEM((8, VEC), jnp.int32),
            pltpu.VMEM((MINE, CELL, D), BF16),
            pltpu.VMEM((MINE, D, CELL), BF16),
            pltpu.VMEM((MINE, ROWS, D), BF16),
            pltpu.VMEM((PLANE, 2, MINE, VEC), F32),
            pltpu.VMEM((PLANE * MINE, VEC), BF16),
            pltpu.VMEM((VEC, VEC), BF16),
            pltpu.VMEM((MINE, 8, CELL), F32),
            pltpu.VMEM((MINE, ROWS, CELL), F32),
            pltpu.VMEM((MINE, ROWS, CELL), F32),
            pltpu.VMEM((SRC + 1, 1, VEC), F32),
            pltpu.VMEM((2 * LATE, 1, VEC), F32),
            pltpu.VMEM((SRC, 1, VEC), F32),
            pltpu.VMEM((SRC, FRESH + 1, 1, VEC), F32),
            pltpu.VMEM((MINE, 1, CELL), F32),
            pltpu.VMEM((SIDE, MINE, 1, CELL), F32),
            pltpu.VMEM((2, 3, CELL, D), BF16),
            pltpu.VMEM((2 + QUARTER, CELL, D), F32),
            pltpu.VMEM((3, CELL, D), BF16),
            pltpu.VMEM((3, CELL, D), BF16),
            pltpu.VMEM((3, ROUTED, ROWS, D), BF16),
            pltpu.VMEM((3, ROUTED, 1, ROWS), F32),
            pltpu.VMEM((3, ROUTED, 1, ROWS), F32),
            pltpu.VMEM((ROUTED, CELL, CELL), F32),
            dma((3, 16)),
            dma((3, 16)),
            dma((3,)),
            dma((3,)),
            dma((3,)),
            dma((8,)),
            dma((8,)),
            dma((2, 22)),
            dma((2, 22)),
            dma((2, 16)),
            dma((2, 16)),
            dma((4,)),
            dma((2, 3)),
            dma((2, 3)),
            dma((4,)),
            dma((4, 4)),
            dma((4, 4)),
            dma((4, 4)),
            dma((4, 4)),
        ],
        compiler_params=pltpu.CompilerParams(
            collective_id=0, has_side_effects=True, vmem_limit_bytes=48 * 1024 * 1024
        ),
        name="refine",
    )(vectors, candidates.T, centroids.reshape(cells, CELL, D))
    return refined.reshape(cells * CELL, D)


def solution(mesh):
    placed = (P(("grp", "own"), None), P(("grp", "own"), None), P("own", None))
    return jax.shard_map(
        body, mesh=mesh, in_specs=placed, out_specs=P("own", None), check_vma=False
    )
```
